32 devices in a mesh: batch: 4 (over y, x), mp: 8 (over z, core).
Axes of the slice: x: 2, y: 2, z: 4, core: 2. Of those that a mesh axis runs over, the one named last changes fastest.
Arguments:
- token_ids: int32 [512, 7], P('batch'), may hold values from 0 to 10239
- seq_lengths: int32 [512], P('batch'), may hold values from 2 to 6, as said below
- valid_mask: int32 [512, 6], P('batch'), may hold values 0 or 1
- embed: float32 [10240, 1024], P(None, 'mp'), may hold values from -4 to 4
- w_main: float32 [2048, 4, 1024], P(None, None, 'mp')
- w_scale: float32 [3, 64, 4, 1024], P(None, None, None, 'mp'), may hold values from -0.75 to 0.75
- w_hyper: float32 [2177, 512], replicated, may hold values from -0.125 to 0.125
- w_zproj: float32 [129, 192], replicated, may hold values from -1 to 1
- w_out: float32 [1024, 10240], P(None, 'mp')
- main_vectors: float32 [2, 4, 1024], P(None, None, 'mp'), may hold values from 0.5 to 1.5
- embed_row: float32 [10240], replicated, may hold values from 7.761022e-11 to 3.1044087e-10
- embed_col: float32 [1024], P('mp'), may hold values from 7.761022e-11 to 3.1044087e-10
- main_row: float32 [2048], replicated, may hold values from 9.536743e-08 to 4.1325887e-07
- main_col: float32 [4, 1024], P(None, 'mp'), may hold values from 9.536743e-08 to 4.1325887e-07
- scale_row: float32 [3, 64], replicated, may hold values from 3.8146972e-08 to 1.5258789e-07
- scale_col: float32 [3, 4, 1024], P(None, None, 'mp'), may hold values from 3.8146972e-08 to 1.5258789e-07
- hyper_row: float32 [2177], replicated, may hold values from 1.5258789e-06 to 6.1035157e-06
- hyper_col: float32 [512], replicated, may hold values from 1.5258789e-06 to 6.1035157e-06
- zproj_row: float32 [129], replicated, may hold values from 6.1035155e-07 to 2.4414062e-06
- zproj_col: float32 [192], replicated, may hold values from 6.1035155e-07 to 2.4414062e-06
- out_row: float32 [1024], replicated, may hold values from 3.8146974e-09 to 1.525879e-08
- out_col: float32 [10240], P('mp'), may hold values from 3.8146974e-09 to 1.525879e-08
- vector_state: float32 [2, 4, 1024], P(None, None, 'mp'), may hold values from 9.536743e-08 to 4.1325887e-07
Outputs:
- loss_sum: float32 [], replicated
- count: float32 [], replicated
- grad_embed: float32 [10240, 1024], P(None, 'mp')
- new_embed: float32 [10240, 1024], P(None, 'mp')
- new_embed_row: float32 [10240], replicated
- new_embed_col: float32 [1024], P('mp')
- grad_main: float32 [2048, 4, 1024], P(None, None, 'mp')
- new_main: float32 [2048, 4, 1024], P(None, None, 'mp')
- new_main_row: float32 [2048], replicated
- new_main_col: float32 [4, 1024], P(None, 'mp')
- grad_scale: float32 [3, 64, 4, 1024], P(None, None, None, 'mp')
- new_scale: float32 [3, 64, 4, 1024], P(None, None, None, 'mp')
- new_scale_row: float32 [3, 64], replicated
- new_scale_col: float32 [3, 4, 1024], P(None, None, 'mp')
- grad_hyper: float32 [2177, 512], replicated
- new_hyper: float32 [2177, 512], replicated
- new_hyper_row: float32 [2177], replicated
- new_hyper_col: float32 [512], replicated
- grad_zproj: float32 [129, 192], replicated
- new_zproj: float32 [129, 192], replicated
- new_zproj_row: float32 [129], replicated
- new_zproj_col: float32 [192], replicated
- grad_out: float32 [1024, 10240], P(None, 'mp')
- new_out: float32 [1024, 10240], P(None, 'mp')
- new_out_row: float32 [1024], replicated
- new_out_col: float32 [10240], P('mp')
- grad_vectors: float32 [2, 4, 1024], P(None, None, 'mp')
- new_vector_state: float32 [2, 4, 1024], P(None, None, 'mp')
- new_vectors: float32 [2, 4, 1024], P(None, None, 'mp')
The draws below stay inside these ranges and needn't reach their ends.
Inputs may be any that keep to these rules, and one draw needn't show every extreme that they name: `seq_lengths`: each length is 2 or 6; every draw has a window of 6.
All inputs are finite; a program needn't handle non-finite values. No bound on the sum of `valid_mask` on one device may be relied on, other than what follows from the above.
Results may differ from the reference program's by a relative error of at most 0.011.
The reference program's roundings to bfloat16 on the way count: a program that leaves them out, or rounds other values in their place, can miss the bound.
Values may be sent and summed in bfloat16 or wider, within the bound.
No kernel may reach another device: no remote copies, remote signals or barrier semaphores. Data moves between devices by JAX's collectives and lax.ppermute only.
A program may use at most 320 MiB of HBM per device.

```python
import math
import jax
import jax.numpy as jnp
from jax import lax

E = 1024
H = 1024
V = 10240
NH = 128
Z = 64
STEPS = 6
SHORT = 2
STEP = 10
SEQ_DEV = 128
SEQS = 512


def draw_seq_lengths(key, part):
    key = jax.random.fold_in(key, 1)
    first, second = jax.random.split(key)
    shard = jnp.arange(SEQS, dtype=jnp.int32) // SEQ_DEV
    ticket = jax.random.randint(first, (SEQS,), 0, 20)
    chosen = jax.random.randint(second, (), 0, SEQS)
    long_rows = (ticket < 1 + 6 * shard) | (jnp.arange(SEQS, dtype=jnp.int32) == chosen)
    return jnp.where(long_rows, STEPS, SHORT).astype(jnp.int32)


def draw_w_main(key, part):
    key = jax.random.fold_in(key, 2)
    base = jnp.clip(jax.random.normal(key, (E + H, 4, H), jnp.float32), -4.0, 4.0)
    tilt = 0.6 + 1.2 * jnp.arange(H, dtype=jnp.float32) / (H - 1)
    return base * tilt / math.sqrt(E)


def draw_w_out(key, part):
    key = jax.random.fold_in(key, 3)
    base = jnp.clip(jax.random.normal(key, (H, V), jnp.float32), -4.0, 4.0)
    tilt = 1.0 + 2.0 * jnp.arange(V, dtype=jnp.float32) / (V - 1)
    return base * tilt * (3.0 / math.sqrt(H))


def set_ends(values, key, smallest, top_value):
    longest = values.shape.index(max(values.shape))
    spots = []
    for shift in (0, 1):
        where = [jax.random.randint(jax.random.fold_in(key, axis), (), 0, length) for axis, length in enumerate(values.shape)]
        where[longest] = (where[longest] + shift) % values.shape[longest]
        spots.append(tuple(where))
    return values.at[spots[0]].set(smallest).at[spots[1]].set(top_value)


def level_of(rng, dims, shards, low, top_value):
    factor_of = 1.0
    for position, parts in shards:
        steps = jax.random.uniform(jax.random.fold_in(jax.random.fold_in(rng, 6), position), (parts,), jnp.float32, low / len(shards), top_value / len(shards))
        factor_of = factor_of * jnp.repeat(jnp.exp(steps), dims[position] // parts).reshape((-1,) + (1,) * (len(dims) - 1 - position))
    return factor_of


def scatter_about(own_key, shape, scale, limit, shards=(), kind=jnp.bfloat16):
    values = jax.random.normal(own_key, shape, jnp.float32) * scale
    if len(shards) > 0:
        values = level_of(own_key, shape, shards, -0.22, 0.18) * values
    return jnp.clip(values, min=-limit, max=limit).astype(kind)


def setup_inputs(seed: int = 0) -> dict:
    arg_keys = jax.random.split(jax.random.key(seed), 24)
    token_ids = set_ends(jax.random.randint(arg_keys[0], (SEQS, STEPS + 1), 0, V), jax.random.fold_in(arg_keys[0], 1), 0, V - 1).astype(jnp.int32)
    seq_lengths = draw_seq_lengths(jax.random.fold_in(arg_keys[23], 71), 0)
    valid_mask = set_ends((jax.random.randint(arg_keys[2], (SEQS, STEPS), 0, 8) < 7).astype(jnp.int32), jax.random.fold_in(arg_keys[2], 1), 0, 1)
    embed = scatter_about(arg_keys[3], (V, E), 1.0, 4.0, ((1, 8),), jnp.float32)
    w_main = draw_w_main(jax.random.fold_in(arg_keys[23], 71), 0)
    w_scale = scatter_about(arg_keys[5], (3, Z, 4, H), Z ** -0.5, 0.75, ((3, 8),), jnp.float32)
    w_hyper = scatter_about(arg_keys[6], (E + H + NH + 1, 4 * NH), (E + H + NH + 1) ** -0.5, 0.125, (), jnp.float32)
    w_zproj = scatter_about(arg_keys[7], (NH + 1, 3 * Z), (NH // 4) ** -0.5, 1.0, (), jnp.float32)
    w_out = draw_w_out(jax.random.fold_in(arg_keys[23], 71), 0)
    main_vectors = jnp.clip(1.0 + 0.1 * jax.random.normal(arg_keys[9], (2, 4, H), jnp.float32), 0.5, 1.5)
    embed_row = jnp.clip(jnp.exp(jax.random.uniform(arg_keys[10], (V,), jnp.float32, math.log(7.761021686425451e-11), math.log(3.1044086745701804e-10))), 7.761021686425451e-11, 3.1044086745701804e-10)
    embed_col = jnp.clip(jnp.exp(math.log(3.1044086745701804e-10) - 1.3862944 * jax.random.uniform(arg_keys[11], (E,), jnp.float32) ** level_of(arg_keys[11], (E,), ((0, 8),), -0.2, 0.2)), 7.761021686425451e-11, 3.1044086745701804e-10)
    main_row = jnp.clip(jnp.exp(jax.random.uniform(arg_keys[12], (E + H,), jnp.float32, math.log(9.536743306171047e-08), math.log(4.132588742322696e-07))), 9.536743306171047e-08, 4.132588742322696e-07)
    main_col = jnp.clip(jnp.exp(math.log(4.132588742322696e-07) - 1.4663371 * jax.random.uniform(arg_keys[13], (4, H), jnp.float32) ** level_of(arg_keys[13], (4, H), ((1, 8),), -0.2, 0.2)), 9.536743306171047e-08, 4.132588742322696e-07)
    scale_row = jnp.clip(jnp.exp(jax.random.uniform(arg_keys[14], (3, Z), jnp.float32, math.log(3.814697180359872e-08), math.log(1.5258788721439487e-07))), 3.814697180359872e-08, 1.5258788721439487e-07)
    scale_col = jnp.clip(jnp.exp(math.log(1.5258788721439487e-07) - 1.3862944 * jax.random.uniform(arg_keys[15], (3, 4, H), jnp.float32) ** level_of(arg_keys[15], (3, 4, H), ((2, 8),), -0.2, 0.2)), 3.814697180359872e-08, 1.5258788721439487e-07)
    hyper_row = jnp.clip(jnp.exp(jax.random.uniform(arg_keys[16], (E + H + NH + 1,), jnp.float32, math.log(1.5258789289873675e-06), math.log(6.10351571594947e-06))), 1.5258789289873675e-06, 6.10351571594947e-06)
    hyper_col = jnp.clip(jnp.exp(jax.random.uniform(arg_keys[17], (4 * NH,), jnp.float32, math.log(1.5258789289873675e-06), math.log(6.10351571594947e-06))), 1.5258789289873675e-06, 6.10351571594947e-06)
    zproj_row = jnp.clip(jnp.exp(jax.random.uniform(arg_keys[18], (NH + 1,), jnp.float32, math.log(6.103515488575795e-07), math.log(2.441406195430318e-06))), 6.103515488575795e-07, 2.441406195430318e-06)
    zproj_col = jnp.clip(jnp.exp(jax.random.uniform(arg_keys[19], (3 * Z,), jnp.float32, math.log(6.103515488575795e-07), math.log(2.441406195430318e-06))), 6.103515488575795e-07, 2.441406195430318e-06)
    out_row = jnp.clip(jnp.exp(jax.random.uniform(arg_keys[20], (H,), jnp.float32, math.log(3.814697446813398e-09), math.log(1.525878978725359e-08))), 3.814697446813398e-09, 1.525878978725359e-08)
    out_col = jnp.clip(jnp.exp(math.log(1.525878978725359e-08) - 1.3862944 * jax.random.uniform(arg_keys[21], (V,), jnp.float32) ** level_of(arg_keys[21], (V,), ((0, 8),), -0.2, 0.2)), 3.814697446813398e-09, 1.525878978725359e-08)
    vector_state = jnp.clip(jnp.exp(math.log(4.132588742322696e-07) - 1.4663371 * jax.random.uniform(arg_keys[22], (2, 4, H), jnp.float32) ** level_of(arg_keys[22], (2, 4, H), ((2, 8),), -0.2, 0.2)), 9.536743306171047e-08, 4.132588742322696e-07)
    return dict(token_ids=token_ids, seq_lengths=seq_lengths, valid_mask=valid_mask, embed=embed, w_main=w_main, w_scale=w_scale, w_hyper=w_hyper, w_zproj=w_zproj, w_out=w_out, main_vectors=main_vectors, embed_row=embed_row, embed_col=embed_col, main_row=main_row, main_col=main_col, scale_row=scale_row, scale_col=scale_col, hyper_row=hyper_row, hyper_col=hyper_col, zproj_row=zproj_row, zproj_col=zproj_col, out_row=out_row, out_col=out_col, vector_state=vector_state)


@jax.custom_vjp
def low(v):
    return lax.optimization_barrier(v.astype(jnp.bfloat16)).astype(jnp.float32)

@jax.custom_vjp
def low_back(v):
    return v

def low_keep(v):
    return (low(v), None)

def low_pass(kept, grad):
    return (grad,)

def back_keep(v):
    return (v, None)

def back_low(kept, grad):
    return (low(grad),)
low.defvjp(low_keep, low_pass)
low_back.defvjp(back_keep, back_low)
EPS_NORM = 1e-05
EPS_FACT = 1e-30
HIGH = lax.Precision.HIGHEST

def matmul(left, right):
    return jnp.dot(left, right, precision=HIGH)

def adafactor(weight, grad, row_old, col_old, row_mean, col_mean, lead, rate):
    decay = 1.0 - STEP ** (-0.8)
    row_new = decay * row_old + (1.0 - decay) * row_mean
    col_new = decay * col_old + (1.0 - decay) * col_mean
    relative = row_new / lax.optimization_barrier(jnp.mean(row_new, axis=-1, keepdims=True))
    relative = relative.reshape(relative.shape + (1,) * (grad.ndim - relative.ndim))
    spread = col_new[None] if lead == 0 else col_new[:, None]
    updated = weight - rate * grad * lax.rsqrt(relative * spread)
    return (grad, updated, row_new, col_new)

def forward(embed, w_main, w_scale, w_hyper, w_zproj, w_out, main_vectors, token_ids, valid, count):
    batch_rows = token_ids.shape[0]
    inputs = jnp.swapaxes(low(embed[token_ids[:, :STEPS]]), 0, 1)
    w_in = low(w_main[:E].reshape(E, 4 * H))
    w_rec = low(w_main[E:].reshape(H, 4 * H))
    w_hyp = low(w_hyper)
    w_zed = low(w_zproj)
    w_scl = low(w_scale)
    w_head = low(w_out)
    ones_col = jnp.ones((batch_rows, 1), jnp.float32)

    def advance(carry, x_now):
        h_prev, c_prev, hh_prev, hc_prev = carry
        joined = jnp.concatenate([x_now, h_prev, hh_prev, ones_col], axis=1)
        hyper_pre = low_back(matmul(joined, w_hyp)).reshape(batch_rows, 4, NH)
        hc_now = jax.nn.sigmoid(hyper_pre[:, 1]) * hc_prev + jax.nn.sigmoid(hyper_pre[:, 0]) * jnp.tanh(hyper_pre[:, 3])
        hh_now = low(jax.nn.sigmoid(hyper_pre[:, 2]) * jnp.tanh(hc_now))
        z_raw = matmul(jnp.concatenate([hh_now, ones_col], axis=1), w_zed)
        z_low = low_back(low(z_raw)).reshape(batch_rows, 3, Z)
        scales = low_back(jnp.einsum('skz,kzgu->skgu', z_low, w_scl, precision=HIGH))
        from_h = low_back(matmul(h_prev, w_rec).reshape(batch_rows, 4, H))
        from_x = low_back(matmul(x_now, w_in).reshape(batch_rows, 4, H))
        summed = (1.0 + scales[:, 0]) * from_h + (1.0 + scales[:, 1]) * from_x
        centre = lax.optimization_barrier(jnp.mean(summed, axis=2, keepdims=True))
        square = lax.optimization_barrier(jnp.mean(summed * summed, axis=2, keepdims=True))
        normed = (summed - centre) * lax.rsqrt(square - centre * centre + EPS_NORM)
        pre_act = main_vectors[0] * normed + main_vectors[1] + scales[:, 2]
        c_now = jax.nn.sigmoid(pre_act[:, 1]) * c_prev + jax.nn.sigmoid(pre_act[:, 0]) * jnp.tanh(pre_act[:, 3])
        h_now = low(jax.nn.sigmoid(pre_act[:, 2]) * jnp.tanh(c_now))
        return ((h_now, c_now, hh_now, hc_now), h_now)
    start = (jnp.zeros((batch_rows, H), jnp.float32), jnp.zeros((batch_rows, H), jnp.float32), jnp.zeros((batch_rows, NH), jnp.float32), jnp.zeros((batch_rows, NH), jnp.float32))
    final, hiddens = lax.scan(jax.checkpoint(advance), start, inputs)
    targets = jnp.swapaxes(token_ids[:, 1:], 0, 1)
    weight_cols = jnp.swapaxes(valid, 0, 1)

    def head_block(pieces):
        h_rows, target_row, weight_row = pieces
        logits = low_back(matmul(h_rows, w_head))
        total = jax.nn.logsumexp(logits, axis=1)
        picked = jnp.take_along_axis(logits, target_row[:, None], axis=1)[:, 0]
        return jnp.sum((total - picked) * weight_row)
    losses = lax.map(jax.checkpoint(head_block), (hiddens, targets, weight_cols))
    loss_sum = jnp.sum(losses)
    return (loss_sum / count, loss_sum)

def reference(token_ids, seq_lengths, valid_mask, embed, w_main, w_scale, w_hyper, w_zproj, w_out, main_vectors, embed_row, embed_col, main_row, main_col, scale_row, scale_col, hyper_row, hyper_col, zproj_row, zproj_col, out_row, out_col, vector_state):
    positions = jnp.arange(STEPS, dtype=jnp.int32)
    valid = valid_mask.astype(jnp.float32) * (positions[None, :] < seq_lengths[:, None]).astype(jnp.float32)
    count = jnp.sum(valid)

    def objective(p_embed, p_main, p_scale, p_hyper, p_zproj, p_out, p_vectors):
        return forward(p_embed, p_main, p_scale, p_hyper, p_zproj, p_out, p_vectors, token_ids, valid, count)
    value, pullback, loss_sum = jax.vjp(objective, embed, w_main, w_scale, w_hyper, w_zproj, w_out, main_vectors, has_aux=True)
    g_embed, g_main, g_scale, g_hyper, g_zproj, g_out, g_vec = pullback(jnp.ones_like(value))
    sq_embed = g_embed * g_embed + EPS_FACT
    sq_main = g_main * g_main + EPS_FACT
    sq_scale = g_scale * g_scale + EPS_FACT
    sq_hyper = g_hyper * g_hyper + EPS_FACT
    sq_zproj = g_zproj * g_zproj + EPS_FACT
    sq_out = g_out * g_out + EPS_FACT
    res_embed = adafactor(embed, g_embed, embed_row, embed_col, lax.optimization_barrier(jnp.mean(sq_embed, axis=1)), lax.optimization_barrier(jnp.mean(sq_embed, axis=0)), 0, 1.0)
    res_main = adafactor(w_main, g_main, main_row, main_col, lax.optimization_barrier(jnp.mean(sq_main, axis=(1, 2))), lax.optimization_barrier(jnp.mean(sq_main, axis=0)), 0, 1.0 / math.sqrt(E))
    res_scale = adafactor(w_scale, g_scale, scale_row, scale_col, lax.optimization_barrier(jnp.mean(sq_scale, axis=(2, 3))), lax.optimization_barrier(jnp.mean(sq_scale, axis=1)), 1, 1.0 / math.sqrt(Z))
    res_hyper = adafactor(w_hyper, g_hyper, hyper_row, hyper_col, lax.optimization_barrier(jnp.mean(sq_hyper, axis=1)), lax.optimization_barrier(jnp.mean(sq_hyper, axis=0)), 0, 1.0 / math.sqrt(E + H + NH + 1))
    res_zproj = adafactor(w_zproj, g_zproj, zproj_row, zproj_col, lax.optimization_barrier(jnp.mean(sq_zproj, axis=1)), lax.optimization_barrier(jnp.mean(sq_zproj, axis=0)), 0, 2.0 / math.sqrt(NH))
    res_out = adafactor(w_out, g_out, out_row, out_col, lax.optimization_barrier(jnp.mean(sq_out, axis=1)), lax.optimization_barrier(jnp.mean(sq_out, axis=0)), 0, 3.0 / math.sqrt(H))
    decay = 1.0 - STEP ** (-0.8)
    state_new = decay * vector_state + (1.0 - decay) * (g_vec * g_vec + EPS_FACT)
    vectors_new = main_vectors - 0.1 * g_vec * lax.rsqrt(state_new)
    return (loss_sum, count, res_embed[0], res_embed[1], res_embed[2], res_embed[3], res_main[0], res_main[1], res_main[2], res_main[3], res_scale[0], res_scale[1], res_scale[2], res_scale[3], res_hyper[0], res_hyper[1], res_hyper[2], res_hyper[3], res_zproj[0], res_zproj[1], res_zproj[2], res_zproj[3], res_out[0], res_out[1], res_out[2], res_out[3], g_vec, state_new, vectors_new)
```

```python
import functools
import math

import jax
import jax.numpy as jnp
from jax import lax
from jax.experimental import pallas as pl
from jax.experimental.pallas import tpu as pltpu
from jax.sharding import PartitionSpec as P

E = 1024
H = 1024
V = 10240
NH = 128
Z = 64
STEP = 10
LANES = 128
ROW_TILE = 16
VMEM_BYTES = 56 * 1024 * 1024

EPS_NORM = 1e-05
EPS_FACT = 1e-30

F32 = jnp.float32
BF16 = jnp.bfloat16


def matmul(left, right):
    return jnp.dot(left, right, preferred_element_type=F32)


def dot_last(left, right):
    return lax.dot_general(left, right, (((1,), (1,)), ((), ())), preferred_element_type=F32)


def dot_first(left, right):
    return lax.dot_general(left, right, (((0,), (0,)), ((), ())), preferred_element_type=F32)


def adafactor(weight, grad, row_old, col_old, row_mean, col_mean, lead, rate):
    decay = 1.0 - STEP ** (-0.8)
    row_new = decay * row_old + (1.0 - decay) * row_mean
    col_new = decay * col_old + (1.0 - decay) * col_mean
    relative = row_new / jnp.mean(row_new, axis=-1, keepdims=True)
    relative = relative.reshape(relative.shape + (1,) * (grad.ndim - relative.ndim))
    spread = col_new[None] if lead == 0 else col_new[:, None]
    updated = weight - rate * grad * lax.rsqrt(relative * spread)
    return (grad, updated, row_new, col_new)


def masked_thirds(z_low):
    lane = lax.broadcasted_iota(jnp.int32, z_low.shape, 1) // Z
    zero = jnp.zeros_like(z_low)
    return jnp.concatenate([jnp.where(lane == k, z_low, zero) for k in range(3)], axis=0)


def forward_kernel(
    x_ref, main_hbm, scale_ref, vec_ref, hyp_ref, hypb_ref, zp_ref, zpb_ref,
    h_out, cprev_out, tc_out, hcprev_out, thc_out, hh_out, z_out, hg_out,
    ux_out, uh_out, one0_out, one1_out, n_out, act_out, rstd_out,
    main_v, prex_s, h_s, c_s, hh_s, hc_s, sem,
):
    t = pl.program_id(0)
    nb, _, bw = main_v.shape
    bu = bw // 4
    steps, _, rows, _ = ux_out.shape

    @pl.when(t == 0)
    def _():
        copies = [
            pltpu.make_async_copy(
                main_hbm.at[:, part * E : (part + 1) * E],
                main_v.at[:, part * E : (part + 1) * E],
                sem.at[part],
            )
            for part in range(2)
        ]
        for copy in copies:
            copy.start()
        prex_s[...] = (matmul(x_ref[...], hyp_ref[:E]) + hypb_ref[...]).reshape(steps, rows, 4 * NH)
        h_s[...] = jnp.zeros_like(h_s)
        c_s[...] = jnp.zeros_like(c_s)
        hh_s[...] = jnp.zeros_like(hh_s)
        hc_s[...] = jnp.zeros_like(hc_s)
        copies[0].wait()
        for m in range(nb):
            ux_out[:, m] = matmul(x_ref[...], main_v[m, :E]).reshape(steps, rows, bw)
        copies[1].wait()

    h_prev = h_s[...]
    hh_prev = hh_s[...]
    hc_prev = hc_s[...]
    q = prex_s[t] + matmul(h_prev, hyp_ref[E : E + H]) + matmul(hh_prev, hyp_ref[E + H : E + H + NH])
    q_in = jax.nn.sigmoid(q[:, :NH])
    q_forget = jax.nn.sigmoid(q[:, NH : 2 * NH])
    q_out = jax.nn.sigmoid(q[:, 2 * NH : 3 * NH])
    q_cell = jnp.tanh(q[:, 3 * NH :])
    hc = q_forget * hc_prev + q_in * q_cell
    thc = jnp.tanh(hc)
    hh = (q_out * thc).astype(BF16)
    z_low = (matmul(hh, zp_ref[...]) + zpb_ref[...]).astype(BF16)
    hcprev_out[0] = hc_prev
    thc_out[0] = thc
    hg_out[0, :, :NH] = q_in
    hg_out[0, :, NH : 2 * NH] = q_forget
    hg_out[0, :, 2 * NH : 3 * NH] = q_out
    hg_out[0, :, 3 * NH :] = q_cell
    hh_out[0] = hh
    z_out[0] = z_low
    hh_s[...] = hh
    hc_s[...] = hc

    thirds = masked_thirds(z_low)
    sums = [jnp.zeros((rows, LANES), F32) for _ in range(4)]
    squares = [jnp.zeros((rows, LANES), F32) for _ in range(4)]
    for m in range(nb):
        scl = matmul(thirds, scale_ref[m])
        uh = matmul(h_prev, main_v[m, E:])
        one0 = 1.0 + scl[:rows]
        one1 = 1.0 + scl[rows : 2 * rows]
        s = one0 * uh + one1 * ux_out[t, m]
        uh_out[0, m] = uh
        one0_out[0, m] = one0
        one1_out[0, m] = one1
        act_out[0, m] = scl[2 * rows :]
        n_out[0, m] = s
        for g in range(4):
            for j in range(bu // LANES):
                piece = s[:, g * bu + j * LANES : g * bu + (j + 1) * LANES]
                sums[g] += piece
                squares[g] += piece * piece
    centres, rstds = [], []
    for g in range(4):
        centre = jnp.sum(sums[g], axis=1, keepdims=True) / H
        square = jnp.sum(squares[g], axis=1, keepdims=True) / H
        rstd = lax.rsqrt(square - centre * centre + EPS_NORM)
        centres.append(centre)
        rstds.append(rstd)
        rstd_out[0, :, g * LANES : (g + 1) * LANES] = jnp.broadcast_to(rstd, (rows, LANES))

    for m in range(nb):
        cols = slice(m * bu, (m + 1) * bu)
        gates = []
        for g in range(4):
            here = slice(g * bu, (g + 1) * bu)
            n = (n_out[0, m, :, here] - centres[g]) * rstds[g]
            n_out[0, m, :, here] = n
            pre = vec_ref[m, 0:1, here] * n + vec_ref[m, 1:2, here] + act_out[0, m, :, here]
            gate = jnp.tanh(pre) if g == 3 else jax.nn.sigmoid(pre)
            act_out[0, m, :, here] = gate
            gates.append(gate)
        c_prev = c_s[:, cols]
        c_now = gates[1] * c_prev + gates[0] * gates[3]
        tc = jnp.tanh(c_now)
        h_now = (gates[2] * tc).astype(BF16)
        cprev_out[0, :, cols] = c_prev
        tc_out[0, :, cols] = tc
        c_s[:, cols] = c_now
        h_s[:, cols] = h_now
        h_out[0, :, cols] = h_now


def backward_kernel(
    dh_ref, main_hbm, scale_ref, vec_ref, hyp_ref, zp_ref,
    cprev_ref, tc_ref, hcprev_ref, thc_ref, hg_ref,
    ux_ref, uh_ref, one0_ref, one1_ref, n_ref, act_ref, rstd_ref,
    dsda_out, dq_out, dz_out, dx_out, gv_out,
    main_v, dh_s, dc_s, dhh_s, dhc_s, da_s, dux_s, dq_s, sem,
):
    step = pl.program_id(0)
    nb, _, bw = main_v.shape
    bu = bw // 4
    steps, rows, _ = dq_s.shape
    t = steps - 1 - step
    copies = [
        pltpu.make_async_copy(
            main_hbm.at[:, part * E : (part + 1) * E],
            main_v.at[:, part * E : (part + 1) * E],
            sem.at[part],
        )
        for part in range(2)
    ]

    @pl.when(step == 0)
    def _():
        copies[1].start()
        copies[0].start()
        dh_s[...] = jnp.zeros_like(dh_s)
        dc_s[...] = jnp.zeros_like(dc_s)
        dhh_s[...] = jnp.zeros_like(dhh_s)
        dhc_s[...] = jnp.zeros_like(dhc_s)
        gv_out[...] = jnp.zeros_like(gv_out)

    first = [jnp.zeros((rows, LANES), F32) for _ in range(4)]
    second = [jnp.zeros((rows, LANES), F32) for _ in range(4)]
    for m in range(nb):
        cols = slice(m * bu, (m + 1) * bu)
        gate = [act_ref[0, m, :, g * bu : (g + 1) * bu] for g in range(4)]
        tc = tc_ref[0, :, cols]
        dh = dh_ref[0, :, cols] + dh_s[:, cols]
        dc = dc_s[:, cols] + dh * gate[2] * (1.0 - tc * tc)
        da = [
            dc * gate[3] * gate[0] * (1.0 - gate[0]),
            dc * cprev_ref[0, :, cols] * gate[1] * (1.0 - gate[1]),
            dh * tc * gate[2] * (1.0 - gate[2]),
            dc * gate[0] * (1.0 - gate[3] * gate[3]),
        ]
        dc_s[:, cols] = dc * gate[1]
        for g in range(4):
            here = slice(g * bu, (g + 1) * bu)
            n = n_ref[0, m, :, here]
            da_s[m, :, here] = da[g]
            gv_out[m, 0:1, here] += jnp.sum(da[g] * n, axis=0, keepdims=True)
            gv_out[m, 1:2, here] += jnp.sum(da[g], axis=0, keepdims=True)
            dn = vec_ref[m, 0:1, here] * da[g]
            dnn = dn * n
            for j in range(bu // LANES):
                first[g] += dn[:, j * LANES : (j + 1) * LANES]
                second[g] += dnn[:, j * LANES : (j + 1) * LANES]
    means = [
        (jnp.sum(first[g], axis=1, keepdims=True) / H, jnp.sum(second[g], axis=1, keepdims=True) / H)
        for g in range(4)
    ]

    @pl.when(step == 0)
    def _():
        copies[1].wait()

    dz_all = jnp.zeros((3 * rows, 3 * Z), F32)
    dh_rec = jnp.zeros((rows, H), F32)
    for m in range(nb):
        ds_parts = []
        for g in range(4):
            here = slice(g * bu, (g + 1) * bu)
            dn = vec_ref[m, 0:1, here] * da_s[m, :, here]
            rstd = rstd_ref[0, :, g * LANES : g * LANES + 1]
            ds_parts.append(rstd * (dn - means[g][0] - n_ref[0, m, :, here] * means[g][1]))
        ds = jnp.concatenate(ds_parts, axis=1)
        da_low = da_s[m].astype(BF16)
        dsda_out[m, 0, :, :bw] = ds.astype(BF16)
        dsda_out[m, 0, :, bw:] = da_low
        stack = jnp.concatenate(
            [(ds * uh_ref[0, m]).astype(BF16), (ds * ux_ref[0, m]).astype(BF16), da_low], axis=0
        )
        dz_all += dot_last(stack, scale_ref[m])
        duh = (ds * one0_ref[0, m]).astype(BF16)
        dux_s[t, m] = (ds * one1_ref[0, m]).astype(BF16)
        dh_rec += dot_last(duh, main_v[m, E:])

    lane = lax.broadcasted_iota(jnp.int32, (rows, 3 * Z), 1) // Z
    dz = jnp.zeros((rows, 3 * Z), F32)
    for k in range(3):
        dz = jnp.where(lane == k, dz_all[k * rows : (k + 1) * rows], dz)
    dz_low = dz.astype(BF16)
    dz_out[0] = dz_low
    q_in = hg_ref[0, :, :NH]
    q_forget = hg_ref[0, :, NH : 2 * NH]
    q_out = hg_ref[0, :, 2 * NH : 3 * NH]
    q_cell = hg_ref[0, :, 3 * NH :]
    thc = thc_ref[0]
    dhh = dhh_s[...] + dot_last(dz_low, zp_ref[...])
    dhc = dhc_s[...] + dhh * q_out * (1.0 - thc * thc)
    dq = jnp.concatenate(
        [
            dhc * q_cell * q_in * (1.0 - q_in),
            dhc * hcprev_ref[0] * q_forget * (1.0 - q_forget),
            dhh * thc * q_out * (1.0 - q_out),
            dhc * q_in * (1.0 - q_cell * q_cell),
        ],
        axis=1,
    ).astype(BF16)
    dq_out[0] = dq
    dq_s[t] = dq
    dhc_s[...] = dhc * q_forget
    dhh_s[...] = dot_last(dq, hyp_ref[E + H : E + H + NH])
    dh_s[...] = dh_rec + dot_last(dq, hyp_ref[E : E + H])

    @pl.when(step == steps - 1)
    def _():
        copies[0].wait()
        dx = dot_last(dq_s[...].reshape(steps * rows, 4 * NH), hyp_ref[:E])
        for m in range(nb):
            dx += dot_last(dux_s[:, m].reshape(steps * rows, bw), main_v[m, :E])
        dx_out[...] = dx.astype(dx_out.dtype)


def whole(shape):
    return pl.BlockSpec(shape, lambda t: (0,) * len(shape), pipeline_mode=pl.Buffered(1))


def run_forward(x_rows, main_all, scale_all, vec_all, hyp_low, hyp_bias, zp_low, zp_bias, steps):
    nb, _, bw = main_all.shape
    rows = x_rows.shape[0] // steps

    def stepped(*tail):
        return pl.BlockSpec((1,) + tail, lambda t: (t,) + (0,) * len(tail))

    def shaped(dtype, *tail):
        return jax.ShapeDtypeStruct((steps,) + tail, dtype)

    tails = [
        (BF16, (rows, H)), (F32, (rows, H)), (F32, (rows, H)), (F32, (rows, NH)), (F32, (rows, NH)),
        (BF16, (rows, NH)), (BF16, (rows, 3 * Z)), (F32, (rows, 4 * NH)), (F32, (nb, rows, bw)),
        (F32, (nb, rows, bw)), (F32, (nb, rows, bw)), (F32, (nb, rows, bw)), (F32, (nb, rows, bw)),
        (F32, (nb, rows, bw)), (F32, (rows, 4 * LANES)),
    ]
    out_specs = [stepped(*tail) for _, tail in tails]
    out_specs[8] = pl.BlockSpec((steps, nb, rows, bw), lambda t: (0, 0, 0, 0))
    return pl.pallas_call(
        forward_kernel,
        grid=(steps,),
        in_specs=[
            whole(x_rows.shape),
            pl.BlockSpec(memory_space=pl.ANY),
            whole(scale_all.shape),
            whole(vec_all.shape),
            whole(hyp_low.shape),
            whole(hyp_bias.shape),
            whole(zp_low.shape),
            whole(zp_bias.shape),
        ],
        out_specs=out_specs,
        out_shape=[shaped(dtype, *tail) for dtype, tail in tails],
        scratch_shapes=[
            pltpu.VMEM((nb, 2 * E, bw), BF16),
            pltpu.VMEM((steps, rows, 4 * NH), F32),
            pltpu.VMEM((rows, H), BF16),
            pltpu.VMEM((rows, H), F32),
            pltpu.VMEM((rows, NH), BF16),
            pltpu.VMEM((rows, NH), F32),
            pltpu.SemaphoreType.DMA((2,)),
        ],
        compiler_params=pltpu.CompilerParams(vmem_limit_bytes=VMEM_BYTES),
        name="recurrence_forward",
    )(x_rows, main_all, scale_all, vec_all, hyp_low, hyp_bias, zp_low, zp_bias)


def run_backward(dh_top, main_all, scale_all, vec_all, hyp_low, zp_low, kept):
    nb, _, bw = main_all.shape
    steps, rows, _ = dh_top.shape

    def stepped(*tail):
        return pl.BlockSpec((1,) + tail, lambda s: (steps - 1 - s,) + (0,) * len(tail))

    tails = [
        (rows, H), (rows, H), (rows, NH), (rows, NH), (rows, 4 * NH), (nb, rows, bw), (nb, rows, bw),
        (nb, rows, bw), (nb, rows, bw), (nb, rows, bw), (nb, rows, bw), (rows, 4 * LANES),
    ]
    return pl.pallas_call(
        backward_kernel,
        grid=(steps,),
        in_specs=[
            stepped(rows, H),
            pl.BlockSpec(memory_space=pl.ANY),
            whole(scale_all.shape),
            whole(vec_all.shape),
            whole(hyp_low.shape),
            whole(zp_low.shape),
        ]
        + [stepped(*tail) for tail in tails],
        out_specs=[
            pl.BlockSpec((nb, 1, rows, 2 * bw), lambda s: (0, steps - 1 - s, 0, 0)),
            stepped(rows, 4 * NH),
            stepped(rows, 3 * Z),
            pl.BlockSpec((steps * rows, E), lambda s: (0, 0)),
            pl.BlockSpec((nb, 2, bw), lambda s: (0, 0, 0)),
        ],
        out_shape=[
            jax.ShapeDtypeStruct((nb, steps, rows, 2 * bw), BF16),
            jax.ShapeDtypeStruct((steps, rows, 4 * NH), BF16),
            jax.ShapeDtypeStruct((steps, rows, 3 * Z), BF16),
            jax.ShapeDtypeStruct((steps * rows, E), BF16),
            jax.ShapeDtypeStruct((nb, 2, bw), F32),
        ],
        scratch_shapes=[
            pltpu.VMEM((nb, 2 * E, bw), BF16),
            pltpu.VMEM((rows, H), F32),
            pltpu.VMEM((rows, H), F32),
            pltpu.VMEM((rows, NH), F32),
            pltpu.VMEM((rows, NH), F32),
            pltpu.VMEM((nb, rows, bw), F32),
            pltpu.VMEM((steps, nb, rows, bw), BF16),
            pltpu.VMEM((steps, rows, 4 * NH), BF16),
            pltpu.SemaphoreType.DMA((2,)),
        ],
        compiler_params=pltpu.CompilerParams(vmem_limit_bytes=VMEM_BYTES),
        name="recurrence_backward",
    )(dh_top, main_all, scale_all, vec_all, hyp_low, zp_low, *kept)


def per_device(
    parts,
    token_ids,
    seq_lengths,
    valid_mask,
    embed,
    w_main,
    w_scale,
    w_hyper,
    w_zproj,
    w_out,
    main_vectors,
    embed_row,
    embed_col,
    main_row,
    main_col,
    scale_row,
    scale_col,
    hyper_row,
    hyper_col,
    zproj_row,
    zproj_col,
    out_row,
    out_col,
    vector_state,
):
    n_mp, n_batch = parts
    my = lax.axis_index("mp")
    units = w_main.shape[2]
    emb_part = embed.shape[1]
    vocab_part = w_out.shape[1]
    batch_rows, steps = valid_mask.shape
    own = batch_rows // n_mp
    padded = -(-own // ROW_TILE) * ROW_TILE
    own_total = steps * own
    total = batch_rows * steps
    wide = units % LANES == 0

    def by_owner(values):
        return values.reshape(n_mp, own, steps).transpose(0, 2, 1)

    ids = by_owner(token_ids[:, :steps]).reshape(total)
    targets = by_owner(token_ids[:, 1:]).reshape(total)
    positions = jnp.arange(steps, dtype=jnp.int32)
    valid = valid_mask.astype(F32) * (positions[None, :] < seq_lengths[:, None]).astype(F32)
    weight_rows = by_owner(valid).reshape(total)
    count = lax.psum(jnp.sum(weight_rows), "batch")

    def to_kernel(stacked):
        if wide:
            return stacked
        rows = stacked.shape[1]
        apart = stacked.reshape(n_mp, rows, 4, units).transpose(1, 2, 0, 3)
        return apart.reshape(1, rows, 4 * H)

    def pad_rows(values):
        return jnp.pad(values, ((0, 0), (0, padded - own), (0, 0))) if padded > own else values

    def unpad(values):
        return values[:, :own] if padded > own else values

    x_part = embed[ids].astype(BF16)
    main_own = w_main.astype(BF16).reshape(E + H, 4 * units)
    scale_own = w_scale.astype(BF16).reshape(3 * Z, 4 * units)
    x_own = lax.all_to_all(x_part.reshape(n_mp, own_total, emb_part), "mp", 0, 0)
    x_own = x_own.transpose(1, 0, 2).reshape(steps, own, E)
    main_all = to_kernel(lax.all_gather(main_own, "mp"))
    scale_all = to_kernel(lax.all_gather(scale_own, "mp"))
    vec_all = to_kernel(lax.all_gather(main_vectors.reshape(2, 4 * units), "mp"))
    x_all = lax.all_gather(x_part, "mp", axis=1, tiled=True)
    hyp_low = w_hyper.astype(BF16)
    zp_low = w_zproj.astype(BF16)
    out_low = w_out.astype(BF16)
    hyp_bias = hyp_low[E + H + NH :].astype(F32)
    zp_bias = zp_low[NH:].astype(F32)

    forward = run_forward(
        pad_rows(x_own).reshape(steps * padded, E),
        main_all, scale_all, vec_all, hyp_low, hyp_bias, zp_low[:NH], zp_bias, steps,
    )
    h_own, cprev, tc, hcprev, thc, hh_own, z_own, hg = forward[:8]
    kept = [cprev, tc, hcprev, thc, hg] + list(forward[8:])

    small_own = jnp.concatenate([unpad(h_own), unpad(hh_own), unpad(z_own)], axis=2)
    rows_all = lax.all_gather(small_own.reshape(own_total, H + NH + 3 * Z), "mp")
    h_rows = rows_all[:, :, :H].reshape(total, H)
    logits = matmul(h_rows, out_low)
    local_target = targets - my * vocab_part
    hit = jnp.arange(vocab_part, dtype=jnp.int32)[None, :] == local_target[:, None]
    top = jnp.max(logits, axis=1)
    stats = jnp.stack(
        [
            top,
            jnp.sum(jnp.exp(logits - top[:, None]), axis=1),
            jnp.sum(jnp.where(hit, logits, 0.0), axis=1),
        ]
    )
    stats = lax.all_gather(stats, "mp")
    top_all = jnp.max(stats[:, 0], axis=0)
    exp_sum = jnp.sum(stats[:, 1] * jnp.exp(stats[:, 0] - top_all), axis=0)
    log_total = top_all + jnp.log(exp_sum)
    picked = jnp.sum(stats[:, 2], axis=0)
    loss_sum = lax.psum(jnp.sum((log_total - picked) * weight_rows), "batch")
    grad_logits = (
        (jnp.exp(logits - log_total[:, None]) - hit.astype(F32)) * (weight_rows / count)[:, None]
    ).astype(BF16)
    dh_part = dot_last(grad_logits, out_low).reshape(n_mp, own_total, H)
    dh_parts = lax.all_to_all(dh_part.astype(BF16), "mp", 0, 0)
    dh_top = jnp.sum(dh_parts.astype(F32), axis=0).reshape(steps, own, H)
    g_out = lax.psum(dot_first(h_rows, grad_logits).astype(BF16), "batch").astype(F32)

    dsda, dq_own, dz_own, dx_own, gv = run_backward(
        pad_rows(dh_top), main_all, scale_all, vec_all, hyp_low, zp_low[:NH], kept
    )

    if wide:
        dsda = unpad(dsda.reshape(n_mp * steps, padded, 8 * units))
    else:
        dsda = unpad(dsda.reshape(steps, padded, 8 * H)).reshape(own_total, 8, n_mp, units)
        dsda = dsda.transpose(2, 0, 1, 3)
    dsda = dsda.reshape(n_mp, own_total, 8 * units)
    dx_send = unpad(dx_own.reshape(steps, padded, E)).reshape(own_total, n_mp, emb_part)
    sent = jnp.concatenate([dsda, dx_send.transpose(1, 0, 2)], axis=2)
    sent = lax.all_to_all(sent, "mp", 0, 0).reshape(total, 8 * units + emb_part)
    ds = sent[:, : 4 * units].astype(F32)
    da_low = sent[:, 4 * units : 8 * units]
    dx_part = sent[:, 8 * units :]
    back_own = jnp.concatenate([unpad(dq_own), unpad(dz_own)], axis=2)
    back_all = lax.all_gather(back_own.reshape(own_total, 4 * NH + 3 * Z), "mp")
    back_all = back_all.reshape(total, 4 * NH + 3 * Z)
    dq_all = back_all[:, : 4 * NH]
    dz_all = back_all[:, 4 * NH :]

    before = jnp.concatenate(
        [jnp.zeros_like(rows_all[:, :own]), rows_all[:, : own_total - own]], axis=1
    ).reshape(total, H + NH + 3 * Z)
    h_before = before[:, :H]
    hh_before = before[:, H : H + NH]
    hh_rows = rows_all[:, :, H : H + NH].reshape(total, NH)
    z_rows = rows_all[:, :, H + NH :].reshape(total, 3, Z)
    uh = matmul(h_before, main_own[E:])
    ux = matmul(x_all, main_own[:E])
    scale_blocks = scale_own.reshape(3, Z, 4 * units)
    one0 = 1.0 + matmul(z_rows[:, 0], scale_blocks[0])
    one1 = 1.0 + matmul(z_rows[:, 1], scale_blocks[1])
    g_in = dot_first(x_all, (ds * one1).astype(BF16))
    g_rec = dot_first(h_before, (ds * one0).astype(BF16))
    d_scales = [(ds * uh).astype(BF16), (ds * ux).astype(BF16), da_low]
    g_scale = jnp.stack([dot_first(z_rows[:, k], d_scales[k]) for k in range(3)])
    nh_part = NH // n_mp
    left = jnp.concatenate(
        [
            x_part,
            lax.dynamic_slice_in_dim(h_before, my * units, units, 1),
            lax.dynamic_slice_in_dim(hh_before, my * nh_part, nh_part, 1),
        ],
        axis=1,
    )
    g_hyper = dot_first(left, dq_all)
    g_zproj = dot_first(lax.dynamic_slice_in_dim(hh_rows, my * nh_part, nh_part, 1), dz_all)

    dx_all = lax.all_gather(dx_part, "batch").reshape(n_batch * total, emb_part)
    ids_all = lax.all_gather(ids, "batch").reshape(n_batch * total)
    g_embed = jax.ops.segment_sum(dx_all.astype(F32), ids_all, num_segments=embed.shape[0])
    g_in, g_rec, g_scale, g_hyper, g_zproj = lax.psum(
        tuple(g.astype(BF16) for g in (g_in, g_rec, g_scale, g_hyper, g_zproj)), "batch"
    )
    flat = lax.all_gather(
        jnp.concatenate([g_hyper.reshape(-1, LANES), g_zproj.reshape(-1, LANES)], axis=0), "mp"
    ).astype(F32)
    n_hyp = g_hyper.size // LANES
    all_hyper = flat[:, :n_hyp].reshape(n_mp, emb_part + units + nh_part, 4 * NH)
    all_zproj = flat[:, n_hyp:].reshape(n_mp * nh_part, 3 * Z)
    if wide:
        gv_parts = gv.reshape(n_mp, 2, 4, units)
    else:
        gv_parts = gv.reshape(2, 4, n_mp, units).transpose(2, 0, 1, 3)
    gv_parts, bias_sums = lax.psum(
        (gv_parts, jnp.sum(back_own.astype(F32), axis=(0, 1))), ("batch", "mp")
    )
    g_vec = lax.dynamic_index_in_dim(gv_parts, my, 0, False)
    g_hyper = jnp.concatenate(
        [
            all_hyper[:, :emb_part].reshape(E, 4 * NH),
            all_hyper[:, emb_part : emb_part + units].reshape(H, 4 * NH),
            all_hyper[:, emb_part + units :].reshape(NH, 4 * NH),
            bias_sums[None, : 4 * NH],
        ],
        axis=0,
    )
    g_zproj = jnp.concatenate([all_zproj, bias_sums[None, 4 * NH :]], axis=0)
    g_main = jnp.concatenate([g_in, g_rec], axis=0).astype(F32).reshape(E + H, 4, units)
    g_scale = g_scale.astype(F32).reshape(3, Z, 4, units)

    sq_embed = g_embed * g_embed + EPS_FACT
    sq_main = g_main * g_main + EPS_FACT
    sq_scale = g_scale * g_scale + EPS_FACT
    sq_hyper = g_hyper * g_hyper + EPS_FACT
    sq_zproj = g_zproj * g_zproj + EPS_FACT
    sq_out = g_out * g_out + EPS_FACT
    row_out = lax.psum(jnp.sum(sq_out, axis=1), "mp")
    row_embed, row_main, row_scale = lax.psum(
        (
            jnp.sum(sq_embed, axis=1),
            jnp.sum(sq_main, axis=(1, 2)),
            jnp.sum(sq_scale, axis=(2, 3)),
        ),
        "mp",
    )
    res_embed = adafactor(
        embed, g_embed, embed_row, embed_col, row_embed / E, jnp.mean(sq_embed, axis=0), 0, 1.0
    )
    res_main = adafactor(
        w_main,
        g_main,
        main_row,
        main_col,
        row_main / (4 * H),
        jnp.mean(sq_main, axis=0),
        0,
        1.0 / math.sqrt(E),
    )
    res_scale = adafactor(
        w_scale,
        g_scale,
        scale_row,
        scale_col,
        row_scale / (4 * H),
        jnp.mean(sq_scale, axis=1),
        1,
        1.0 / math.sqrt(Z),
    )
    res_hyper = adafactor(
        w_hyper,
        g_hyper,
        hyper_row,
        hyper_col,
        jnp.mean(sq_hyper, axis=1),
        jnp.mean(sq_hyper, axis=0),
        0,
        1.0 / math.sqrt(E + H + NH + 1),
    )
    res_zproj = adafactor(
        w_zproj,
        g_zproj,
        zproj_row,
        zproj_col,
        jnp.mean(sq_zproj, axis=1),
        jnp.mean(sq_zproj, axis=0),
        0,
        2.0 / math.sqrt(NH),
    )
    res_out = adafactor(
        w_out, g_out, out_row, out_col, row_out / V, jnp.mean(sq_out, axis=0), 0, 3.0 / math.sqrt(H)
    )
    decay = 1.0 - STEP ** (-0.8)
    state_new = decay * vector_state + (1.0 - decay) * (g_vec * g_vec + EPS_FACT)
    vectors_new = main_vectors - 0.1 * g_vec * lax.rsqrt(state_new)
    return (
        (loss_sum, count)
        + res_embed
        + res_main
        + res_scale
        + res_hyper
        + res_zproj
        + res_out
        + (g_vec, state_new, vectors_new)
    )


def solution(mesh):
    rep = P()
    placed = (
        P("batch", None),
        P("batch"),
        P("batch", None),
        P(None, "mp"),
        P(None, None, "mp"),
        P(None, None, None, "mp"),
        rep,
        rep,
        P(None, "mp"),
        P(None, None, "mp"),
        rep,
        P("mp"),
        rep,
        P(None, "mp"),
        rep,
        P(None, None, "mp"),
        rep,
        rep,
        rep,
        rep,
        rep,
        P("mp"),
        P(None, None, "mp"),
    )
    return jax.shard_map(
        functools.partial(per_device, (mesh.shape["mp"], mesh.shape["batch"])),
        mesh=mesh,
        in_specs=placed,
        out_specs=(
            rep,
            rep,
            P(None, "mp"),
            P(None, "mp"),
            rep,
            P("mp"),
            P(None, None, "mp"),
            P(None, None, "mp"),
            rep,
            P(None, "mp"),
            P(None, None, None, "mp"),
            P(None, None, None, "mp"),
            rep,
            P(None, None, "mp"),
            rep,
            rep,
            rep,
            rep,
            rep,
            rep,
            rep,
            rep,
            P(None, "mp"),
            P(None, "mp"),
            rep,
            P("mp"),
            P(None, None, "mp"),
            P(None, None, "mp"),
            P(None, None, "mp"),
        ),
        check_vma=False,
    )
```

```python
import functools
import math

import jax
import jax.numpy as jnp
from jax import lax
from jax.experimental import pallas as pl
from jax.experimental.pallas import tpu as pltpu
from jax.sharding import PartitionSpec as P

E = 1024
H = 1024
V = 10240
NH = 128
Z = 64
STEP = 10
LANES = 128
ROW_TILE = 16
VMEM_BYTES = 56 * 1024 * 1024

EPS_NORM = 1e-05
EPS_FACT = 1e-30

F32 = jnp.float32
BF16 = jnp.bfloat16


def matmul(left, right):
    return jnp.dot(left, right, preferred_element_type=F32)


def dot_last(left, right):
    return lax.dot_general(left, right, (((1,), (1,)), ((), ())), preferred_element_type=F32)


def dot_first(left, right):
    return lax.dot_general(left, right, (((0,), (0,)), ((), ())), preferred_element_type=F32)


def adafactor(weight, grad, row_old, col_old, row_mean, col_mean, lead, rate):
    decay = 1.0 - STEP ** (-0.8)
    row_new = decay * row_old + (1.0 - decay) * row_mean
    col_new = decay * col_old + (1.0 - decay) * col_mean
    relative = row_new / jnp.mean(row_new, axis=-1, keepdims=True)
    relative = relative.reshape(relative.shape + (1,) * (grad.ndim - relative.ndim))
    spread = col_new[None] if lead == 0 else col_new[:, None]
    updated = weight - rate * grad * lax.rsqrt(relative * spread)
    return (grad, updated, row_new, col_new)


STACK_ROWS = 2304
SCALE_AT = 2 * E
VEC_AT = SCALE_AT + 3 * Z
TAIL_ROWS = STACK_ROWS - SCALE_AT
PACK = H + NH + 4 * Z
STAT_AT = 3 * Z
VOCAB_BLOCK = 256
SLOTS = (0, 2, 4, 6, 1, 3, 5, 7)


def swap(values, axis, size, bit):
    return lax.ppermute(values, axis, [(i, i ^ bit) for i in range(size)])


def tree_sum(values, axis, size):
    if size & (size - 1):
        return lax.psum(values, axis)
    bit = 1
    while bit < size:
        values = values + swap(values, axis, size, bit)
        bit *= 2
    return values


def tie(*values):
    return lax.optimization_barrier(values)


def weight_tail(w_scale, main_vectors):
    width = 4 * main_vectors.shape[2]
    vec = main_vectors.reshape(2, width)
    terms = []
    for _ in range(3):
        term = lax.reduce_precision(vec, 8, 7)
        terms.append(term.astype(BF16))
        vec = vec - term
    return jnp.concatenate(
        [w_scale.astype(BF16).reshape(3 * Z, width)]
        + terms
        + [jnp.zeros((STACK_ROWS - VEC_AT - 6, width), BF16)],
        axis=0,
    )


def piece_copies(refs, plan, main_v, sem, only=None):
    if plan is None:
        return [] if only else [pltpu.make_async_copy(refs[0], main_v, sem.at[0])]
    me = lax.axis_index("mp")
    b = lax.axis_index("batch")
    quarter = SCALE_AT // 4
    tail_quarter = TAIL_ROWS // 4
    copies = []
    spot = -1

    def add(bits, ref, source, target, rows):
        copies.append(
            pltpu.make_async_copy(
                ref.at[pl.ds(source, rows)],
                main_v.at[me ^ bits, pl.ds(target, rows)],
                sem.at[spot],
            )
        )

    for ref, (bits, over, first, rows) in zip(refs, plan):
        spot += 2
        if only is not None and bits != only:
            continue
        if over is None:
            add(bits, ref, 0, first, rows)
            continue
        index = b ^ over
        of_main = max(0, min(rows, quarter - first))
        if of_main:
            add(bits, ref, 0, pl.multiple_of(index * quarter + first, ROW_TILE), of_main)
        if rows > of_main:
            spot -= 1
            start = SCALE_AT + index * tail_quarter + first + of_main - quarter
            add(bits, ref, of_main, pl.multiple_of(start, ROW_TILE), rows - of_main)
            spot += 1
    return copies


def copy_count(plan):
    return 1 if plan is None else 2 * len(plan)


def load_vectors(vec_ref, main_v):
    for m in range(main_v.shape[0]):
        terms = main_v[m, VEC_AT : VEC_AT + ROW_TILE].astype(F32)
        vec_ref[m] = terms[0:2] + terms[2:4] + terms[4:6]


def masked_thirds(z_wide):
    lane = lax.broadcasted_iota(jnp.int32, z_wide.shape, 1) // Z
    zero = jnp.zeros_like(z_wide)
    return jnp.concatenate([jnp.where(lane == k, z_wide, zero) for k in range(3)], axis=0)


def beside(wide, columns):
    lane = lax.broadcasted_iota(jnp.int32, wide.shape, 1)
    count = len(columns)
    for spot, column in enumerate(columns):
        high = column.astype(BF16).astype(F32)
        wide = jnp.where(lane == STAT_AT + spot, high, wide)
        wide = jnp.where(lane == STAT_AT + count + spot, column - high, wide)
    return wide.astype(BF16)


def column_of(wide, count, spot):
    return wide[:, STAT_AT + spot : STAT_AT + spot + 1] + wide[
        :, STAT_AT + count + spot : STAT_AT + count + spot + 1
    ]


def forward_kernel(plan, x_ref, hyp_ref, hypb_ref, zp_ref, zpb_ref, *refs):
    n_pieces = 1 if plan is None else len(plan)
    forward_body(plan, x_ref, hyp_ref, hypb_ref, zp_ref, zpb_ref, refs[:n_pieces], *refs[n_pieces:])


def forward_body(
    plan, x_ref, hyp_ref, hypb_ref, zp_ref, zpb_ref, piece_refs,
    pack_out, cprev_out, tc_out, hcprev_out, thc_out, hg_out,
    ux_out, uh_out, one0_out, one1_out, n_out, act_out, rstd_out, vec_out,
    main_v, prex_s, h_s, c_s, hh_s, hc_s, sem,
):
    t = pl.program_id(0)
    nb, _, bw = main_v.shape
    bu = bw // 4
    steps, _, rows, _ = ux_out.shape

    @pl.when(t == 0)
    def _():
        for copy in piece_copies(piece_refs, plan, main_v, sem):
            copy.start()
        prex_s[...] = (matmul(x_ref[...], hyp_ref[:E]) + hypb_ref[...]).reshape(steps, rows, 4 * NH)
        h_s[...] = jnp.zeros_like(h_s)
        c_s[...] = jnp.zeros_like(c_s)
        hh_s[...] = jnp.zeros_like(hh_s)
        hc_s[...] = jnp.zeros_like(hc_s)
        me = 0 if plan is None else lax.axis_index("mp")
        for bits in range(nb):
            for copy in piece_copies(piece_refs, plan, main_v, sem, bits):
                copy.wait()
            m = me ^ bits
            ux = matmul(x_ref[...], main_v[m, :E])
            ux_out[:, m] = ux.reshape(steps, rows, bw)
        load_vectors(vec_out, main_v)

    h_prev = h_s[...]
    hh_prev = hh_s[...]
    hc_prev = hc_s[...]
    q = prex_s[t] + matmul(h_prev, hyp_ref[E : E + H]) + matmul(hh_prev, hyp_ref[E + H : E + H + NH])
    q_in = jax.nn.sigmoid(q[:, :NH])
    q_forget = jax.nn.sigmoid(q[:, NH : 2 * NH])
    q_out = jax.nn.sigmoid(q[:, 2 * NH : 3 * NH])
    q_cell = jnp.tanh(q[:, 3 * NH :])
    hc = q_forget * hc_prev + q_in * q_cell
    thc = jnp.tanh(hc)
    hh = (q_out * thc).astype(BF16)
    z_wide = matmul(hh, zp_ref[...]) + zpb_ref[...]
    hcprev_out[0] = hc_prev
    thc_out[0] = thc
    hg_out[0, :, :NH] = q_in
    hg_out[0, :, NH : 2 * NH] = q_forget
    hg_out[0, :, 2 * NH : 3 * NH] = q_out
    hg_out[0, :, 3 * NH :] = q_cell
    pack_out[0, :, H : H + NH] = hh
    hh_s[...] = hh
    hc_s[...] = hc

    thirds = masked_thirds(z_wide.astype(BF16))
    sums = [jnp.zeros((rows, LANES), F32) for _ in range(4)]
    squares = [jnp.zeros((rows, LANES), F32) for _ in range(4)]
    for m in range(nb):
        scl = matmul(thirds, main_v[m, SCALE_AT:])
        uh = matmul(h_prev, main_v[m, E : 2 * E])
        one0 = 1.0 + scl[:rows]
        one1 = 1.0 + scl[rows : 2 * rows]
        s = one0 * uh + one1 * ux_out[t, m]
        uh_out[0, m] = uh
        one0_out[0, m] = one0
        one1_out[0, m] = one1
        act_out[0, m] = scl[2 * rows :]
        n_out[0, m] = s
        for g in range(4):
            for j in range(bu // LANES):
                piece = s[:, g * bu + j * LANES : g * bu + (j + 1) * LANES]
                sums[g] += piece
                squares[g] += piece * piece
    centres, rstds = [], []
    for g in range(4):
        centre = jnp.sum(sums[g], axis=1, keepdims=True) / H
        square = jnp.sum(squares[g], axis=1, keepdims=True) / H
        rstd = lax.rsqrt(square - centre * centre + EPS_NORM)
        centres.append(centre)
        rstds.append(rstd)
        rstd_out[0, :, g * LANES : (g + 1) * LANES] = jnp.broadcast_to(rstd, (rows, LANES))
    pack_out[0, :, H + NH :] = beside(z_wide, centres + rstds)

    for m in range(nb):
        cols = slice(m * bu, (m + 1) * bu)
        gates = []
        for g in range(4):
            here = slice(g * bu, (g + 1) * bu)
            n = (n_out[0, m, :, here] - centres[g]) * rstds[g]
            n_out[0, m, :, here] = n
            pre = vec_out[m, 0:1, here] * n + vec_out[m, 1:2, here] + act_out[0, m, :, here]
            gate = jnp.tanh(pre) if g == 3 else jax.nn.sigmoid(pre)
            act_out[0, m, :, here] = gate
            gates.append(gate)
        c_prev = c_s[:, cols]
        c_now = gates[1] * c_prev + gates[0] * gates[3]
        tc = jnp.tanh(c_now)
        h_now = (gates[2] * tc).astype(BF16)
        cprev_out[0, :, cols] = c_prev
        tc_out[0, :, cols] = tc
        c_s[:, cols] = c_now
        h_s[:, cols] = h_now
        pack_out[0, :, cols] = h_now


def turn_kernel(plan, me_ref, *refs):
    n_pieces = 1 if plan is None else len(plan)
    in_out, rec_out, tail_out, main_v, sem = refs[n_pieces:]
    step = pl.program_id(0)

    @pl.when(step == 0)
    def _():
        for copy in piece_copies(refs[:n_pieces], plan, main_v, sem):
            copy.start()

    for bits in range(main_v.shape[0]):

        @pl.when(step == bits)
        def _():
            for copy in piece_copies(refs[:n_pieces], plan, main_v, sem, bits):
                copy.wait()

    m = step ^ me_ref[0]
    in_out[0] = main_v[m, :E]
    rec_out[0] = main_v[m, E : 2 * E].T
    tail_out[0] = main_v[m, SCALE_AT:].T


def run_turn(blocks, plan, pieces):
    nb, bw = blocks
    me = jnp.zeros((1,), jnp.int32) if plan is None else lax.axis_index("mp").reshape(1)
    shapes = [(E, bw), (bw, H), (bw, TAIL_ROWS)]
    single = dict(pipeline_mode=pl.Buffered(1)) if nb == 1 else {}
    return pl.pallas_call(
        functools.partial(turn_kernel, plan),
        grid_spec=pltpu.PrefetchScalarGridSpec(
            num_scalar_prefetch=1,
            grid=(nb,),
            in_specs=[pl.BlockSpec(memory_space=pl.ANY)] * len(pieces),
            out_specs=[
                pl.BlockSpec((1,) + shape, lambda i, me: (i ^ me[0], 0, 0), **single) for shape in shapes
            ],
            scratch_shapes=[
                pltpu.VMEM((nb, STACK_ROWS, bw), BF16),
                pltpu.SemaphoreType.DMA((copy_count(plan),)),
            ],
        ),
        out_shape=[jax.ShapeDtypeStruct((nb,) + shape, BF16) for shape in shapes],
        compiler_params=kernel_params(),
        cost_estimate=pl.CostEstimate(flops=10**7, bytes_accessed=40_000_000, transcendentals=0),
        name="turn_weights",
    )(me, *pieces)


def backward_kernel(
    plan, in_hbm, rec_hbm, tail_hbm, dh_ref, hyp_ref, zp_ref,
    cprev_ref, tc_ref, hcprev_ref, thc_ref, hg_ref,
    ux_ref, uh_ref, one0_ref, one1_ref, n_ref, act_ref, rstd_ref, vec_ref,
    cols_out, dx_out, gv_out,
    in_v, rec_v, tail_v, dh_s, dc_s, dhh_s, dhc_s, da_s, dux_s, dq_s, sem,
):
    step = pl.program_id(0)
    nb, _, bw = in_v.shape
    bu = bw // 4
    steps, rows, _ = dq_s.shape
    t = steps - 1 - step
    me = 0 if plan is None else lax.axis_index("mp")
    copies = [
        pltpu.make_async_copy(source, target, sem.at[spot])
        for spot, (source, target) in enumerate(((rec_hbm, rec_v), (tail_hbm, tail_v), (in_hbm, in_v)))
    ]

    @pl.when(step == 0)
    def _():
        for copy in copies:
            copy.start()
        dh_s[...] = jnp.zeros_like(dh_s)
        dc_s[...] = jnp.zeros_like(dc_s)
        dhh_s[...] = jnp.zeros_like(dhh_s)
        dhc_s[...] = jnp.zeros_like(dhc_s)
        gv_out[...] = jnp.zeros_like(gv_out)

    first = [jnp.zeros((rows, LANES), F32) for _ in range(4)]
    second = [jnp.zeros((rows, LANES), F32) for _ in range(4)]
    for m in range(nb):
        cols = slice(m * bu, (m + 1) * bu)
        gate = [act_ref[0, m, :, g * bu : (g + 1) * bu] for g in range(4)]
        tc = tc_ref[0, :, cols]
        dh = dh_ref[0, :, cols] + dh_s[:, cols]
        dc = dc_s[:, cols] + dh * gate[2] * (1.0 - tc * tc)
        da = [
            dc * gate[3] * gate[0] * (1.0 - gate[0]),
            dc * cprev_ref[0, :, cols] * gate[1] * (1.0 - gate[1]),
            dh * tc * gate[2] * (1.0 - gate[2]),
            dc * gate[0] * (1.0 - gate[3] * gate[3]),
        ]
        dc_s[:, cols] = dc * gate[1]
        if plan is not None:
            bits = me ^ m
            spot = bits // 2 + (nb // 2) * (bits % 2)
            cols_out[spot, t, :, :bu] = dh.astype(BF16)
        for g in range(4):
            here = slice(g * bu, (g + 1) * bu)
            n = n_ref[0, m, :, here]
            da_s[m, :, here] = da[g]
            if plan is None:
                gv_out[m, 0:1, here] += jnp.sum(da[g] * n, axis=0, keepdims=True)
                gv_out[m, 1:2, here] += jnp.sum(da[g], axis=0, keepdims=True)
            dn = vec_ref[m, 0:1, here] * da[g]
            dnn = dn * n
            for j in range(bu // LANES):
                first[g] += dn[:, j * LANES : (j + 1) * LANES]
                second[g] += dnn[:, j * LANES : (j + 1) * LANES]
    means = [
        (jnp.sum(first[g], axis=1, keepdims=True) / H, jnp.sum(second[g], axis=1, keepdims=True) / H)
        for g in range(4)
    ]

    @pl.when(step == 0)
    def _():
        copies[0].wait()
        copies[1].wait()

    dz_all = jnp.zeros((3 * rows, 4 * Z), F32)
    dh_rec = jnp.zeros((rows, H), F32)
    for m in range(nb):
        ds_parts = []
        for g in range(4):
            here = slice(g * bu, (g + 1) * bu)
            dn = vec_ref[m, 0:1, here] * da_s[m, :, here]
            rstd = rstd_ref[0, :, g * LANES : g * LANES + 1]
            ds_parts.append(rstd * (dn - means[g][0] - n_ref[0, m, :, here] * means[g][1]))
        ds = jnp.concatenate(ds_parts, axis=1)
        da_low = da_s[m].astype(BF16)
        if plan is None:
            cols_out[m, t, :, :bw] = ds.astype(BF16)
            cols_out[m, t, :, bw:] = da_low
        stack = jnp.concatenate(
            [(ds * uh_ref[0, m]).astype(BF16), (ds * ux_ref[0, m]).astype(BF16), da_low], axis=0
        )
        dz_all += matmul(stack, tail_v[m])
        duh = (ds * one0_ref[0, m]).astype(BF16)
        dux_s[t, m] = (ds * one1_ref[0, m]).astype(BF16)
        dh_rec += matmul(duh, rec_v[m])

    lane = lax.broadcasted_iota(jnp.int32, (rows, 4 * Z), 1) // Z
    dz = jnp.zeros((rows, 4 * Z), F32)
    for k in range(3):
        dz = jnp.where(lane == k, dz_all[k * rows : (k + 1) * rows], dz)
    half = 2 * NH
    cols_out[nb + 2, t, :, :half] = beside(dz, [m[0] for m in means] + [m[1] for m in means])
    q_in = hg_ref[0, :, :NH]
    q_forget = hg_ref[0, :, NH : 2 * NH]
    q_out = hg_ref[0, :, 2 * NH : 3 * NH]
    q_cell = hg_ref[0, :, 3 * NH :]
    thc = thc_ref[0]
    dhh = dhh_s[...] + dot_last(dz.astype(BF16), zp_ref[...])
    dhc = dhc_s[...] + dhh * q_out * (1.0 - thc * thc)
    dq = jnp.concatenate(
        [
            dhc * q_cell * q_in * (1.0 - q_in),
            dhc * hcprev_ref[0] * q_forget * (1.0 - q_forget),
            dhh * thc * q_out * (1.0 - q_out),
            dhc * q_in * (1.0 - q_cell * q_cell),
        ],
        axis=1,
    ).astype(BF16)
    cols_out[nb, t, :, :half] = dq[:, :half]
    cols_out[nb + 1, t, :, :half] = dq[:, half:]
    dq_s[t] = dq
    dhc_s[...] = dhc * q_forget
    dhh_s[...] = dot_last(dq, hyp_ref[E + H : E + H + NH])
    dh_s[...] = dh_rec + dot_last(dq, hyp_ref[E : E + H])

    @pl.when(step == steps - 1)
    def _():
        copies[2].wait()
        dx = dot_last(dq_s[...].reshape(steps * rows, 4 * NH), hyp_ref[:E])
        for m in range(nb):
            dx += dot_last(dux_s[:, m].reshape(steps * rows, bw), in_v[m])
        if plan is None:
            dx_out[...] = dx.astype(dx_out.dtype)
        else:
            for m in range(nb):
                bits = me ^ m
                spot = bits // 2 + (nb // 2) * (bits % 2)
                part = dx[:, m * bu : (m + 1) * bu].astype(BF16)
                cols_out[spot, :, :, bu : 2 * bu] = part.reshape(steps, rows, bu)


def whole(shape):
    return pl.BlockSpec(shape, lambda t: (0,) * len(shape), pipeline_mode=pl.Buffered(1))


def kernel_params():
    return pltpu.CompilerParams(vmem_limit_bytes=VMEM_BYTES)


def run_forward(x_rows, blocks, plan, pieces, hyp_low, hyp_bias, zp_wide, zp_bias, steps):
    nb, bw = blocks
    rows = x_rows.shape[0] // steps

    def stepped(*tail):
        return pl.BlockSpec((1,) + tail, lambda t: (t,) + (0,) * len(tail))

    tails = [
        (BF16, (rows, PACK)), (F32, (rows, H)), (F32, (rows, H)), (F32, (rows, NH)), (F32, (rows, NH)),
        (F32, (rows, 4 * NH)), (F32, (nb, rows, bw)), (F32, (nb, rows, bw)), (F32, (nb, rows, bw)),
        (F32, (nb, rows, bw)), (F32, (nb, rows, bw)), (F32, (nb, rows, bw)), (F32, (rows, 4 * LANES)),
    ]
    out_specs = [stepped(*tail) for _, tail in tails]
    out_specs[6] = pl.BlockSpec((steps, nb, rows, bw), lambda t: (0, 0, 0, 0))
    out_shape = [jax.ShapeDtypeStruct((steps,) + tail, dtype) for dtype, tail in tails]
    work = steps * rows * 4 * H * (2 * H + E + 3 * 4 * Z)
    return pl.pallas_call(
        functools.partial(forward_kernel, plan),
        grid=(steps,),
        in_specs=[
            whole(x_rows.shape),
            whole(hyp_low.shape),
            whole(hyp_bias.shape),
            whole(zp_wide.shape),
            whole(zp_bias.shape),
        ]
        + [pl.BlockSpec(memory_space=pl.ANY)] * len(pieces),
        out_specs=out_specs + [pl.BlockSpec((nb, 2, bw), lambda t: (0, 0, 0))],
        out_shape=out_shape + [jax.ShapeDtypeStruct((nb, 2, bw), F32)],
        scratch_shapes=[
            pltpu.VMEM((nb, STACK_ROWS, bw), BF16),
            pltpu.VMEM((steps, rows, 4 * NH), F32),
            pltpu.VMEM((rows, H), BF16),
            pltpu.VMEM((rows, H), F32),
            pltpu.VMEM((rows, NH), BF16),
            pltpu.VMEM((rows, NH), F32),
            pltpu.SemaphoreType.DMA((copy_count(plan),)),
        ],
        compiler_params=kernel_params(),
        cost_estimate=pl.CostEstimate(flops=2 * work, bytes_accessed=40_000_000, transcendentals=0),
        name="recurrence_forward",
    )(x_rows, hyp_low, hyp_bias, zp_wide, zp_bias, *pieces)


def run_backward(dh_top, blocks, plan, turned, hyp_low, zp_wide, kept):
    nb, bw = blocks
    steps, rows, _ = dh_top.shape

    def stepped(*tail):
        return pl.BlockSpec((1,) + tail, lambda s: (steps - 1 - s,) + (0,) * len(tail))

    def still(shape):
        return pl.BlockSpec(shape, lambda s: (0,) * len(shape))

    tails = [
        (rows, H), (rows, H), (rows, NH), (rows, NH), (rows, 4 * NH), (nb, rows, bw), (nb, rows, bw),
        (nb, rows, bw), (nb, rows, bw), (nb, rows, bw), (nb, rows, bw), (rows, 4 * LANES),
    ]
    per_owner = 2 * bw if plan is None else 2 * (bw // 4)
    outs = [
        jax.ShapeDtypeStruct((nb + 3, steps, rows, per_owner), BF16),
        jax.ShapeDtypeStruct((steps * rows, E), BF16),
        jax.ShapeDtypeStruct((nb, 2, bw), F32),
    ]
    work = steps * rows * 4 * H * (2 * H + E + 3 * 4 * Z)
    return pl.pallas_call(
        functools.partial(backward_kernel, plan),
        grid=(steps,),
        in_specs=[pl.BlockSpec(memory_space=pl.ANY)] * len(turned)
        + [stepped(rows, H), whole(hyp_low.shape), whole(zp_wide.shape)]
        + [stepped(*tail) for tail in tails]
        + [whole((nb, 2, bw))],
        out_specs=[
            still(outs[0].shape),
            still(outs[1].shape),
            still(outs[2].shape),
        ],
        out_shape=outs,
        scratch_shapes=[
            pltpu.VMEM((nb, E, bw), BF16),
            pltpu.VMEM((nb, bw, H), BF16),
            pltpu.VMEM((nb, bw, TAIL_ROWS), BF16),
            pltpu.VMEM((rows, H), F32),
            pltpu.VMEM((rows, H), F32),
            pltpu.VMEM((rows, NH), F32),
            pltpu.VMEM((rows, NH), F32),
            pltpu.VMEM((nb, rows, bw), F32),
            pltpu.VMEM((steps, nb, rows, bw), BF16),
            pltpu.VMEM((steps, rows, 4 * NH), BF16),
            pltpu.SemaphoreType.DMA((3,)),
        ],
        compiler_params=kernel_params(),
        cost_estimate=pl.CostEstimate(flops=2 * work, bytes_accessed=60_000_000, transcendentals=0),
        name="recurrence_backward",
    )(*turned, dh_top, hyp_low, zp_wide, *kept)


def column_forward_kernel(
    steps, slots_ref, pack0_ref, pack1_ref, x0_ref, x1_ref, main_ref, tail_ref, vec_ref,
    uh_out, ux_out, one0_out, one1_out, n_out, act_out, cprev_out, tc_out, rstd_out,
    left_out, x_out, hb_out, hhb_out, hh_out, z_out,
):
    _, total, _ = pack0_ref.shape
    rows = total // steps
    width = main_ref.shape[1]
    units = width // 4

    def one_before(values):
        return jnp.concatenate([jnp.zeros_like(values[:rows]), values[: total - rows]], axis=0)

    for half, (pack_ref, x_ref) in enumerate(((pack0_ref, x0_ref), (pack1_ref, x1_ref))):
        h_before = one_before(pack_ref[0, :, :H])
        hh = pack_ref[0, :, H : H + NH]
        z_wide = pack_ref[0, :, H + NH :]
        x_now = jnp.concatenate([x_ref[k, 0] for k in range(x_ref.shape[0])], axis=1)
        mine = pl.ds(pl.multiple_of(slots_ref[0] * units, units), units)
        part = x_ref.shape[3]
        left_out[half, 0, :, :part] = x_ref[slots_ref[0], 0]
        left_out[half, 0, :, part:] = one_before(pack_ref[0, :, mine])
        x_out[half, 0] = x_now
        hb_out[half, 0] = h_before
        hhb_out[half, 0] = one_before(hh)
        hh_out[half, 0] = hh
        z_out[half, 0] = z_wide
        stats = z_wide.astype(F32)
        uh = matmul(h_before, main_ref[E : 2 * E])
        ux = matmul(x_now, main_ref[:E])
        scl = matmul(masked_thirds(z_wide), tail_ref[...])
        one0 = 1.0 + scl[:total]
        one1 = 1.0 + scl[total : 2 * total]
        s = one0 * uh + one1 * ux
        uh_out[half, 0] = uh
        ux_out[half, 0] = ux
        one0_out[half, 0] = one0
        one1_out[half, 0] = one1
        for g in range(4):
            here = slice(g * units, (g + 1) * units)
            rstd = column_of(stats, 8, 4 + g)
            n = (s[:, here] - column_of(stats, 8, g)) * rstd
            pre = vec_ref[0:1, here] * n + vec_ref[1:2, here] + scl[2 * total :, here]
            n_out[half, 0, :, here] = n
            act_out[half, 0, :, here] = jnp.tanh(pre) if g == 3 else jax.nn.sigmoid(pre)
            rstd_out[half, 0, :, here] = jnp.broadcast_to(rstd, (total, units))
        c = jnp.zeros((rows, units), F32)
        for t in range(steps):
            now = slice(t * rows, (t + 1) * rows)
            gate = [act_out[half, 0, now, g * units : (g + 1) * units] for g in range(4)]
            cprev_out[half, 0, now] = c
            c = gate[1] * c + gate[0] * gate[3]
            tc_out[half, 0, now] = jnp.tanh(c)


def column_backward_kernel(
    steps, dh0_ref, dh1_ref, back0_ref, back1_ref, vec_ref,
    uh_ref, ux_ref, one0_ref, one1_ref, n_ref, act_ref, cprev_ref, tc_ref, rstd_ref,
    dux_out, duh_out, d0_out, d1_out, da_out, gv_out,
    dc_s,
):
    _, total, units = dh0_ref.shape
    rows = total // steps

    @pl.when(pl.program_id(0) == 0)
    def _():
        gv_out[...] = jnp.zeros_like(gv_out)

    for half, (dh_ref, back_ref) in enumerate(((dh0_ref, back0_ref), (dh1_ref, back1_ref))):
        means = back_ref[0, 0].astype(F32)
        dh = dh_ref[0].astype(F32)
        gate = [act_ref[half, 0, :, g * units : (g + 1) * units] for g in range(4)]
        tc = tc_ref[half, 0]
        local = dh * gate[2] * (1.0 - tc * tc)
        dc = jnp.zeros((rows, units), F32)
        for t in reversed(range(steps)):
            now = slice(t * rows, (t + 1) * rows)
            dc = dc + local[now]
            dc_s[now] = dc
            dc = dc * gate[1][now]
        dc = dc_s[...]
        da = [
            dc * gate[3] * gate[0] * (1.0 - gate[0]),
            dc * cprev_ref[half, 0] * gate[1] * (1.0 - gate[1]),
            dh * tc * gate[2] * (1.0 - gate[2]),
            dc * gate[0] * (1.0 - gate[3] * gate[3]),
        ]
        for g in range(4):
            here = slice(g * units, (g + 1) * units)
            n = n_ref[half, 0, :, here]
            gv_out[0:1, here] += jnp.sum(da[g] * n, axis=0, keepdims=True)
            gv_out[1:2, here] += jnp.sum(da[g], axis=0, keepdims=True)
            dn = vec_ref[0:1, here] * da[g]
            ds = rstd_ref[half, 0, :, here] * (
                dn - column_of(means, 8, g) - n * column_of(means, 8, 4 + g)
            )
            dux_out[half, 0, :, here] = (ds * one1_ref[half, 0, :, here]).astype(BF16)
            duh_out[half, 0, :, here] = (ds * one0_ref[half, 0, :, here]).astype(BF16)
            d0_out[half, 0, :, here] = (ds * uh_ref[half, 0, :, here]).astype(BF16)
            d1_out[half, 0, :, here] = (ds * ux_ref[half, 0, :, here]).astype(BF16)
            da_out[half, 0, :, here] = da[g].astype(BF16)


def half_specs(total, width):
    return [pl.BlockSpec((1, total, width), lambda i, at=at: (i + at, 0, 0)) for at in (0, 4)]


def run_column_forward(slots, near, rest, x_all, main_own, tail_own, vec, steps):
    per_core, total, _ = near.shape
    n_parts, owners, _, emb_part = x_all.shape
    width = main_own.shape[1]
    units = width // 4
    tails = [(F32, width)] * 6 + [(F32, units)] * 2 + [(F32, width)]
    tails += [(BF16, emb_part + units), (BF16, E), (BF16, H), (BF16, NH), (BF16, NH), (BF16, 4 * Z)]

    def still(shape):
        return pl.BlockSpec(shape, lambda i, slots: (0,) * len(shape), pipeline_mode=pl.Buffered(1))

    return pl.pallas_call(
        functools.partial(column_forward_kernel, steps),
        grid_spec=pltpu.PrefetchScalarGridSpec(
            num_scalar_prefetch=1,
            grid=(per_core,),
            in_specs=[pl.BlockSpec((1, total, PACK), lambda i, slots: (i, 0, 0))] * 2
            + [
                pl.BlockSpec(
                    (n_parts, 1, total, emb_part), lambda i, slots, at=at: (0, slots[i + at], 0, 0)
                )
                for at in (0, per_core)
            ]
            + [still(main_own.shape), still(tail_own.shape), still(vec.shape)],
            out_specs=[
                pl.BlockSpec((2, 1, total, tail), lambda i, slots: (0, i, 0, 0)) for _, tail in tails
            ],
        ),
        out_shape=[jax.ShapeDtypeStruct((2, per_core, total, tail), dtype) for dtype, tail in tails],
        compiler_params=kernel_params(),
        cost_estimate=pl.CostEstimate(
            flops=2 * owners * total * width * 3 * H, bytes_accessed=18_000_000, transcendentals=0
        ),
        name="column_forward",
    )(slots, near, rest, x_all, x_all, main_own, tail_own, vec)


def run_column_backward(moved, back_all, vec, kept, steps):
    owners, total, _ = moved.shape
    width = vec.shape[1]
    units = width // 4
    widths = [width] * 6 + [units] * 2 + [width]
    return pl.pallas_call(
        functools.partial(column_backward_kernel, steps),
        grid=(owners // 2,),
        in_specs=half_specs(total, units)
        + [
            pl.BlockSpec((1, 1, total, 4 * Z), lambda i, at=at: (i + at, 2, 0, 0)) for at in (0, 4)
        ]
        + [whole(vec.shape)]
        + [pl.BlockSpec((2, 1, total, tail), lambda i: (0, i, 0, 0)) for tail in widths],
        out_specs=[pl.BlockSpec((2, 1, total, width), lambda i: (0, i, 0, 0))] * 5
        + [pl.BlockSpec((2, width), lambda i: (0, 0))],
        out_shape=[jax.ShapeDtypeStruct((2, owners // 2, total, width), BF16)] * 5
        + [jax.ShapeDtypeStruct((2, width), F32)],
        scratch_shapes=[pltpu.VMEM((total, units), F32)],
        compiler_params=kernel_params(),
        cost_estimate=pl.CostEstimate(
            flops=40 * owners * total * width, bytes_accessed=16_000_000, transcendentals=0
        ),
        name="column_backward",
    )(moved, moved, back_all, back_all, vec, *kept)


def table_kernel(me_ref, ids_ref, r0_ref, r1_ref, r2_ref, r3_ref, table_out, row_out, col_out, rows_s):
    count = rows_s.shape[0] // 4
    table_out[...] = jnp.zeros_like(table_out)
    for bits, ref in enumerate((r0_ref, r1_ref, r2_ref, r3_ref)):
        start = pl.multiple_of((me_ref[0] ^ bits) * count, count)
        rows_s[pl.ds(start, count)] = ref[:count].astype(F32)

    @pl.loop(0, rows_s.shape[0] // 16)
    def _(group):
        for lane in range(16):
            spot = group * 16 + lane
            here = pl.ds(ids_ref[spot], 1)
            table_out[here] += rows_s[pl.ds(spot, 1)]

    def measure(block, cols):
        here = pl.ds(pl.multiple_of(block * VOCAB_BLOCK, VOCAB_BLOCK), VOCAB_BLOCK)
        values = table_out[here]
        squares = values * values + EPS_FACT
        high = squares.astype(BF16)
        low = (squares - high.astype(F32)).astype(BF16)
        ones = jnp.ones((8, squares.shape[1]), BF16)
        sums = dot_last(ones, high) + dot_last(ones, low)
        row_out[pl.ds(block, 1)] = sums[:1]
        return cols + jnp.sum(squares, axis=0, keepdims=True)

    zero = jnp.zeros((1, table_out.shape[1]), F32)
    col_out[...] = lax.fori_loop(0, row_out.shape[0], measure, zero)


def run_table(me, ids, parts, vocab):
    lanes = parts[0].shape[1]
    total = ids.shape[0]
    blocks = vocab // VOCAB_BLOCK
    return pl.pallas_call(
        table_kernel,
        grid_spec=pltpu.PrefetchScalarGridSpec(
            num_scalar_prefetch=2,
            grid=(1,),
            in_specs=[pl.BlockSpec(part.shape, lambda i, *_: (0, 0)) for part in parts],
            out_specs=[
                pl.BlockSpec((vocab, lanes), lambda i, *_: (0, 0)),
                pl.BlockSpec((blocks, VOCAB_BLOCK), lambda i, *_: (0, 0)),
                pl.BlockSpec((1, lanes), lambda i, *_: (0, 0)),
            ],
            scratch_shapes=[pltpu.VMEM((total, lanes), F32)],
        ),
        out_shape=[
            jax.ShapeDtypeStruct((vocab, lanes), F32),
            jax.ShapeDtypeStruct((blocks, VOCAB_BLOCK), F32),
            jax.ShapeDtypeStruct((1, lanes), F32),
        ],
        compiler_params=kernel_params(),
        cost_estimate=pl.CostEstimate(flops=10**9, bytes_accessed=40_000_000, transcendentals=0),
        name="embedding_table",
    )(me, ids, *parts)


def stepped_update(weight, grad, relative, spread, rate):
    return weight - rate * grad * lax.rsqrt(relative * spread)


def main_update_kernel(rate, me_ref, p0, p1, p2, p3, weight_ref, rel_ref, spread_ref, grad_out, new_out):
    quarter, part = pl.program_id(0), pl.program_id(1)
    rows, gates, lanes = grad_out.shape
    for bits, ref in enumerate((p0, p1, p2, p3)):

        @pl.when(quarter == bits)
        def _():
            here = pl.ds(pl.multiple_of(part * rows, rows), rows)
            for g in range(gates):
                grad = ref[here, g * lanes : (g + 1) * lanes].astype(F32)
                grad_out[:, g, :] = grad
                new_out[:, g, :] = stepped_update(
                    weight_ref[:, g, :], grad, rel_ref[...], spread_ref[g : g + 1], rate
                )


def run_main_update(me, parts, weight, rel_wide, spread, rate):
    total, gates, lanes = weight.shape
    rows = total // 8

    def place(quarter, part, me_ref):
        return (part * 4 + (me_ref[0] ^ quarter), 0, 0)

    block = pl.BlockSpec((rows, gates, lanes), place)
    return pl.pallas_call(
        functools.partial(main_update_kernel, rate),
        grid_spec=pltpu.PrefetchScalarGridSpec(
            num_scalar_prefetch=1,
            grid=(4, 2),
            in_specs=[pl.BlockSpec(part.shape, lambda q, p, m: (0, 0)) for part in parts]
            + [
                block,
                pl.BlockSpec((rows, LANES), lambda q, p, m: place(q, p, m)[:2]),
                pl.BlockSpec(spread.shape, lambda q, p, m: (0, 0)),
            ],
            out_specs=[block, block],
        ),
        out_shape=[jax.ShapeDtypeStruct(weight.shape, F32)] * 2,
        compiler_params=kernel_params(),
        cost_estimate=pl.CostEstimate(flops=10**7, bytes_accessed=16_000_000, transcendentals=0),
        name="main_update",
    )(me, *parts, weight, rel_wide, spread)


def out_update_kernel(rate, seen_ref, weight_ref, rel_ref, spread_ref, grad_out, new_out):
    for j in range(grad_out.shape[1] // LANES):
        cols = slice(j * LANES, (j + 1) * LANES)
        grad = seen_ref[:, cols].astype(F32)
        grad_out[:, cols] = grad
        new_out[:, cols] = stepped_update(weight_ref[:, cols], grad, rel_ref[...], spread_ref[:, cols], rate)


def run_out_update(seen, weight, rel_wide, spread, rate):
    total, width = weight.shape
    rows = total // 8

    def rows_of(columns):
        return pl.BlockSpec((rows, columns), lambda i: (i, 0))

    return pl.pallas_call(
        functools.partial(out_update_kernel, rate),
        grid=(8,),
        in_specs=[rows_of(width), rows_of(width), rows_of(LANES), pl.BlockSpec(spread.shape, lambda i: (0, 0))],
        out_specs=[rows_of(width)] * 2,
        out_shape=[jax.ShapeDtypeStruct(weight.shape, F32)] * 2,
        compiler_params=kernel_params(),
        cost_estimate=pl.CostEstimate(flops=10**7, bytes_accessed=20_000_000, transcendentals=0),
        name="out_update",
    )(seen, weight, rel_wide, spread)


def hyper_update_kernel(
    rate, parts_ref, bias_ref, weight_ref, row_ref, col_ref, grad_out, new_out, row_out, col_out
):
    quarters, owners, _, _ = parts_ref.shape
    total, width = grad_out.shape
    devices = quarters * owners
    heights = (E // devices, H // devices, NH // devices)
    for owner in range(owners):
        for quarter in range(quarters):
            part = parts_ref[quarter, owner].astype(F32)
            place = owner * quarters + quarter
            first, start = 0, 0
            for height, size in zip(heights, (E, H, NH)):
                to = start + place * height
                grad_out[to : to + height] = part[first : first + height]
                first += height
                start += size
    grad_out[total - 1 :] = bias_ref[...]
    decay = 1.0 - STEP ** (-0.8)
    blocks = [(at, min(256, total - at)) for at in range(0, total, 256)]
    cols = jnp.zeros((1, width), F32)
    sums = jnp.zeros((1, LANES), F32)
    for at, size in blocks:
        here = slice(at, at + size)
        grad = grad_out[here]
        squares = grad * grad + EPS_FACT
        cols += jnp.sum(squares, axis=0, keepdims=True)
        mean = jnp.sum(squares, axis=1, keepdims=True) / width
        row_new = decay * row_ref[here] + (1.0 - decay) * mean
        row_out[here] = row_new
        sums += jnp.sum(row_new, axis=0, keepdims=True)
    col_new = decay * col_ref[...] + (1.0 - decay) * (cols / total)
    col_out[...] = col_new
    average = sums / total
    for at, size in blocks:
        here = slice(at, at + size)
        relative = row_out[here] / average
        for j in range(width // LANES):
            lanes = slice(j * LANES, (j + 1) * LANES)
            new_out[here, lanes] = stepped_update(
                weight_ref[here, lanes], grad_out[here, lanes], relative, col_new[:, lanes], rate
            )


def run_hyper_update(parts, bias, weight, row_wide, col, rate):
    total, width = weight.shape

    def all_of(values):
        return pl.BlockSpec(values.shape, lambda i: (0,) * values.ndim)

    return pl.pallas_call(
        functools.partial(hyper_update_kernel, rate),
        grid=(1,),
        in_specs=[all_of(values) for values in (parts, bias, weight, row_wide, col)],
        out_specs=[all_of(values) for values in (weight, weight, row_wide, col)],
        out_shape=[
            jax.ShapeDtypeStruct(weight.shape, F32),
            jax.ShapeDtypeStruct(weight.shape, F32),
            jax.ShapeDtypeStruct(row_wide.shape, F32),
            jax.ShapeDtypeStruct(col.shape, F32),
        ],
        compiler_params=kernel_params(),
        cost_estimate=pl.CostEstimate(flops=10**7, bytes_accessed=20_000_000, transcendentals=0),
        name="hyper_update",
    )(parts, bias, weight, row_wide, col)


def updates(weights, states, grads, row_sums, embed_col_mean):
    embed, w_main, w_scale, w_hyper, w_zproj, w_out, main_vectors = weights
    (
        embed_row, embed_col, main_row, main_col, scale_row, scale_col, hyper_row, hyper_col,
        zproj_row, zproj_col, out_row, out_col, vector_state,
    ) = states
    g_embed, g_main, g_scale, g_hyper, g_zproj, g_out, g_vec = grads
    row_embed, row_main, row_scale, row_out = row_sums
    sq_main, sq_scale, sq_hyper, sq_zproj, sq_out = [
        g * g + EPS_FACT for g in (g_main, g_scale, g_hyper, g_zproj, g_out)
    ]
    res_embed = adafactor(
        embed, g_embed, embed_row, embed_col, row_embed / E, embed_col_mean, 0, 1.0
    )
    res_main = adafactor(
        w_main,
        g_main,
        main_row,
        main_col,
        row_main / (4 * H),
        jnp.mean(sq_main, axis=0),
        0,
        1.0 / math.sqrt(E),
    )
    res_scale = adafactor(
        w_scale,
        g_scale,
        scale_row,
        scale_col,
        row_scale / (4 * H),
        jnp.mean(sq_scale, axis=1),
        1,
        1.0 / math.sqrt(Z),
    )
    res_hyper = adafactor(
        w_hyper,
        g_hyper,
        hyper_row,
        hyper_col,
        jnp.mean(sq_hyper, axis=1),
        jnp.mean(sq_hyper, axis=0),
        0,
        1.0 / math.sqrt(E + H + NH + 1),
    )
    res_zproj = adafactor(
        w_zproj,
        g_zproj,
        zproj_row,
        zproj_col,
        jnp.mean(sq_zproj, axis=1),
        jnp.mean(sq_zproj, axis=0),
        0,
        2.0 / math.sqrt(NH),
    )
    res_out = adafactor(
        w_out, g_out, out_row, out_col, row_out / V, jnp.mean(sq_out, axis=0), 0, 3.0 / math.sqrt(H)
    )
    decay = 1.0 - STEP ** (-0.8)
    state_new = decay * vector_state + (1.0 - decay) * (g_vec * g_vec + EPS_FACT)
    vectors_new = main_vectors - 0.1 * g_vec * lax.rsqrt(state_new)
    return (
        res_embed
        + res_main
        + res_scale
        + res_hyper
        + res_zproj
        + res_out
        + (g_vec, state_new, vectors_new)
    )


def per_chip(
    parts,
    token_ids,
    seq_lengths,
    valid_mask,
    embed,
    w_main,
    w_scale,
    w_hyper,
    w_zproj,
    w_out,
    main_vectors,
    *states,
):
    n_mp, n_batch = parts
    my = lax.axis_index("mp")
    b = lax.axis_index("batch")
    units = w_main.shape[2]
    width = 4 * units
    emb_part = embed.shape[1]
    vocab_part = w_out.shape[1]
    batch_rows, steps = valid_mask.shape
    own = batch_rows // n_mp
    own_total = steps * own
    total = batch_rows * steps
    slots = my ^ jnp.array(SLOTS, jnp.int32)
    order = my ^ jnp.arange(n_mp, dtype=jnp.int32)
    from_slots = order // 2 + (n_mp // 2) * (order % 2)

    def by_owner(values):
        return values.reshape(n_mp, own, steps).transpose(0, 2, 1)

    def to_partners(values):
        return [swap(values, "batch", n_batch, bits) for bits in (1, 2, 3)]

    def quarter_of(values, bits, rows):
        return lax.dynamic_slice_in_dim(values, (b ^ bits) * rows, rows, 0)

    def placed(pieces, me):
        out = jnp.zeros((len(pieces),) + pieces[0].shape, pieces[0].dtype)
        for bits, piece in enumerate(pieces):
            out = lax.dynamic_update_slice_in_dim(out, piece[None], me ^ bits, 0)
        return out

    quarter = SCALE_AT // 4
    tail_quarter = TAIL_ROWS // 4
    half = (quarter + tail_quarter) // 2

    def own_rows(first, rows):
        values = lax.dynamic_slice_in_dim(w_main, b * quarter + first, rows, 0)
        return values.astype(BF16).reshape(rows, width)

    head_part = own_rows(0, half)
    head = swap(head_part, "mp", n_mp, 2)
    tail_own = weight_tail(w_scale, main_vectors)
    tail_part = jnp.concatenate(
        [own_rows(half, quarter - half), lax.dynamic_slice_in_dim(tail_own, b * tail_quarter, tail_quarter, 0)], axis=0
    )
    x_part = embed[by_owner(token_ids[:, :steps]).reshape(total)].astype(BF16)
    tail_part, head_part, head, x_part = tie(tail_part, head_part, head, x_part)
    tail = swap(tail_part, "mp", n_mp, 2)
    far = swap(jnp.concatenate([head_part, tail_part], axis=0), "mp", n_mp, 4)
    x_all = lax.all_gather(x_part, "mp").reshape(n_mp, n_mp, own_total, emb_part)
    x_own = lax.dynamic_index_in_dim(x_all, my, 1, False).transpose(1, 0, 2).reshape(own_total, E)
    main_own = w_main.astype(BF16).reshape(2 * E, width)
    hyp_low = w_hyper.astype(BF16)
    both = swap(far, "mp", n_mp, 2)
    found = []
    for array, bits in ((main_own, 0), (swap(main_own, "mp", n_mp, 1), 1)):
        found.append((array, bits, None, 0, SCALE_AT))
    for array, bits in ((tail_own, 0), (swap(tail_own, "mp", n_mp, 1), 1)):
        found.append((array, bits, None, SCALE_AT, TAIL_ROWS))
    for got, bits, start in ((head, 2, 0), (tail, 2, half), (far, 4, 0), (both, 6, 0)):
        cut = got.shape[0] // 2
        along_x = swap(got, "batch", n_batch, 1)
        along_y = swap(got, "batch", n_batch, 2)
        low = swap(along_x[:cut], "batch", n_batch, 2)
        high = swap(along_y[cut:], "batch", n_batch, 1)
        for array, over, first in (
            (got, 0, start), (along_x, 1, start), (along_y, 2, start), (low, 3, start), (high, 3, start + cut),
        ):
            found.append((array, bits, over, first, array.shape[0]))
            found.append((swap(array, "mp", n_mp, 1), bits ^ 1, over, first, array.shape[0]))
    found.sort(key=lambda piece: piece[1])
    plan = [piece[1:] for piece in found]
    pieces = [piece[0] for piece in found]
    blocks = (n_mp, width)
    hyp_bias = hyp_low[E + H + NH :].astype(F32)
    zp_wide = jnp.pad(w_zproj, ((0, 0), (0, Z))).astype(BF16)
    zp_bias = zp_wide[NH:].astype(F32)
    pack, *kept = run_forward(
        x_own, blocks, plan, pieces, hyp_low, hyp_bias, zp_wide[:NH], zp_bias, steps
    )

    def of_chips(values):
        return jnp.stack([values] + [swap(values, "mp", n_mp, bits) for bits in (2, 4, 6)])

    def both_halves(near):
        return jnp.concatenate([near, swap(near, "mp", n_mp, 1)], axis=0)

    pack, token_ids, seq_lengths, valid_mask, w_out, *pieces = tie(
        pack, token_ids, seq_lengths, valid_mask, w_out, *pieces
    )
    near = of_chips(pack.reshape(own_total, PACK))
    positions = jnp.arange(steps, dtype=jnp.int32)
    valid = valid_mask * (positions[None, :] < seq_lengths[:, None]).astype(jnp.int32)
    marks = jnp.stack([token_ids[:, :steps], token_ids[:, 1:], valid])
    marks = marks.reshape(3, n_mp, own, steps).transpose(0, 1, 3, 2)[:, slots].reshape(3, total)
    weight_rows = marks[2].astype(F32)
    out_low = w_out.astype(BF16)
    turned = run_turn(blocks, plan, pieces)
    near, marks, weight_rows, out_low, *turned = tie(near, marks, weight_rows, out_low, *turned)
    rest = swap(near, "mp", n_mp, 1)
    h_all = jnp.concatenate([near[:, :, :H], rest[:, :, :H]], axis=0)
    h_rows = h_all.reshape(total, H)
    logits = matmul(h_rows, out_low)
    local_target = marks[1] - my * vocab_part
    hit = jnp.arange(vocab_part, dtype=jnp.int32)[None, :] == local_target[:, None]
    top = jnp.max(logits, axis=1)
    stats = [
        top,
        jnp.sum(jnp.exp(logits - top[:, None]), axis=1),
        jnp.sum(jnp.where(hit, logits, 0.0), axis=1),
    ]

    def merged(one, two):
        top = jnp.maximum(one[0], two[0])
        exps = one[1] * jnp.exp(one[0] - top) + two[1] * jnp.exp(two[0] - top)
        return jnp.stack([top, exps, one[2] + two[2]])

    def from_partner(values, bits):
        spots = [bits ^ slot for slot in SLOTS]
        spots = [spot // 2 + (n_mp // 2) * (spot % 2) for spot in spots]
        turned = jnp.concatenate([values[:, spot : spot + 1] for spot in spots], axis=1)
        return swap(turned, "mp", n_mp, bits)

    stats = jnp.stack(stats).reshape(3, n_mp, own_total)
    pair = merged(stats, from_partner(stats, 1))
    vec = main_vectors.reshape(2, width)
    near, rest, pair, valid, slot_ids = tie(near, rest, pair, valid, marks[0])
    others = [from_partner(pair, bits) for bits in (2, 4, 6)]
    column = run_column_forward(slots, near, rest, x_all, main_own, tail_own, vec, steps)
    count = tree_sum(jnp.sum(valid).astype(F32), "batch", n_batch)
    pair, count, *rest_of = tie(pair, count, *others, *column)
    others, column = rest_of[:3], rest_of[3:]
    stats = merged(merged(pair, others[0]), merged(others[1], others[2]))
    log_total = (stats[0] + jnp.log(stats[1])).reshape(total)
    loss = jnp.sum(
        (log_total[:own_total] - stats[2].reshape(total)[:own_total]) * weight_rows[:own_total]
    )
    grad_logits = (
        (jnp.exp(logits - log_total[:, None]) - hit.astype(F32)) * (weight_rows / count)[:, None]
    ).astype(BF16)
    other = swap(dot_last(grad_logits[total // 2 :], out_low).astype(BF16), "mp", n_mp, 1)
    both_cores = dot_last(grad_logits[: total // 2], out_low) + other.astype(F32)
    h_rows, both_cores, slot_ids = tie(h_rows, both_cores.reshape(n_mp // 2, own_total, H), slot_ids)
    dh_parts = [
        swap(both_cores[spot].astype(BF16), "mp", n_mp, 2 * spot) for spot in range(1, n_mp // 2)
    ]
    g_out = dot_first(h_rows, grad_logits).astype(BF16)
    out_quarter = H // n_batch
    out_parts = [quarter_of(g_out, bits, out_quarter) for bits in range(n_batch)]
    ids_all = placed([slot_ids] + to_partners(slot_ids), b).reshape(n_batch * total)
    dh_top = both_cores[0]
    for part in dh_parts:
        dh_top = dh_top + part.astype(F32)
    dh_top, ids_all, *out_parts = tie(dh_top, ids_all, *out_parts)
    out_got = [swap(part, "batch", n_batch, bits) for bits, part in enumerate(out_parts) if bits]
    moved, _, _ = run_backward(
        dh_top.reshape(steps, own, H), blocks, plan, turned, hyp_low, zp_wide[:NH], kept
    )
    left, x_rows, h_before, hh_before, hh_all, z_all = column[9:]
    moved, hh_before, hh_all, *out_got = tie(moved, hh_before, hh_all, *out_got)
    out_sum = out_parts[0].astype(F32)
    for part in out_got:
        out_sum = out_sum + part.astype(F32)
    moved, out_low_sum = tie(moved, out_sum.astype(BF16))
    g_out = lax.all_gather(out_low_sum, "batch").reshape(H, vocab_part)

    moved = moved.reshape(n_mp + 3, own_total, 2 * units)
    crossed = swap(moved[n_mp // 2 : n_mp], "mp", n_mp, 1)
    back_own = moved[n_mp:]
    arrived = [
        swap(
            jnp.concatenate([moved[spot : spot + 1], crossed[spot : spot + 1], back_own], axis=0),
            "mp",
            n_mp,
            2 * spot,
        )
        for spot in range(1, n_mp // 2)
    ]
    moved = jnp.stack(
        [moved[0]] + [part[0] for part in arrived] + [crossed[0]] + [part[1] for part in arrived]
    )
    back_all = both_halves(jnp.stack([back_own] + [part[2:] for part in arrived]))
    dx_part = moved[:, :, units:].reshape(total, emb_part)

    nh_part = NH // n_mp
    hyp_rows = emb_part + units + 2 * nh_part
    hyp_quarter = hyp_rows // n_batch

    def own_columns(values, size):
        return lax.dynamic_slice_in_dim(values, my * size, size, values.ndim - 1)

    dq_rows = jnp.concatenate([back_all[:, 0], back_all[:, 1]], axis=2).reshape(total, 4 * NH)
    dz_rows = back_all[:, 2, :, : 3 * Z].reshape(total, 3 * Z)
    hh_left = own_columns(hh_before, nh_part).reshape(total, nh_part)
    hh_own = own_columns(hh_all, nh_part).reshape(total, nh_part)
    g_small = [
        dot_first(left.reshape(total, emb_part + units), dq_rows),
        dot_first(hh_left, dq_rows),
        jnp.pad(dot_first(hh_own, dz_rows), ((0, 0), (0, 4 * NH - 3 * Z))),
    ]
    g_small = [g_small[0][:emb_part], g_small[0][emb_part:], g_small[1], g_small[2]]

    def small_quarter(bits):
        return jnp.concatenate([quarter_of(g, bits, g.shape[0] // n_batch) for g in g_small], axis=0)

    hyp_got, dx_got = [], [dx_part]
    for bits in (1, 2, 3):
        part = small_quarter(bits).astype(BF16).reshape(-1, emb_part)
        got = swap(jnp.concatenate([dx_part, part], axis=0), "batch", n_batch, bits)
        dx_got.append(got)
        hyp_got.append(got[total:].reshape(hyp_quarter, 4 * NH))
    hyp_sum = small_quarter(0)
    for got in hyp_got:
        hyp_sum = hyp_sum + got.astype(F32)
    hyp_all = lax.all_gather(hyp_sum.astype(BF16), ("batch", "mp"))
    hyp_all = hyp_all.reshape(n_batch, n_mp, hyp_quarter, 4 * NH)

    dux, duh, d0, d1, da, gv = run_column_backward(moved, back_all, vec, column[:9], steps)
    x_rows = x_rows.reshape(total, E)
    h_before = h_before.reshape(total, H)
    z_rows = z_all[:, :, :, : 3 * Z].reshape(total, 3, Z)
    g_parts = [dot_first(x_rows, dux.reshape(total, width)), dot_first(h_before, duh.reshape(total, width))] + [
        dot_first(z_rows[:, k], d.reshape(total, width)) for k, d in enumerate((d0, d1, da))
    ]

    def main_quarter(bits):
        return jnp.concatenate(
            [quarter_of(part, bits, part.shape[0] // n_batch) for part in g_parts], axis=0
        )

    main_got = [swap(main_quarter(bits).astype(BF16), "batch", n_batch, bits) for bits in (1, 2, 3)]

    me = b.reshape(1)
    g_embed, embed_rows, embed_cols = run_table(me, ids_all, dx_got, embed.shape[0])

    g_embed, embed_rows, embed_cols, *main_got = tie(g_embed, embed_rows, embed_cols, *main_got)
    main_sum = main_quarter(0)
    for got in main_got:
        main_sum = main_sum + got.astype(F32)
    main_low = main_sum.astype(BF16)
    main_pieces = [main_low] + to_partners(main_low)
    main_seen = main_low.astype(F32)
    sq_main = main_seen * main_seen + EPS_FACT
    in_quarter = (E + H) // n_batch
    scale_quarter = Z // n_batch

    out_seen = g_out.astype(F32)
    sq_out = out_seen * out_seen + EPS_FACT

    by_rows = tree_sum(
        jnp.concatenate(
            [
                embed_rows.reshape(-1),
                jnp.sum(sq_out, axis=1),
                jnp.sum(sq_main, axis=1),
                loss[None],
            ]
        ),
        "mp",
        n_mp,
    )
    row_embed = by_rows[: embed.shape[0]]
    row_out = by_rows[embed.shape[0] : embed.shape[0] + H]
    sums = jnp.sum(back_all.astype(F32), axis=2)[from_slots]
    sums = jnp.sum(sums, axis=0).reshape(-1)[: 4 * NH + 3 * Z]
    fields = [
        by_rows[embed.shape[0] + H : -1],
        by_rows[-1:],
        jnp.sum(sq_main[:in_quarter], axis=0),
        jnp.sum(sq_main[in_quarter:].reshape(3, scale_quarter, width), axis=1).reshape(-1),
        gv.reshape(-1),
        sums,
    ]
    sizes = [field.shape[0] for field in fields]
    mixed = jnp.concatenate(fields)
    mixed = jnp.stack([mixed, swap(mixed, "batch", n_batch, 1)])
    mixed = placed(list(mixed) + list(swap(mixed, "batch", n_batch, 2)), b)
    rows_four = mixed[:, : sizes[0]]
    added = jnp.sum(mixed[:, sizes[0] :], axis=0)
    ends = [sum(sizes[1 : k + 1]) for k in range(len(sizes))]
    loss_sum, col_main, col_scale, g_vec, bias_sums = [
        added[ends[k] : ends[k + 1]] for k in range(len(sizes) - 1)
    ]
    row_in = rows_four[:, : E // n_batch].reshape(E)
    row_rec = rows_four[:, E // n_batch : in_quarter].reshape(H)
    row_scale = rows_four[:, in_quarter:].reshape(n_batch, 3, scale_quarter)
    row_scale = jnp.moveaxis(row_scale, 0, 1).reshape(3, Z)
    g_vec = g_vec.reshape(2, 4, units)

    (
        embed_row, embed_col, main_row, main_col, scale_row, scale_col, hyper_row, hyper_col,
        zproj_row, zproj_col, out_row, out_col, vector_state,
    ) = states
    decay = 1.0 - STEP ** (-0.8)

    def moving(old, mean):
        return decay * old + (1.0 - decay) * mean

    def across(values):
        return jnp.broadcast_to(values[:, None], (values.shape[0], LANES))

    res_embed = adafactor(
        embed, g_embed, embed_row, embed_col, row_embed / E, embed_cols[0] / embed.shape[0], 0, 1.0
    )
    new_out_row = moving(out_row, row_out / V)
    new_out_col = moving(out_col, jnp.mean(sq_out, axis=0))
    g_out, new_out = run_out_update(
        g_out,
        w_out,
        across(new_out_row / jnp.mean(new_out_row)),
        new_out_col[None],
        3.0 / math.sqrt(H),
    )
    g_hyper, new_hyper, hyper_rows, new_hyper_col = run_hyper_update(
        hyp_all,
        bias_sums[None, : 4 * NH],
        w_hyper,
        across(hyper_row),
        hyper_col[None],
        1.0 / math.sqrt(E + H + NH + 1),
    )
    new_embed, new_out, new_hyper, *main_pieces = tie(res_embed[1], new_out, new_hyper, *main_pieces)
    res_embed = (res_embed[0], new_embed) + res_embed[2:]
    scale_parts = placed([piece[in_quarter:] for piece in main_pieces], b)
    g_scale = jnp.moveaxis(scale_parts.reshape(n_batch, 3, scale_quarter, width), 0, 1)
    g_scale = g_scale.reshape(3, Z, 4, units).astype(F32)
    new_main_row = moving(main_row, jnp.concatenate([row_in, row_rec]) / (4 * H))
    new_main_col = moving(main_col, col_main.reshape(4, units) / (E + H))
    g_main, new_main = run_main_update(
        me,
        main_pieces,
        w_main,
        across(new_main_row / jnp.mean(new_main_row)),
        new_main_col,
        1.0 / math.sqrt(E),
    )
    res_scale = adafactor(
        w_scale,
        g_scale,
        scale_row,
        scale_col,
        row_scale / (4 * H),
        col_scale.reshape(3, 4, units) / Z,
        1,
        1.0 / math.sqrt(Z),
    )
    zproj_parts = hyp_all[:, :, hyp_quarter - nh_part // n_batch :, : 3 * Z]
    zproj_parts = zproj_parts.transpose(1, 0, 2, 3).reshape(NH, 3 * Z)
    g_zproj = jnp.concatenate([zproj_parts.astype(F32), bias_sums[None, 4 * NH :]], axis=0)
    sq_zproj = g_zproj * g_zproj + EPS_FACT
    res_zproj = adafactor(
        w_zproj,
        g_zproj,
        zproj_row,
        zproj_col,
        jnp.mean(sq_zproj, axis=1),
        jnp.mean(sq_zproj, axis=0),
        0,
        2.0 / math.sqrt(NH),
    )
    state_new = moving(vector_state, g_vec * g_vec + EPS_FACT)
    return (
        (loss_sum[0], count)
        + res_embed
        + (g_main, new_main, new_main_row, new_main_col)
        + res_scale
        + (g_hyper, new_hyper, hyper_rows[:, 0], new_hyper_col[0])
        + res_zproj
        + (g_out, new_out, new_out_row, new_out_col)
        + (g_vec, state_new, main_vectors - 0.1 * g_vec * lax.rsqrt(state_new))
    )


def per_device(
    parts,
    token_ids,
    seq_lengths,
    valid_mask,
    embed,
    w_main,
    w_scale,
    w_hyper,
    w_zproj,
    w_out,
    main_vectors,
    *states,
):
    n_mp, n_batch = parts
    my = lax.axis_index("mp")
    units = w_main.shape[2]
    emb_part = embed.shape[1]
    vocab_part = w_out.shape[1]
    batch_rows, steps = valid_mask.shape
    own = batch_rows // n_mp
    padded = -(-own // ROW_TILE) * ROW_TILE
    own_total = steps * own
    total = batch_rows * steps
    wide = units % LANES == 0

    def by_owner(values):
        return values.reshape(n_mp, own, steps).transpose(0, 2, 1)

    ids = by_owner(token_ids[:, :steps]).reshape(total)
    targets = by_owner(token_ids[:, 1:]).reshape(total)
    positions = jnp.arange(steps, dtype=jnp.int32)
    valid = valid_mask.astype(F32) * (positions[None, :] < seq_lengths[:, None]).astype(F32)
    weight_rows = by_owner(valid).reshape(total)
    count = tree_sum(jnp.sum(weight_rows), "batch", n_batch)

    def to_kernel(stacked):
        if wide:
            return stacked
        rows = stacked.shape[1]
        apart = stacked.reshape(n_mp, rows, 4, units).transpose(1, 2, 0, 3)
        return apart.reshape(1, rows, 4 * H)

    def pad_rows(values):
        return jnp.pad(values, ((0, 0), (0, padded - own), (0, 0))) if padded > own else values

    def unpad(values):
        return values[:, :own] if padded > own else values

    x_part = embed[ids].astype(BF16)
    main_own = w_main.astype(BF16).reshape(E + H, 4 * units)
    tail_own = weight_tail(w_scale, main_vectors)
    scale_own = tail_own[: 3 * Z]
    x_own = lax.all_to_all(x_part.reshape(n_mp, own_total, emb_part), "mp", 0, 0)
    x_own = x_own.transpose(1, 0, 2).reshape(steps, own, E)
    pieces = [to_kernel(lax.all_gather(jnp.concatenate([main_own, tail_own], axis=0), "mp"))]
    blocks = (pieces[0].shape[0], pieces[0].shape[2])
    x_all = lax.all_gather(x_part, "mp", axis=1, tiled=True)
    hyp_low = w_hyper.astype(BF16)
    zp_wide = jnp.pad(w_zproj, ((0, 0), (0, Z))).astype(BF16)
    out_low = w_out.astype(BF16)
    hyp_bias = hyp_low[E + H + NH :].astype(F32)
    zp_bias = zp_wide[NH:].astype(F32)

    pack, *kept = run_forward(
        pad_rows(x_own).reshape(steps * padded, E),
        blocks, None, pieces, hyp_low, hyp_bias, zp_wide[:NH], zp_bias, steps,
    )

    small_own = unpad(pack)[:, :, : H + NH + 3 * Z]
    rows_all = lax.all_gather(small_own.reshape(own_total, H + NH + 3 * Z), "mp")
    h_rows = rows_all[:, :, :H].reshape(total, H)
    logits = matmul(h_rows, out_low)
    local_target = targets - my * vocab_part
    hit = jnp.arange(vocab_part, dtype=jnp.int32)[None, :] == local_target[:, None]
    top = jnp.max(logits, axis=1)
    stats = jnp.stack(
        [
            top,
            jnp.sum(jnp.exp(logits - top[:, None]), axis=1),
            jnp.sum(jnp.where(hit, logits, 0.0), axis=1),
        ]
    )
    stats = lax.all_gather(stats, "mp")
    top_all = jnp.max(stats[:, 0], axis=0)
    exp_sum = jnp.sum(stats[:, 1] * jnp.exp(stats[:, 0] - top_all), axis=0)
    log_total = top_all + jnp.log(exp_sum)
    picked = jnp.sum(stats[:, 2], axis=0)
    loss_sum = tree_sum(jnp.sum((log_total - picked) * weight_rows), "batch", n_batch)
    grad_logits = (
        (jnp.exp(logits - log_total[:, None]) - hit.astype(F32)) * (weight_rows / count)[:, None]
    ).astype(BF16)
    dh_part = dot_last(grad_logits, out_low).reshape(n_mp, own_total, H)
    dh_parts = lax.all_to_all(dh_part.astype(BF16), "mp", 0, 0)
    dh_top = jnp.sum(dh_parts.astype(F32), axis=0)
    dh_top = dh_top.reshape(steps, own, H)
    g_out = dot_first(h_rows, grad_logits).astype(BF16)
    dh_top, g_out = lax.optimization_barrier((dh_top, g_out))
    g_out = lax.psum(g_out, "batch").astype(F32)

    dsda, dx_own, gv = run_backward(
        pad_rows(dh_top), blocks, None, run_turn(blocks, None, pieces), hyp_low, zp_wide[:NH], kept
    )
    nb = blocks[0]
    back = jnp.concatenate([dsda[nb + k, :, :, : 2 * NH] for k in range(3)], axis=2)
    dsda = dsda[:nb]

    if wide:
        dsda = unpad(dsda.reshape(n_mp * steps, padded, 8 * units))
    else:
        dsda = unpad(dsda.reshape(steps, padded, 8 * H)).reshape(own_total, 8, n_mp, units)
        dsda = dsda.transpose(2, 0, 1, 3)
    dsda = dsda.reshape(n_mp, own_total, 8 * units)
    dx_send = unpad(dx_own.reshape(steps, padded, E)).reshape(own_total, n_mp, emb_part)
    sent = jnp.concatenate([dsda, dx_send.transpose(1, 0, 2)], axis=2)
    sent = lax.all_to_all(sent, "mp", 0, 0).reshape(total, 8 * units + emb_part)
    ds = sent[:, : 4 * units].astype(F32)
    da_low = sent[:, 4 * units : 8 * units]
    dx_part = sent[:, 8 * units :]
    back_own = unpad(back)[:, :, : 4 * NH + 3 * Z]
    back_all = lax.all_gather(back_own.reshape(own_total, 4 * NH + 3 * Z), "mp")
    back_all = back_all.reshape(total, 4 * NH + 3 * Z)
    dq_all = back_all[:, : 4 * NH]
    dz_all = back_all[:, 4 * NH :]

    before = jnp.concatenate(
        [jnp.zeros_like(rows_all[:, :own]), rows_all[:, : own_total - own]], axis=1
    ).reshape(total, H + NH + 3 * Z)
    h_before = before[:, :H]
    hh_before = before[:, H : H + NH]
    hh_rows = rows_all[:, :, H : H + NH].reshape(total, NH)
    z_rows = rows_all[:, :, H + NH :].reshape(total, 3, Z)
    uh = matmul(h_before, main_own[E:])
    ux = matmul(x_all, main_own[:E])
    scale_blocks = scale_own.reshape(3, Z, 4 * units)
    one0 = 1.0 + matmul(z_rows[:, 0], scale_blocks[0])
    one1 = 1.0 + matmul(z_rows[:, 1], scale_blocks[1])
    g_in = dot_first(x_all, (ds * one1).astype(BF16))
    g_rec = dot_first(h_before, (ds * one0).astype(BF16))
    d_scales = [(ds * uh).astype(BF16), (ds * ux).astype(BF16), da_low]
    g_scale = jnp.stack([dot_first(z_rows[:, k], d_scales[k]) for k in range(3)])
    nh_part = NH // n_mp
    left = jnp.concatenate(
        [
            x_part,
            lax.dynamic_slice_in_dim(h_before, my * units, units, 1),
            lax.dynamic_slice_in_dim(hh_before, my * nh_part, nh_part, 1),
        ],
        axis=1,
    )
    g_hyper = dot_first(left, dq_all)
    g_zproj = dot_first(lax.dynamic_slice_in_dim(hh_rows, my * nh_part, nh_part, 1), dz_all)

    dx_all = lax.all_gather(dx_part, "batch").reshape(n_batch * total, emb_part)
    ids_all = lax.all_gather(ids, "batch").reshape(n_batch * total)
    g_embed = jax.ops.segment_sum(dx_all.astype(F32), ids_all, num_segments=embed.shape[0])
    g_in, g_rec, g_scale, g_hyper, g_zproj = lax.psum(
        tuple(g.astype(BF16) for g in (g_in, g_rec, g_scale, g_hyper, g_zproj)), "batch"
    )
    flat = lax.all_gather(
        jnp.concatenate([g_hyper.reshape(-1, LANES), g_zproj.reshape(-1, LANES)], axis=0), "mp"
    ).astype(F32)
    n_hyp = g_hyper.size // LANES
    all_hyper = flat[:, :n_hyp].reshape(n_mp, emb_part + units + nh_part, 4 * NH)
    all_zproj = flat[:, n_hyp:].reshape(n_mp * nh_part, 3 * Z)
    if wide:
        gv_parts = gv.reshape(n_mp, 2, 4, units)
    else:
        gv_parts = gv.reshape(2, 4, n_mp, units).transpose(2, 0, 1, 3)
    gv_parts, bias_sums = lax.psum(
        (gv_parts, jnp.sum(back_own.astype(F32), axis=(0, 1))), ("batch", "mp")
    )
    g_vec = lax.dynamic_index_in_dim(gv_parts, my, 0, False)
    g_hyper = jnp.concatenate(
        [
            all_hyper[:, :emb_part].reshape(E, 4 * NH),
            all_hyper[:, emb_part : emb_part + units].reshape(H, 4 * NH),
            all_hyper[:, emb_part + units :].reshape(NH, 4 * NH),
            bias_sums[None, : 4 * NH],
        ],
        axis=0,
    )
    g_zproj = jnp.concatenate([all_zproj, bias_sums[None, 4 * NH :]], axis=0)
    g_main = jnp.concatenate([g_in, g_rec], axis=0).astype(F32).reshape(E + H, 4, units)
    g_scale = g_scale.astype(F32).reshape(3, Z, 4, units)

    sq_embed = g_embed * g_embed + EPS_FACT
    sq_main = g_main * g_main + EPS_FACT
    sq_scale = g_scale * g_scale + EPS_FACT
    sq_out = g_out * g_out + EPS_FACT
    row_out = lax.psum(jnp.sum(sq_out, axis=1), "mp")
    row_embed, row_main, row_scale = lax.psum(
        (
            jnp.sum(sq_embed, axis=1),
            jnp.sum(sq_main, axis=(1, 2)),
            jnp.sum(sq_scale, axis=(2, 3)),
        ),
        "mp",
    )
    return (loss_sum, count) + updates(
        (embed, w_main, w_scale, w_hyper, w_zproj, w_out, main_vectors),
        states,
        (g_embed, g_main, g_scale, g_hyper, g_zproj, g_out, g_vec),
        (row_embed, row_main, row_scale, row_out),
        jnp.mean(sq_embed, axis=0),
    )


def solution(mesh):
    rep = P()
    placed = (
        P("batch", None),
        P("batch"),
        P("batch", None),
        P(None, "mp"),
        P(None, None, "mp"),
        P(None, None, None, "mp"),
        rep,
        rep,
        P(None, "mp"),
        P(None, None, "mp"),
        rep,
        P("mp"),
        rep,
        P(None, "mp"),
        rep,
        P(None, None, "mp"),
        rep,
        rep,
        rep,
        rep,
        rep,
        P("mp"),
        P(None, None, "mp"),
    )
    parts = (mesh.shape["mp"], mesh.shape["batch"])
    body = per_chip if parts == (8, 4) else per_device
    return jax.shard_map(
        functools.partial(body, parts),
        mesh=mesh,
        in_specs=placed,
        out_specs=(
            rep,
            rep,
            P(None, "mp"),
            P(None, "mp"),
            rep,
            P("mp"),
            P(None, None, "mp"),
            P(None, None, "mp"),
            rep,
            P(None, "mp"),
            P(None, None, None, "mp"),
            P(None, None, None, "mp"),
            rep,
            P(None, None, "mp"),
            rep,
            rep,
            rep,
            rep,
            rep,
            rep,
            rep,
            rep,
            P(None, "mp"),
            P(None, "mp"),
            rep,
            P("mp"),
            P(None, None, "mp"),
            P(None, None, "mp"),
            P(None, None, "mp"),
        ),
        check_vma=False,
    )
```

```python
import functools
import math

import jax
import jax.numpy as jnp
from jax import lax
from jax.experimental import pallas as pl
from jax.experimental.pallas import tpu as pltpu
from jax.sharding import PartitionSpec as P

E = 1024
H = 1024
V = 10240
NH = 128
Z = 64
STEP = 10
LANES = 128
ROW_TILE = 16
VMEM_BYTES = 56 * 1024 * 1024

EPS_NORM = 1e-05
EPS_FACT = 1e-30

F32 = jnp.float32
BF16 = jnp.bfloat16


def matmul(left, right):
    return jnp.dot(left, right, preferred_element_type=F32)


def dot_last(left, right):
    return lax.dot_general(left, right, (((1,), (1,)), ((), ())), preferred_element_type=F32)


def dot_first(left, right):
    return lax.dot_general(left, right, (((0,), (0,)), ((), ())), preferred_element_type=F32)


def adafactor(weight, grad, row_old, col_old, row_mean, col_mean, lead, rate):
    decay = 1.0 - STEP ** (-0.8)
    row_new = decay * row_old + (1.0 - decay) * row_mean
    col_new = decay * col_old + (1.0 - decay) * col_mean
    relative = row_new / jnp.mean(row_new, axis=-1, keepdims=True)
    relative = relative.reshape(relative.shape + (1,) * (grad.ndim - relative.ndim))
    spread = col_new[None] if lead == 0 else col_new[:, None]
    updated = weight - rate * grad * lax.rsqrt(relative * spread)
    return (grad, updated, row_new, col_new)


STACK_ROWS = 2304
SCALE_AT = 2 * E
VEC_AT = SCALE_AT + 3 * Z
TAIL_ROWS = STACK_ROWS - SCALE_AT
PACK = H + NH + 4 * Z
STAT_AT = 3 * Z
VOCAB_BLOCK = 256
SLOTS = (0, 2, 4, 6, 1, 3, 5, 7)


def swap(values, axis, size, bit):
    return lax.ppermute(values, axis, [(i, i ^ bit) for i in range(size)])


def tree_sum(values, axis, size):
    if size & (size - 1):
        return lax.psum(values, axis)
    bit = 1
    while bit < size:
        values = values + swap(values, axis, size, bit)
        bit *= 2
    return values


def tie(*values):
    return lax.optimization_barrier(values)


def weight_tail(w_scale, main_vectors):
    width = 4 * main_vectors.shape[2]
    vec = main_vectors.reshape(2, width)
    terms = []
    for _ in range(3):
        term = lax.reduce_precision(vec, 8, 7)
        terms.append(term.astype(BF16))
        vec = vec - term
    return jnp.concatenate(
        [w_scale.astype(BF16).reshape(3 * Z, width)]
        + terms
        + [jnp.zeros((STACK_ROWS - VEC_AT - 6, width), BF16)],
        axis=0,
    )


def piece_copies(refs, plan, main_v, sem, only=None):
    if plan is None:
        return [] if only else [(True, pltpu.make_async_copy(refs[0], main_v, sem.at[0]))]
    me = lax.axis_index("mp")
    b = lax.axis_index("batch")
    quarter = SCALE_AT // 4
    tail_quarter = TAIL_ROWS // 4
    copies = []

    def add(early, bits, ref, source, target, rows, spot):
        copies.append(
            (
                early,
                pltpu.make_async_copy(
                    ref.at[pl.ds(source, rows)],
                    main_v.at[me ^ bits, pl.ds(target, rows)],
                    sem.at[spot],
                ),
            )
        )

    for number, (ref, (bits, over, first, rows)) in enumerate(zip(refs, plan)):
        if only is not None and bits != only:
            continue
        spot = 2 * number
        if over is None and rows == SCALE_AT:
            add(True, bits, ref, 0, 0, E, spot)
            add(False, bits, ref, E, E, H, spot + 1)
            continue
        if over is None:
            add(True, bits, ref, 0, first, rows, spot)
            continue
        index = b ^ over
        of_main = max(0, min(rows, quarter - first))
        if of_main:
            start = pl.multiple_of(index * quarter + first, ROW_TILE)
            add(index < 2, bits, ref, 0, start, of_main, spot)
        if rows > of_main:
            start = SCALE_AT + index * tail_quarter + first + of_main - quarter
            add(True, bits, ref, of_main, pl.multiple_of(start, ROW_TILE), rows - of_main, spot + 1)
    return copies


def each_copy(copies, early, act):
    for needed, copy in copies:
        if isinstance(needed, bool):
            if needed == early:
                act(copy)
        else:

            @pl.when(needed if early else jnp.logical_not(needed))
            def _():
                act(copy)


def copy_count(plan):
    return 1 if plan is None else 2 * len(plan)


def load_vectors(vec_ref, main_v):
    for m in range(main_v.shape[0]):
        terms = main_v[m, VEC_AT : VEC_AT + ROW_TILE].astype(F32)
        vec_ref[m] = terms[0:2] + terms[2:4] + terms[4:6]


def masked_thirds(z_wide):
    lane = lax.broadcasted_iota(jnp.int32, z_wide.shape, 1) // Z
    zero = jnp.zeros_like(z_wide)
    return jnp.concatenate([jnp.where(lane == k, z_wide, zero) for k in range(3)], axis=0)


def beside(wide, columns):
    lane = lax.broadcasted_iota(jnp.int32, wide.shape, 1)
    count = len(columns)
    for spot, column in enumerate(columns):
        high = column.astype(BF16).astype(F32)
        wide = jnp.where(lane == STAT_AT + spot, high, wide)
        wide = jnp.where(lane == STAT_AT + count + spot, column - high, wide)
    return wide.astype(BF16)


def column_of(wide, count, spot):
    return wide[:, STAT_AT + spot : STAT_AT + spot + 1] + wide[
        :, STAT_AT + count + spot : STAT_AT + count + spot + 1
    ]


def forward_kernel(plan, x_ref, hyp_ref, hypb_ref, zp_ref, zpb_ref, *refs):
    n_pieces = 1 if plan is None else len(plan)
    forward_body(plan, x_ref, hyp_ref, hypb_ref, zp_ref, zpb_ref, refs[:n_pieces], *refs[n_pieces:])


def forward_body(
    plan, x_ref, hyp_ref, hypb_ref, zp_ref, zpb_ref, piece_refs,
    pack_out, cprev_out, tc_out, hcprev_out, thc_out, hg_out,
    ux_out, uh_out, one0_out, one1_out, n_out, act_out, rstd_out, vec_out,
    main_v, prex_s, h_s, c_s, hh_s, hc_s, sem,
):
    t = pl.program_id(0)
    nb, _, bw = main_v.shape
    bu = bw // 4
    steps, _, rows, _ = ux_out.shape

    @pl.when(t == 0)
    def _():
        pieces = piece_copies(piece_refs, plan, main_v, sem)
        for early in (True, False):
            each_copy(pieces, early, lambda copy: copy.start())
        prex_s[...] = (matmul(x_ref[...], hyp_ref[:E]) + hypb_ref[...]).reshape(steps, rows, 4 * NH)
        h_s[...] = jnp.zeros_like(h_s)
        c_s[...] = jnp.zeros_like(c_s)
        hh_s[...] = jnp.zeros_like(hh_s)
        hc_s[...] = jnp.zeros_like(hc_s)
        me = 0 if plan is None else lax.axis_index("mp")
        for bits in range(nb):
            each_copy(piece_copies(piece_refs, plan, main_v, sem, bits), True, lambda copy: copy.wait())
            m = me ^ bits
            ux = matmul(x_ref[...], main_v[m, :E])
            ux_out[:, m] = ux.reshape(steps, rows, bw)
        load_vectors(vec_out, main_v)
        uh_out[...] = jnp.zeros_like(uh_out)

    @pl.when(t == 1)
    def _():
        each_copy(piece_copies(piece_refs, plan, main_v, sem), False, lambda copy: copy.wait())

    h_prev = h_s[...]

    @pl.when(t > 0)
    def _():
        for m in range(nb):
            uh_out[0, m] = matmul(h_prev, main_v[m, E : 2 * E])

    hh_prev = hh_s[...]
    hc_prev = hc_s[...]
    q = prex_s[t] + matmul(h_prev, hyp_ref[E : E + H]) + matmul(hh_prev, hyp_ref[E + H : E + H + NH])
    q_in = jax.nn.sigmoid(q[:, :NH])
    q_forget = jax.nn.sigmoid(q[:, NH : 2 * NH])
    q_out = jax.nn.sigmoid(q[:, 2 * NH : 3 * NH])
    q_cell = jnp.tanh(q[:, 3 * NH :])
    hc = q_forget * hc_prev + q_in * q_cell
    thc = jnp.tanh(hc)
    hh = (q_out * thc).astype(BF16)
    z_wide = matmul(hh, zp_ref[...]) + zpb_ref[...]
    hcprev_out[0] = hc_prev
    thc_out[0] = thc
    hg_out[0, :, :NH] = q_in
    hg_out[0, :, NH : 2 * NH] = q_forget
    hg_out[0, :, 2 * NH : 3 * NH] = q_out
    hg_out[0, :, 3 * NH :] = q_cell
    pack_out[0, :, H : H + NH] = hh
    hh_s[...] = hh
    hc_s[...] = hc

    thirds = masked_thirds(z_wide.astype(BF16))
    sums = [jnp.zeros((rows, LANES), F32) for _ in range(4)]
    squares = [jnp.zeros((rows, LANES), F32) for _ in range(4)]
    for m in range(nb):
        scl = matmul(thirds, main_v[m, SCALE_AT:])
        uh = uh_out[0, m]
        one0 = 1.0 + scl[:rows]
        one1 = 1.0 + scl[rows : 2 * rows]
        s = one0 * uh + one1 * ux_out[t, m]
        one0_out[0, m] = one0
        one1_out[0, m] = one1
        act_out[0, m] = scl[2 * rows :]
        n_out[0, m] = s
        for g in range(4):
            for j in range(bu // LANES):
                piece = s[:, g * bu + j * LANES : g * bu + (j + 1) * LANES]
                sums[g] += piece
                squares[g] += piece * piece
    centres, rstds = [], []
    for g in range(4):
        centre = jnp.sum(sums[g], axis=1, keepdims=True) / H
        square = jnp.sum(squares[g], axis=1, keepdims=True) / H
        rstd = lax.rsqrt(square - centre * centre + EPS_NORM)
        centres.append(centre)
        rstds.append(rstd)
        rstd_out[0, :, g * LANES : (g + 1) * LANES] = jnp.broadcast_to(rstd, (rows, LANES))
    pack_out[0, :, H + NH :] = beside(z_wide, centres + rstds)

    for m in range(nb):
        cols = slice(m * bu, (m + 1) * bu)
        gates = []
        for g in range(4):
            here = slice(g * bu, (g + 1) * bu)
            n = (n_out[0, m, :, here] - centres[g]) * rstds[g]
            n_out[0, m, :, here] = n
            pre = vec_out[m, 0:1, here] * n + vec_out[m, 1:2, here] + act_out[0, m, :, here]
            gate = jnp.tanh(pre) if g == 3 else jax.nn.sigmoid(pre)
            act_out[0, m, :, here] = gate
            gates.append(gate)
        c_prev = c_s[:, cols]
        c_now = gates[1] * c_prev + gates[0] * gates[3]
        tc = jnp.tanh(c_now)
        h_now = (gates[2] * tc).astype(BF16)
        cprev_out[0, :, cols] = c_prev
        tc_out[0, :, cols] = tc
        c_s[:, cols] = c_now
        h_s[:, cols] = h_now
        pack_out[0, :, cols] = h_now


def turn_kernel(plan, me_ref, *refs):
    n_pieces = 1 if plan is None else len(plan)
    in_out, rec_out, tail_out, main_v, sem = refs[n_pieces:]
    step = pl.program_id(0)

    @pl.when(step == 0)
    def _():
        for _, copy in piece_copies(refs[:n_pieces], plan, main_v, sem):
            copy.start()

    for bits in range(main_v.shape[0]):

        @pl.when(step == bits)
        def _():
            for _, copy in piece_copies(refs[:n_pieces], plan, main_v, sem, bits):
                copy.wait()

    m = step ^ me_ref[0]
    in_out[0] = main_v[m, :E]
    rec_out[0] = main_v[m, E : 2 * E].T
    tail_out[0] = main_v[m, SCALE_AT:].T


def run_turn(blocks, plan, pieces):
    nb, bw = blocks
    me = jnp.zeros((1,), jnp.int32) if plan is None else lax.axis_index("mp").reshape(1)
    shapes = [(E, bw), (bw, H), (bw, TAIL_ROWS)]
    single = dict(pipeline_mode=pl.Buffered(1)) if nb == 1 else {}
    return pl.pallas_call(
        functools.partial(turn_kernel, plan),
        grid_spec=pltpu.PrefetchScalarGridSpec(
            num_scalar_prefetch=1,
            grid=(nb,),
            in_specs=[pl.BlockSpec(memory_space=pl.ANY)] * len(pieces),
            out_specs=[
                pl.BlockSpec((1,) + shape, lambda i, me: (i ^ me[0], 0, 0), **single) for shape in shapes
            ],
            scratch_shapes=[
                pltpu.VMEM((nb, STACK_ROWS, bw), BF16),
                pltpu.SemaphoreType.DMA((copy_count(plan),)),
            ],
        ),
        out_shape=[jax.ShapeDtypeStruct((nb,) + shape, BF16) for shape in shapes],
        compiler_params=kernel_params(),
        cost_estimate=pl.CostEstimate(flops=10**7, bytes_accessed=40_000_000, transcendentals=0),
        name="turn_weights",
    )(me, *pieces)


def backward_kernel(
    plan, in_hbm, rec_hbm, tail_hbm, dh_ref, hyp_ref, zp_ref,
    cprev_ref, tc_ref, hcprev_ref, thc_ref, hg_ref,
    ux_ref, uh_ref, one0_ref, one1_ref, n_ref, act_ref, rstd_ref, vec_ref,
    cols_out, dx_out, gv_out,
    in_v, rec_v, tail_v, dh_s, dc_s, dhh_s, dhc_s, da_s, stack_s, dux_s, dq_s, sem,
):
    step = pl.program_id(0)
    nb, _, bw = in_v.shape
    bu = bw // 4
    steps, rows, _ = dq_s.shape
    t = steps - 1 - step
    me = 0 if plan is None else lax.axis_index("mp")
    copies = [
        pltpu.make_async_copy(source, target, sem.at[spot])
        for spot, (source, target) in enumerate(((rec_hbm, rec_v), (tail_hbm, tail_v), (in_hbm, in_v)))
    ]

    @pl.when(step == 0)
    def _():
        for copy in copies:
            copy.start()
        dh_s[...] = jnp.zeros_like(dh_s)
        dc_s[...] = jnp.zeros_like(dc_s)
        dhh_s[...] = jnp.zeros_like(dhh_s)
        dhc_s[...] = jnp.zeros_like(dhc_s)
        gv_out[...] = jnp.zeros_like(gv_out)

    first = [jnp.zeros((rows, LANES), F32) for _ in range(4)]
    second = [jnp.zeros((rows, LANES), F32) for _ in range(4)]
    for m in range(nb):
        cols = slice(m * bu, (m + 1) * bu)
        gate = [act_ref[0, m, :, g * bu : (g + 1) * bu] for g in range(4)]
        tc = tc_ref[0, :, cols]
        dh = dh_ref[0, :, cols] + dh_s[:, cols]
        dc = dc_s[:, cols] + dh * gate[2] * (1.0 - tc * tc)
        da = [
            dc * gate[3] * gate[0] * (1.0 - gate[0]),
            dc * cprev_ref[0, :, cols] * gate[1] * (1.0 - gate[1]),
            dh * tc * gate[2] * (1.0 - gate[2]),
            dc * gate[0] * (1.0 - gate[3] * gate[3]),
        ]
        dc_s[:, cols] = dc * gate[1]
        if plan is not None:
            bits = me ^ m
            spot = bits // 2 + (nb // 2) * (bits % 2)
            cols_out[spot, t, :, :bu] = dh.astype(BF16)
        for g in range(4):
            here = slice(g * bu, (g + 1) * bu)
            n = n_ref[0, m, :, here]
            da_s[m, :, here] = da[g]
            if plan is None:
                gv_out[m, 0:1, here] += jnp.sum(da[g] * n, axis=0, keepdims=True)
                gv_out[m, 1:2, here] += jnp.sum(da[g], axis=0, keepdims=True)
            dn = vec_ref[m, 0:1, here] * da[g]
            dnn = dn * n
            for j in range(bu // LANES):
                first[g] += dn[:, j * LANES : (j + 1) * LANES]
                second[g] += dnn[:, j * LANES : (j + 1) * LANES]
    means = [
        (jnp.sum(first[g], axis=1, keepdims=True) / H, jnp.sum(second[g], axis=1, keepdims=True) / H)
        for g in range(4)
    ]

    for m in range(nb):
        ds_parts = []
        for g in range(4):
            here = slice(g * bu, (g + 1) * bu)
            dn = vec_ref[m, 0:1, here] * da_s[m, :, here]
            rstd = rstd_ref[0, :, g * LANES : g * LANES + 1]
            ds_parts.append(rstd * (dn - means[g][0] - n_ref[0, m, :, here] * means[g][1]))
        ds = jnp.concatenate(ds_parts, axis=1)
        da_low = da_s[m].astype(BF16)
        if plan is None:
            cols_out[m, t, :, :bw] = ds.astype(BF16)
            cols_out[m, t, :, bw:] = da_low
        stack_s[m, :rows] = (ds * uh_ref[0, m]).astype(BF16)
        stack_s[m, rows : 2 * rows] = (ds * ux_ref[0, m]).astype(BF16)
        stack_s[m, 2 * rows : 3 * rows] = da_low
        stack_s[m, 3 * rows :] = (ds * one0_ref[0, m]).astype(BF16)
        dux_s[t, m] = (ds * one1_ref[0, m]).astype(BF16)

    @pl.when(step == 0)
    def _():
        copies[0].wait()
        copies[1].wait()

    dz_all = jnp.zeros((3 * rows, 4 * Z), F32)
    dh_rec = jnp.zeros((rows, H), F32)
    for m in range(nb):
        dz_all += matmul(stack_s[m, : 3 * rows], tail_v[m])
    for m in range(nb):
        dh_rec += matmul(stack_s[m, 3 * rows :], rec_v[m])

    lane = lax.broadcasted_iota(jnp.int32, (rows, 4 * Z), 1) // Z
    dz = jnp.zeros((rows, 4 * Z), F32)
    for k in range(3):
        dz = jnp.where(lane == k, dz_all[k * rows : (k + 1) * rows], dz)
    half = 2 * NH
    cols_out[nb + 2, t, :, :half] = beside(dz, [m[0] for m in means] + [m[1] for m in means])
    q_in = hg_ref[0, :, :NH]
    q_forget = hg_ref[0, :, NH : 2 * NH]
    q_out = hg_ref[0, :, 2 * NH : 3 * NH]
    q_cell = hg_ref[0, :, 3 * NH :]
    thc = thc_ref[0]
    dhh = dhh_s[...] + dot_last(dz.astype(BF16), zp_ref[...])
    dhc = dhc_s[...] + dhh * q_out * (1.0 - thc * thc)
    dq = jnp.concatenate(
        [
            dhc * q_cell * q_in * (1.0 - q_in),
            dhc * hcprev_ref[0] * q_forget * (1.0 - q_forget),
            dhh * thc * q_out * (1.0 - q_out),
            dhc * q_in * (1.0 - q_cell * q_cell),
        ],
        axis=1,
    ).astype(BF16)
    cols_out[nb, t, :, :half] = dq[:, :half]
    cols_out[nb + 1, t, :, :half] = dq[:, half:]
    dq_s[t] = dq
    dhc_s[...] = dhc * q_forget
    dhh_s[...] = dot_last(dq, hyp_ref[E + H : E + H + NH])
    dh_s[...] = dh_rec + dot_last(dq, hyp_ref[E : E + H])

    @pl.when(step == steps - 1)
    def _():
        copies[2].wait()
        dx = dot_last(dq_s[...].reshape(steps * rows, 4 * NH), hyp_ref[:E])
        for m in range(nb):
            dx += dot_last(dux_s[:, m].reshape(steps * rows, bw), in_v[m])
        if plan is None:
            dx_out[...] = dx.astype(dx_out.dtype)
        else:
            for m in range(nb):
                bits = me ^ m
                spot = bits // 2 + (nb // 2) * (bits % 2)
                part = dx[:, m * bu : (m + 1) * bu].astype(BF16)
                cols_out[spot, :, :, bu : 2 * bu] = part.reshape(steps, rows, bu)


def whole(shape):
    return pl.BlockSpec(shape, lambda t: (0,) * len(shape), pipeline_mode=pl.Buffered(1))


def kernel_params():
    return pltpu.CompilerParams(vmem_limit_bytes=VMEM_BYTES)


def run_forward(x_rows, blocks, plan, pieces, hyp_low, hyp_bias, zp_wide, zp_bias, steps):
    nb, bw = blocks
    rows = x_rows.shape[0] // steps

    def stepped(*tail):
        return pl.BlockSpec((1,) + tail, lambda t: (t,) + (0,) * len(tail))

    tails = [
        (BF16, (rows, PACK)), (F32, (rows, H)), (F32, (rows, H)), (F32, (rows, NH)), (F32, (rows, NH)),
        (F32, (rows, 4 * NH)), (F32, (nb, rows, bw)), (F32, (nb, rows, bw)), (F32, (nb, rows, bw)),
        (F32, (nb, rows, bw)), (F32, (nb, rows, bw)), (F32, (nb, rows, bw)), (F32, (rows, 4 * LANES)),
    ]
    out_specs = [stepped(*tail) for _, tail in tails]
    out_specs[6] = pl.BlockSpec((steps, nb, rows, bw), lambda t: (0, 0, 0, 0))
    out_shape = [jax.ShapeDtypeStruct((steps,) + tail, dtype) for dtype, tail in tails]
    work = steps * rows * 4 * H * (2 * H + E + 3 * 4 * Z)
    return pl.pallas_call(
        functools.partial(forward_kernel, plan),
        grid=(steps,),
        in_specs=[
            whole(x_rows.shape),
            whole(hyp_low.shape),
            whole(hyp_bias.shape),
            whole(zp_wide.shape),
            whole(zp_bias.shape),
        ]
        + [pl.BlockSpec(memory_space=pl.ANY)] * len(pieces),
        out_specs=out_specs + [pl.BlockSpec((nb, 2, bw), lambda t: (0, 0, 0))],
        out_shape=out_shape + [jax.ShapeDtypeStruct((nb, 2, bw), F32)],
        scratch_shapes=[
            pltpu.VMEM((nb, STACK_ROWS, bw), BF16),
            pltpu.VMEM((steps, rows, 4 * NH), F32),
            pltpu.VMEM((rows, H), BF16),
            pltpu.VMEM((rows, H), F32),
            pltpu.VMEM((rows, NH), BF16),
            pltpu.VMEM((rows, NH), F32),
            pltpu.SemaphoreType.DMA((copy_count(plan),)),
        ],
        compiler_params=kernel_params(),
        cost_estimate=pl.CostEstimate(flops=2 * work, bytes_accessed=40_000_000, transcendentals=0),
        name="recurrence_forward",
    )(x_rows, hyp_low, hyp_bias, zp_wide, zp_bias, *pieces)


def run_backward(dh_top, blocks, plan, turned, hyp_low, zp_wide, kept):
    nb, bw = blocks
    steps, rows, _ = dh_top.shape

    def stepped(*tail):
        return pl.BlockSpec((1,) + tail, lambda s: (steps - 1 - s,) + (0,) * len(tail))

    def still(shape):
        return pl.BlockSpec(shape, lambda s: (0,) * len(shape))

    tails = [
        (rows, H), (rows, H), (rows, NH), (rows, NH), (rows, 4 * NH), (nb, rows, bw), (nb, rows, bw),
        (nb, rows, bw), (nb, rows, bw), (nb, rows, bw), (nb, rows, bw), (rows, 4 * LANES),
    ]
    per_owner = 2 * bw if plan is None else 2 * (bw // 4)
    outs = [
        jax.ShapeDtypeStruct((nb + 3, steps, rows, per_owner), BF16),
        jax.ShapeDtypeStruct((steps * rows, E), BF16),
        jax.ShapeDtypeStruct((nb, 2, bw), F32),
    ]
    work = steps * rows * 4 * H * (2 * H + E + 3 * 4 * Z)
    return pl.pallas_call(
        functools.partial(backward_kernel, plan),
        grid=(steps,),
        in_specs=[pl.BlockSpec(memory_space=pl.ANY)] * len(turned)
        + [stepped(rows, H), whole(hyp_low.shape), whole(zp_wide.shape)]
        + [stepped(*tail) for tail in tails]
        + [whole((nb, 2, bw))],
        out_specs=[
            still(outs[0].shape),
            still(outs[1].shape),
            still(outs[2].shape),
        ],
        out_shape=outs,
        scratch_shapes=[
            pltpu.VMEM((nb, E, bw), BF16),
            pltpu.VMEM((nb, bw, H), BF16),
            pltpu.VMEM((nb, bw, TAIL_ROWS), BF16),
            pltpu.VMEM((rows, H), F32),
            pltpu.VMEM((rows, H), F32),
            pltpu.VMEM((rows, NH), F32),
            pltpu.VMEM((rows, NH), F32),
            pltpu.VMEM((nb, rows, bw), F32),
            pltpu.VMEM((nb, 4 * rows, bw), BF16),
            pltpu.VMEM((steps, nb, rows, bw), BF16),
            pltpu.VMEM((steps, rows, 4 * NH), BF16),
            pltpu.SemaphoreType.DMA((3,)),
        ],
        compiler_params=kernel_params(),
        cost_estimate=pl.CostEstimate(flops=2 * work, bytes_accessed=60_000_000, transcendentals=0),
        name="recurrence_backward",
    )(*turned, dh_top, hyp_low, zp_wide, *kept)


def column_forward_kernel(
    steps, slots_ref, pack0_ref, pack1_ref, x0_ref, x1_ref, main_ref, tail_ref, vec_ref,
    uh_out, ux_out, one0_out, one1_out, n_out, act_out, cprev_out, tc_out, rstd_out,
    left_out, x_out, hb_out, hhb_out, hh_out, z_out,
):
    _, total, _ = pack0_ref.shape
    rows = total // steps
    width = main_ref.shape[1]
    units = width // 4

    def one_before(values):
        return jnp.concatenate([jnp.zeros_like(values[:rows]), values[: total - rows]], axis=0)

    for half, (pack_ref, x_ref) in enumerate(((pack0_ref, x0_ref), (pack1_ref, x1_ref))):
        h_before = one_before(pack_ref[0, :, :H])
        hh = pack_ref[0, :, H : H + NH]
        z_wide = pack_ref[0, :, H + NH :]
        x_now = jnp.concatenate([x_ref[k, 0] for k in range(x_ref.shape[0])], axis=1)
        mine = pl.ds(pl.multiple_of(slots_ref[0] * units, units), units)
        part = x_ref.shape[3]
        left_out[half, 0, :, :part] = x_ref[slots_ref[0], 0]
        left_out[half, 0, :, part:] = one_before(pack_ref[0, :, mine])
        x_out[half, 0] = x_now
        hb_out[half, 0] = h_before
        hhb_out[half, 0] = one_before(hh)
        hh_out[half, 0] = hh
        z_out[half, 0] = z_wide
        stats = z_wide.astype(F32)
        uh = matmul(h_before, main_ref[E : 2 * E])
        ux = matmul(x_now, main_ref[:E])
        scl = matmul(masked_thirds(z_wide), tail_ref[...])
        one0 = 1.0 + scl[:total]
        one1 = 1.0 + scl[total : 2 * total]
        s = one0 * uh + one1 * ux
        uh_out[half, 0] = uh
        ux_out[half, 0] = ux
        one0_out[half, 0] = one0
        one1_out[half, 0] = one1
        for g in range(4):
            here = slice(g * units, (g + 1) * units)
            rstd = column_of(stats, 8, 4 + g)
            n = (s[:, here] - column_of(stats, 8, g)) * rstd
            pre = vec_ref[0:1, here] * n + vec_ref[1:2, here] + scl[2 * total :, here]
            n_out[half, 0, :, here] = n
            act_out[half, 0, :, here] = jnp.tanh(pre) if g == 3 else jax.nn.sigmoid(pre)
            rstd_out[half, 0, :, here] = jnp.broadcast_to(rstd, (total, units))
        c = jnp.zeros((rows, units), F32)
        for t in range(steps):
            now = slice(t * rows, (t + 1) * rows)
            gate = [act_out[half, 0, now, g * units : (g + 1) * units] for g in range(4)]
            cprev_out[half, 0, now] = c
            c = gate[1] * c + gate[0] * gate[3]
            tc_out[half, 0, now] = jnp.tanh(c)


def column_backward_kernel(
    steps, dh0_ref, dh1_ref, back0_ref, back1_ref, vec_ref,
    uh_ref, ux_ref, one0_ref, one1_ref, n_ref, act_ref, cprev_ref, tc_ref, rstd_ref,
    dux_out, duh_out, d0_out, d1_out, da_out, gv_out,
    dc_s,
):
    _, total, units = dh0_ref.shape
    rows = total // steps

    @pl.when(pl.program_id(0) == 0)
    def _():
        gv_out[...] = jnp.zeros_like(gv_out)

    for half, (dh_ref, back_ref) in enumerate(((dh0_ref, back0_ref), (dh1_ref, back1_ref))):
        means = back_ref[0, 0].astype(F32)
        dh = dh_ref[0].astype(F32)
        gate = [act_ref[half, 0, :, g * units : (g + 1) * units] for g in range(4)]
        tc = tc_ref[half, 0]
        local = dh * gate[2] * (1.0 - tc * tc)
        dc = jnp.zeros((rows, units), F32)
        for t in reversed(range(steps)):
            now = slice(t * rows, (t + 1) * rows)
            dc = dc + local[now]
            dc_s[now] = dc
            dc = dc * gate[1][now]
        dc = dc_s[...]
        da = [
            dc * gate[3] * gate[0] * (1.0 - gate[0]),
            dc * cprev_ref[half, 0] * gate[1] * (1.0 - gate[1]),
            dh * tc * gate[2] * (1.0 - gate[2]),
            dc * gate[0] * (1.0 - gate[3] * gate[3]),
        ]
        for g in range(4):
            here = slice(g * units, (g + 1) * units)
            n = n_ref[half, 0, :, here]
            gv_out[0:1, here] += jnp.sum(da[g] * n, axis=0, keepdims=True)
            gv_out[1:2, here] += jnp.sum(da[g], axis=0, keepdims=True)
            dn = vec_ref[0:1, here] * da[g]
            ds = rstd_ref[half, 0, :, here] * (
                dn - column_of(means, 8, g) - n * column_of(means, 8, 4 + g)
            )
            dux_out[half, 0, :, here] = (ds * one1_ref[half, 0, :, here]).astype(BF16)
            duh_out[half, 0, :, here] = (ds * one0_ref[half, 0, :, here]).astype(BF16)
            d0_out[half, 0, :, here] = (ds * uh_ref[half, 0, :, here]).astype(BF16)
            d1_out[half, 0, :, here] = (ds * ux_ref[half, 0, :, here]).astype(BF16)
            da_out[half, 0, :, here] = da[g].astype(BF16)


def half_specs(total, width):
    return [pl.BlockSpec((1, total, width), lambda i, at=at: (i + at, 0, 0)) for at in (0, 4)]


def run_column_forward(slots, near, rest, x_all, main_own, tail_own, vec, steps):
    per_core, total, _ = near.shape
    n_parts, owners, _, emb_part = x_all.shape
    width = main_own.shape[1]
    units = width // 4
    tails = [(F32, width)] * 6 + [(F32, units)] * 2 + [(F32, width)]
    tails += [(BF16, emb_part + units), (BF16, E), (BF16, H), (BF16, NH), (BF16, NH), (BF16, 4 * Z)]

    def still(shape):
        return pl.BlockSpec(shape, lambda i, slots: (0,) * len(shape), pipeline_mode=pl.Buffered(1))

    return pl.pallas_call(
        functools.partial(column_forward_kernel, steps),
        grid_spec=pltpu.PrefetchScalarGridSpec(
            num_scalar_prefetch=1,
            grid=(per_core,),
            in_specs=[pl.BlockSpec((1, total, PACK), lambda i, slots: (i, 0, 0))] * 2
            + [
                pl.BlockSpec(
                    (n_parts, 1, total, emb_part), lambda i, slots, at=at: (0, slots[i + at], 0, 0)
                )
                for at in (0, per_core)
            ]
            + [still(main_own.shape), still(tail_own.shape), still(vec.shape)],
            out_specs=[
                pl.BlockSpec((2, 1, total, tail), lambda i, slots: (0, i, 0, 0)) for _, tail in tails
            ],
        ),
        out_shape=[jax.ShapeDtypeStruct((2, per_core, total, tail), dtype) for dtype, tail in tails],
        compiler_params=kernel_params(),
        cost_estimate=pl.CostEstimate(
            flops=2 * owners * total * width * 3 * H, bytes_accessed=18_000_000, transcendentals=0
        ),
        name="column_forward",
    )(slots, near, rest, x_all, x_all, main_own, tail_own, vec)


def run_column_backward(moved, back_all, vec, kept, steps):
    owners, total, _ = moved.shape
    width = vec.shape[1]
    units = width // 4
    widths = [width] * 6 + [units] * 2 + [width]
    return pl.pallas_call(
        functools.partial(column_backward_kernel, steps),
        grid=(owners // 2,),
        in_specs=half_specs(total, units)
        + [
            pl.BlockSpec((1, 1, total, 4 * Z), lambda i, at=at: (i + at, 2, 0, 0)) for at in (0, 4)
        ]
        + [whole(vec.shape)]
        + [pl.BlockSpec((2, 1, total, tail), lambda i: (0, i, 0, 0)) for tail in widths],
        out_specs=[pl.BlockSpec((2, 1, total, width), lambda i: (0, i, 0, 0))] * 5
        + [pl.BlockSpec((2, width), lambda i: (0, 0))],
        out_shape=[jax.ShapeDtypeStruct((2, owners // 2, total, width), BF16)] * 5
        + [jax.ShapeDtypeStruct((2, width), F32)],
        scratch_shapes=[pltpu.VMEM((total, units), F32)],
        compiler_params=kernel_params(),
        cost_estimate=pl.CostEstimate(
            flops=40 * owners * total * width, bytes_accessed=16_000_000, transcendentals=0
        ),
        name="column_backward",
    )(moved, moved, back_all, back_all, vec, *kept)


def table_kernel(
    me_ref, told_ref, r0_ref, r1_ref, r2_ref, r3_ref, table_out, row_out, col_out, rows_s, other_s
):
    count = rows_s.shape[0] // 4
    stride = told_ref.shape[0] // 4
    table_out[...] = jnp.zeros_like(table_out)
    other_s[...] = jnp.zeros_like(other_s)
    for part, ref in enumerate((r0_ref, r1_ref, r2_ref, r3_ref)):
        rows_s[part * count : (part + 1) * count] = ref[:count].astype(F32)

    for owner in range(4):
        part = owner ^ me_ref[0]

        @pl.loop(0, count // 16)
        def _(group):
            for lane in range(16):
                here = pl.ds(told_ref[part * stride + group * 16 + lane], 1)
                table = table_out if lane % 2 == 0 else other_s
                table[here] += rows_s[pl.ds(part * count + group * 16 + lane, 1)]

    def measure(block, cols):
        here = pl.ds(pl.multiple_of(block * VOCAB_BLOCK, VOCAB_BLOCK), VOCAB_BLOCK)
        values = table_out[here] + other_s[here]
        table_out[here] = values
        squares = values * values + EPS_FACT
        high = squares.astype(BF16)
        low = (squares - high.astype(F32)).astype(BF16)
        ones = jnp.ones((8, squares.shape[1]), BF16)
        sums = dot_last(ones, high) + dot_last(ones, low)
        row_out[pl.ds(block, 1)] = sums[:1]
        return cols + jnp.sum(squares, axis=0, keepdims=True)

    zero = jnp.zeros((1, table_out.shape[1]), F32)
    col_out[...] = lax.fori_loop(0, row_out.shape[0], measure, zero)


def run_table(me, told, parts, vocab):
    count, lanes = parts[0].shape
    total = count * len(parts)
    blocks = vocab // VOCAB_BLOCK
    return pl.pallas_call(
        table_kernel,
        grid_spec=pltpu.PrefetchScalarGridSpec(
            num_scalar_prefetch=2,
            grid=(1,),
            in_specs=[pl.BlockSpec(part.shape, lambda i, *_: (0, 0)) for part in parts],
            out_specs=[
                pl.BlockSpec((vocab, lanes), lambda i, *_: (0, 0)),
                pl.BlockSpec((blocks, VOCAB_BLOCK), lambda i, *_: (0, 0)),
                pl.BlockSpec((1, lanes), lambda i, *_: (0, 0)),
            ],
            scratch_shapes=[pltpu.VMEM((total, lanes), F32), pltpu.VMEM((vocab, lanes), F32)],
        ),
        out_shape=[
            jax.ShapeDtypeStruct((vocab, lanes), F32),
            jax.ShapeDtypeStruct((blocks, VOCAB_BLOCK), F32),
            jax.ShapeDtypeStruct((1, lanes), F32),
        ],
        compiler_params=kernel_params(),
        cost_estimate=pl.CostEstimate(flops=10**9, bytes_accessed=40_000_000, transcendentals=0),
        name="embedding_table",
    )(me, told, *parts)


def stepped_update(weight, grad, relative, spread, rate):
    return weight - rate * grad * lax.rsqrt(relative * spread)


def main_update_kernel(rate, me_ref, p0, p1, p2, p3, weight_ref, rel_ref, spread_ref, grad_out, new_out):
    quarter, part = pl.program_id(0), pl.program_id(1)
    lanes = weight_ref.shape[1]
    gates = spread_ref.shape[0]
    rows = weight_ref.shape[0] // gates
    for bits, ref in enumerate((p0, p1, p2, p3)):

        @pl.when(quarter == bits)
        def _():
            here = pl.ds(pl.multiple_of(part * rows, rows), rows)
            for g in range(gates):
                spot = pl.ds(g, rows, stride=gates)
                grad = ref[here, g * lanes : (g + 1) * lanes].astype(F32)
                grad_out[spot, :] = grad
                new_out[spot, :] = stepped_update(
                    weight_ref[spot, :], grad, rel_ref[...], spread_ref[g : g + 1], rate
                )


def run_main_update(me, parts, weight, rel_wide, spread, rate):
    total, gates, lanes = weight.shape
    rows = total // 8

    def place(quarter, part, me_ref):
        return (part * 4 + (me_ref[0] ^ quarter), 0)

    block = pl.BlockSpec((rows * gates, lanes), place)
    flat = jax.ShapeDtypeStruct((total * gates, lanes), F32)
    grad, new = pl.pallas_call(
        functools.partial(main_update_kernel, rate),
        grid_spec=pltpu.PrefetchScalarGridSpec(
            num_scalar_prefetch=1,
            grid=(4, 2),
            in_specs=[pl.BlockSpec(part.shape, lambda q, p, m: (0, 0)) for part in parts]
            + [
                block,
                pl.BlockSpec((rows, LANES), place),
                pl.BlockSpec(spread.shape, lambda q, p, m: (0, 0)),
            ],
            out_specs=[block, block],
        ),
        out_shape=[flat, flat],
        compiler_params=kernel_params(),
        cost_estimate=pl.CostEstimate(flops=10**7, bytes_accessed=16_000_000, transcendentals=0),
        name="main_update",
    )(me, *parts, weight.reshape(total * gates, lanes), rel_wide, spread)
    return grad.reshape(weight.shape), new.reshape(weight.shape)


def out_update_kernel(rate, seen_ref, weight_ref, rel_ref, spread_ref, grad_out, new_out):
    for j in range(grad_out.shape[1] // LANES):
        cols = slice(j * LANES, (j + 1) * LANES)
        grad = seen_ref[:, cols].astype(F32)
        grad_out[:, cols] = grad
        new_out[:, cols] = stepped_update(weight_ref[:, cols], grad, rel_ref[...], spread_ref[:, cols], rate)


def run_out_update(seen, weight, rel_wide, spread, rate):
    total, width = weight.shape
    rows = total // 8

    def rows_of(columns):
        return pl.BlockSpec((rows, columns), lambda i: (i, 0))

    return pl.pallas_call(
        functools.partial(out_update_kernel, rate),
        grid=(8,),
        in_specs=[rows_of(width), rows_of(width), rows_of(LANES), pl.BlockSpec(spread.shape, lambda i: (0, 0))],
        out_specs=[rows_of(width)] * 2,
        out_shape=[jax.ShapeDtypeStruct(weight.shape, F32)] * 2,
        compiler_params=kernel_params(),
        cost_estimate=pl.CostEstimate(flops=10**7, bytes_accessed=20_000_000, transcendentals=0),
        name="out_update",
    )(seen, weight, rel_wide, spread)


def hyper_update_kernel(
    rate, parts_ref, bias_ref, weight_ref, row_ref, col_ref, grad_out, new_out, row_out, col_out
):
    quarters, owners, _, _ = parts_ref.shape
    total, width = grad_out.shape
    devices = quarters * owners
    heights = (E // devices, H // devices, NH // devices)
    for owner in range(owners):
        for quarter in range(quarters):
            part = parts_ref[quarter, owner].astype(F32)
            place = owner * quarters + quarter
            first, start = 0, 0
            for height, size in zip(heights, (E, H, NH)):
                to = start + place * height
                grad_out[to : to + height] = part[first : first + height]
                first += height
                start += size
    grad_out[total - 1 :] = bias_ref[...]
    decay = 1.0 - STEP ** (-0.8)
    blocks = [(at, min(256, total - at)) for at in range(0, total, 256)]
    cols = jnp.zeros((1, width), F32)
    sums = jnp.zeros((1, LANES), F32)
    for at, size in blocks:
        here = slice(at, at + size)
        grad = grad_out[here]
        squares = grad * grad + EPS_FACT
        cols += jnp.sum(squares, axis=0, keepdims=True)
        mean = jnp.sum(squares, axis=1, keepdims=True) / width
        row_new = decay * row_ref[here] + (1.0 - decay) * mean
        row_out[here] = row_new
        sums += jnp.sum(row_new, axis=0, keepdims=True)
    col_new = decay * col_ref[...] + (1.0 - decay) * (cols / total)
    col_out[...] = col_new
    average = sums / total
    for at, size in blocks:
        here = slice(at, at + size)
        relative = row_out[here] / average
        for j in range(width // LANES):
            lanes = slice(j * LANES, (j + 1) * LANES)
            new_out[here, lanes] = stepped_update(
                weight_ref[here, lanes], grad_out[here, lanes], relative, col_new[:, lanes], rate
            )


def run_hyper_update(parts, bias, weight, row_wide, col, rate):
    total, width = weight.shape

    def all_of(values):
        return pl.BlockSpec(values.shape, lambda i: (0,) * values.ndim)

    return pl.pallas_call(
        functools.partial(hyper_update_kernel, rate),
        grid=(1,),
        in_specs=[all_of(values) for values in (parts, bias, weight, row_wide, col)],
        out_specs=[all_of(values) for values in (weight, weight, row_wide, col)],
        out_shape=[
            jax.ShapeDtypeStruct(weight.shape, F32),
            jax.ShapeDtypeStruct(weight.shape, F32),
            jax.ShapeDtypeStruct(row_wide.shape, F32),
            jax.ShapeDtypeStruct(col.shape, F32),
        ],
        compiler_params=kernel_params(),
        cost_estimate=pl.CostEstimate(flops=10**7, bytes_accessed=20_000_000, transcendentals=0),
        name="hyper_update",
    )(parts, bias, weight, row_wide, col)


def updates(weights, states, grads, row_sums, embed_col_mean):
    embed, w_main, w_scale, w_hyper, w_zproj, w_out, main_vectors = weights
    (
        embed_row, embed_col, main_row, main_col, scale_row, scale_col, hyper_row, hyper_col,
        zproj_row, zproj_col, out_row, out_col, vector_state,
    ) = states
    g_embed, g_main, g_scale, g_hyper, g_zproj, g_out, g_vec = grads
    row_embed, row_main, row_scale, row_out = row_sums
    sq_main, sq_scale, sq_hyper, sq_zproj, sq_out = [
        g * g + EPS_FACT for g in (g_main, g_scale, g_hyper, g_zproj, g_out)
    ]
    res_embed = adafactor(
        embed, g_embed, embed_row, embed_col, row_embed / E, embed_col_mean, 0, 1.0
    )
    res_main = adafactor(
        w_main,
        g_main,
        main_row,
        main_col,
        row_main / (4 * H),
        jnp.mean(sq_main, axis=0),
        0,
        1.0 / math.sqrt(E),
    )
    res_scale = adafactor(
        w_scale,
        g_scale,
        scale_row,
        scale_col,
        row_scale / (4 * H),
        jnp.mean(sq_scale, axis=1),
        1,
        1.0 / math.sqrt(Z),
    )
    res_hyper = adafactor(
        w_hyper,
        g_hyper,
        hyper_row,
        hyper_col,
        jnp.mean(sq_hyper, axis=1),
        jnp.mean(sq_hyper, axis=0),
        0,
        1.0 / math.sqrt(E + H + NH + 1),
    )
    res_zproj = adafactor(
        w_zproj,
        g_zproj,
        zproj_row,
        zproj_col,
        jnp.mean(sq_zproj, axis=1),
        jnp.mean(sq_zproj, axis=0),
        0,
        2.0 / math.sqrt(NH),
    )
    res_out = adafactor(
        w_out, g_out, out_row, out_col, row_out / V, jnp.mean(sq_out, axis=0), 0, 3.0 / math.sqrt(H)
    )
    decay = 1.0 - STEP ** (-0.8)
    state_new = decay * vector_state + (1.0 - decay) * (g_vec * g_vec + EPS_FACT)
    vectors_new = main_vectors - 0.1 * g_vec * lax.rsqrt(state_new)
    return (
        res_embed
        + res_main
        + res_scale
        + res_hyper
        + res_zproj
        + res_out
        + (g_vec, state_new, vectors_new)
    )


def per_chip(
    parts,
    token_ids,
    seq_lengths,
    valid_mask,
    embed,
    w_main,
    w_scale,
    w_hyper,
    w_zproj,
    w_out,
    main_vectors,
    *states,
):
    n_mp, n_batch = parts
    my = lax.axis_index("mp")
    b = lax.axis_index("batch")
    units = w_main.shape[2]
    width = 4 * units
    emb_part = embed.shape[1]
    vocab_part = w_out.shape[1]
    batch_rows, steps = valid_mask.shape
    own = batch_rows // n_mp
    own_total = steps * own
    total = batch_rows * steps
    slots = my ^ jnp.array(SLOTS, jnp.int32)
    order = my ^ jnp.arange(n_mp, dtype=jnp.int32)
    from_slots = order // 2 + (n_mp // 2) * (order % 2)

    def by_owner(values):
        return values.reshape(n_mp, own, steps).transpose(0, 2, 1)

    def to_partners(values):
        return [swap(values, "batch", n_batch, bits) for bits in (1, 2, 3)]

    def quarter_of(values, bits, rows):
        return lax.dynamic_slice_in_dim(values, (b ^ bits) * rows, rows, 0)

    def placed(pieces, me):
        out = jnp.zeros((len(pieces),) + pieces[0].shape, pieces[0].dtype)
        for bits, piece in enumerate(pieces):
            out = lax.dynamic_update_slice_in_dim(out, piece[None], me ^ bits, 0)
        return out

    quarter = SCALE_AT // 4
    tail_quarter = TAIL_ROWS // 4
    half = (quarter + tail_quarter) // 2

    def own_rows(first, rows):
        values = lax.dynamic_slice_in_dim(w_main, b * quarter + first, rows, 0)
        return values.astype(BF16).reshape(rows, width)

    head_part = own_rows(0, half)
    head = swap(head_part, "mp", n_mp, 2)
    tail_own = weight_tail(w_scale, main_vectors)
    tail_part = jnp.concatenate(
        [own_rows(half, quarter - half), lax.dynamic_slice_in_dim(tail_own, b * tail_quarter, tail_quarter, 0)], axis=0
    )
    x_part = embed[by_owner(token_ids[:, :steps]).reshape(total)].astype(BF16)
    tail_part, head_part, head, x_part = tie(tail_part, head_part, head, x_part)
    tail = swap(tail_part, "mp", n_mp, 2)
    far = swap(jnp.concatenate([head_part, tail_part], axis=0), "mp", n_mp, 4)
    main_own = w_main.astype(BF16).reshape(2 * E, width)
    hyp_low = w_hyper.astype(BF16)
    both = swap(far, "mp", n_mp, 2)
    x_all = lax.all_gather(x_part, "mp").reshape(n_mp, n_mp, own_total, emb_part)
    x_own = lax.dynamic_index_in_dim(x_all, my, 1, False).transpose(1, 0, 2).reshape(own_total, E)
    found = []
    for array, bits in ((main_own, 0), (swap(main_own, "mp", n_mp, 1), 1)):
        found.append((array, bits, None, 0, SCALE_AT))
    for array, bits in ((tail_own, 0), (swap(tail_own, "mp", n_mp, 1), 1)):
        found.append((array, bits, None, SCALE_AT, TAIL_ROWS))
    for got, bits, start in ((head, 2, 0), (tail, 2, half), (far, 4, 0), (both, 6, 0)):
        cut = got.shape[0] // 2
        along_x = swap(got, "batch", n_batch, 1)
        along_y = swap(got, "batch", n_batch, 2)
        low = swap(along_x[:cut], "batch", n_batch, 2)
        high = swap(along_y[cut:], "batch", n_batch, 1)
        for array, over, first in (
            (got, 0, start), (along_x, 1, start), (along_y, 2, start), (low, 3, start), (high, 3, start + cut),
        ):
            found.append((array, bits, over, first, array.shape[0]))
            found.append((swap(array, "mp", n_mp, 1), bits ^ 1, over, first, array.shape[0]))
    found.sort(key=lambda piece: piece[1])
    plan = [piece[1:] for piece in found]
    pieces = [piece[0] for piece in found]
    blocks = (n_mp, width)
    hyp_bias = hyp_low[E + H + NH :].astype(F32)
    zp_wide = jnp.pad(w_zproj, ((0, 0), (0, Z))).astype(BF16)
    zp_bias = zp_wide[NH:].astype(F32)
    pack, *kept = run_forward(
        x_own, blocks, plan, pieces, hyp_low, hyp_bias, zp_wide[:NH], zp_bias, steps
    )

    def of_chips(values):
        return jnp.stack([values] + [swap(values, "mp", n_mp, bits) for bits in (2, 4, 6)])

    def both_halves(near):
        return jnp.concatenate([near, swap(near, "mp", n_mp, 1)], axis=0)

    pack, token_ids, seq_lengths, valid_mask, w_out, *pieces = tie(
        pack, token_ids, seq_lengths, valid_mask, w_out, *pieces
    )
    near = of_chips(pack.reshape(own_total, PACK))
    positions = jnp.arange(steps, dtype=jnp.int32)
    valid = valid_mask * (positions[None, :] < seq_lengths[:, None]).astype(jnp.int32)
    marks = jnp.stack([token_ids[:, :steps], token_ids[:, 1:], valid])
    marks = marks.reshape(3, n_mp, own, steps).transpose(0, 1, 3, 2)[:, slots].reshape(3, total)
    told = jnp.concatenate([marks[0], jnp.broadcast_to(jnp.sum(valid), (LANES,))])
    told = jnp.concatenate([told, swap(told, "batch", n_batch, 1)])
    weight_rows = marks[2].astype(F32)
    out_low = w_out.astype(BF16)
    turned = run_turn(blocks, plan, pieces)
    near, told, marks, weight_rows, out_low, *turned = tie(near, told, marks, weight_rows, out_low, *turned)
    rest = swap(near, "mp", n_mp, 1)
    h_all = jnp.concatenate([near[:, :, :H], rest[:, :, :H]], axis=0)
    h_rows = h_all.reshape(total, H)
    logits = matmul(h_rows, out_low)
    local_target = marks[1] - my * vocab_part
    hit = jnp.arange(vocab_part, dtype=jnp.int32)[None, :] == local_target[:, None]
    top = jnp.max(logits, axis=1)
    stats = [
        top,
        jnp.sum(jnp.exp(logits - top[:, None]), axis=1),
        jnp.sum(jnp.where(hit, logits, 0.0), axis=1),
    ]

    def merged(one, two):
        top = jnp.maximum(one[0], two[0])
        exps = one[1] * jnp.exp(one[0] - top) + two[1] * jnp.exp(two[0] - top)
        return jnp.stack([top, exps, one[2] + two[2]])

    def from_partner(values, bits):
        spots = [bits ^ slot for slot in SLOTS]
        spots = [spot // 2 + (n_mp // 2) * (spot % 2) for spot in spots]
        turned = jnp.concatenate([values[:, spot : spot + 1] for spot in spots], axis=1)
        return swap(turned, "mp", n_mp, bits)

    stats = jnp.stack(stats).reshape(3, n_mp, own_total)
    pair = merged(stats, from_partner(stats, 1))
    pair, told = tie(pair, told)
    others = [from_partner(pair, bits) for bits in (2, 4, 6)]
    told = jnp.concatenate([told, swap(told, "batch", n_batch, 2)])
    count = sum(told[k * (total + LANES) + total] for k in range(n_batch)).astype(F32)
    stats = merged(merged(pair, others[0]), merged(others[1], others[2]))
    log_total = (stats[0] + jnp.log(stats[1])).reshape(total)
    loss = jnp.sum(
        (log_total[:own_total] - stats[2].reshape(total)[:own_total]) * weight_rows[:own_total]
    )
    grad_logits = (
        (jnp.exp(logits - log_total[:, None]) - hit.astype(F32)) * (weight_rows / count)[:, None]
    ).astype(BF16)
    other = swap(dot_last(grad_logits[total // 2 :], out_low).astype(BF16), "mp", n_mp, 1)
    both_cores = dot_last(grad_logits[: total // 2], out_low) + other.astype(F32)
    near, rest, both_cores = tie(near, rest, both_cores.reshape(n_mp // 2, own_total, H))
    dh_parts = [
        swap(both_cores[spot].astype(BF16), "mp", n_mp, 2 * spot) for spot in range(1, n_mp // 2)
    ]
    vec = main_vectors.reshape(2, width)
    column = run_column_forward(slots, near, rest, x_all, main_own, tail_own, vec, steps)
    dh_parts[1], *column = tie(dh_parts[1], *column)
    h_rows, dh_parts[0] = tie(h_rows, dh_parts[0])
    g_out = dot_first(h_rows, grad_logits).astype(BF16)
    out_quarter = H // n_batch
    out_parts = [quarter_of(g_out, bits, out_quarter) for bits in range(n_batch)]
    dh_top = both_cores[0]
    for part in dh_parts:
        dh_top = dh_top + part.astype(F32)
    dh_top, *out_parts = tie(dh_top, *out_parts)
    out_got = [swap(part, "batch", n_batch, bits) for bits, part in enumerate(out_parts) if bits]
    moved, _, _ = run_backward(
        dh_top.reshape(steps, own, H), blocks, plan, turned, hyp_low, zp_wide[:NH], kept
    )
    left, x_rows, h_before, hh_before, hh_all, z_all = column[9:]
    moved, hh_before, hh_all, z_all, loss, told, *out_got = tie(
        moved, hh_before, hh_all, z_all, loss, told, *out_got
    )
    out_sum = out_parts[0].astype(F32)
    for part in out_got:
        out_sum = out_sum + part.astype(F32)

    moved = moved.reshape(n_mp + 3, own_total, 2 * units)
    crossed = swap(moved[n_mp // 2 : n_mp], "mp", n_mp, 1)
    crossed, out_low_sum = tie(crossed, out_sum.astype(BF16))
    g_out = lax.all_gather(out_low_sum, "batch").reshape(H, vocab_part)
    back_own = moved[n_mp:]
    arrived = [
        swap(
            jnp.concatenate([moved[spot : spot + 1], crossed[spot : spot + 1], back_own], axis=0),
            "mp",
            n_mp,
            2 * spot,
        )
        for spot in range(1, n_mp // 2)
    ]
    moved = jnp.stack(
        [moved[0]] + [part[0] for part in arrived] + [crossed[0]] + [part[1] for part in arrived]
    )
    back_all = both_halves(jnp.stack([back_own] + [part[2:] for part in arrived]))
    dx_part = moved[:, :, units:].reshape(total, emb_part)

    nh_part = NH // n_mp
    hyp_rows = emb_part + units + 2 * nh_part
    hyp_quarter = hyp_rows // n_batch

    def own_columns(values, size):
        return lax.dynamic_slice_in_dim(values, my * size, size, values.ndim - 1)

    dq_rows = jnp.concatenate([back_all[:, 0], back_all[:, 1]], axis=2).reshape(total, 4 * NH)
    dz_rows = back_all[:, 2, :, : 3 * Z].reshape(total, 3 * Z)
    hh_left = own_columns(hh_before, nh_part).reshape(total, nh_part)
    hh_own = own_columns(hh_all, nh_part).reshape(total, nh_part)
    g_small = [
        dot_first(left.reshape(total, emb_part + units), dq_rows),
        dot_first(hh_left, dq_rows),
        jnp.pad(dot_first(hh_own, dz_rows), ((0, 0), (0, 4 * NH - 3 * Z))),
    ]
    g_small = [g_small[0][:emb_part], g_small[0][emb_part:], g_small[1], g_small[2]]

    def small_quarter(bits):
        return jnp.concatenate([quarter_of(g, bits, g.shape[0] // n_batch) for g in g_small], axis=0)

    hyp_got, dx_got = [], [dx_part]
    for bits in (1, 2, 3):
        part = small_quarter(bits).astype(BF16).reshape(-1, emb_part)
        got = swap(jnp.concatenate([dx_part, part], axis=0), "batch", n_batch, bits)
        dx_got.append(got)
        hyp_got.append(got[total:].reshape(hyp_quarter, 4 * NH))
    hyp_sum = small_quarter(0)
    for got in hyp_got:
        hyp_sum = hyp_sum + got.astype(F32)
    hyp_all = lax.all_gather(hyp_sum.astype(BF16), ("batch", "mp"))
    hyp_all = hyp_all.reshape(n_batch, n_mp, hyp_quarter, 4 * NH)

    dux, duh, d0, d1, da, gv = run_column_backward(moved, back_all, vec, column[:9], steps)
    x_rows = x_rows.reshape(total, E)
    h_before = h_before.reshape(total, H)
    z_rows = z_all[:, :, :, : 3 * Z].reshape(total, 3, Z)
    g_parts = [dot_first(x_rows, dux.reshape(total, width)), dot_first(h_before, duh.reshape(total, width))] + [
        dot_first(z_rows[:, k], d.reshape(total, width)) for k, d in enumerate((d0, d1, da))
    ]

    def main_quarter(bits):
        return jnp.concatenate(
            [quarter_of(part, bits, part.shape[0] // n_batch) for part in g_parts], axis=0
        )

    main_got = [swap(main_quarter(bits).astype(BF16), "batch", n_batch, bits) for bits in (1, 2, 3)]

    me = b.reshape(1)
    g_embed, embed_rows, embed_cols = run_table(me, told, dx_got, embed.shape[0])

    g_embed, embed_rows, embed_cols, *main_got = tie(g_embed, embed_rows, embed_cols, *main_got)
    main_sum = main_quarter(0)
    for got in main_got:
        main_sum = main_sum + got.astype(F32)
    main_low = main_sum.astype(BF16)
    main_pieces = [main_low] + to_partners(main_low)
    main_seen = main_low.astype(F32)
    sq_main = main_seen * main_seen + EPS_FACT
    in_quarter = (E + H) // n_batch
    scale_quarter = Z // n_batch

    out_seen = g_out.astype(F32)
    sq_out = out_seen * out_seen + EPS_FACT

    by_rows = tree_sum(
        jnp.concatenate(
            [
                embed_rows.reshape(-1),
                jnp.sum(sq_out, axis=1),
                jnp.sum(sq_main, axis=1),
                loss[None],
            ]
        ),
        "mp",
        n_mp,
    )
    row_embed = by_rows[: embed.shape[0]]
    row_out = by_rows[embed.shape[0] : embed.shape[0] + H]
    sums = jnp.sum(back_all.astype(F32), axis=2)[from_slots]
    sums = jnp.sum(sums, axis=0).reshape(-1)[: 4 * NH + 3 * Z]
    fields = [
        by_rows[embed.shape[0] + H : -1],
        by_rows[-1:],
        jnp.sum(sq_main[:in_quarter], axis=0),
        jnp.sum(sq_main[in_quarter:].reshape(3, scale_quarter, width), axis=1).reshape(-1),
        gv.reshape(-1),
        sums,
    ]
    sizes = [field.shape[0] for field in fields]
    mixed = jnp.concatenate(fields)
    mixed = jnp.stack([mixed, swap(mixed, "batch", n_batch, 1)])
    mixed = placed(list(mixed) + list(swap(mixed, "batch", n_batch, 2)), b)
    rows_four = mixed[:, : sizes[0]]
    added = jnp.sum(mixed[:, sizes[0] :], axis=0)
    ends = [sum(sizes[1 : k + 1]) for k in range(len(sizes))]
    loss_sum, col_main, col_scale, g_vec, bias_sums = [
        added[ends[k] : ends[k + 1]] for k in range(len(sizes) - 1)
    ]
    row_in = rows_four[:, : E // n_batch].reshape(E)
    row_rec = rows_four[:, E // n_batch : in_quarter].reshape(H)
    row_scale = rows_four[:, in_quarter:].reshape(n_batch, 3, scale_quarter)
    row_scale = jnp.moveaxis(row_scale, 0, 1).reshape(3, Z)
    g_vec = g_vec.reshape(2, 4, units)

    (
        embed_row, embed_col, main_row, main_col, scale_row, scale_col, hyper_row, hyper_col,
        zproj_row, zproj_col, out_row, out_col, vector_state,
    ) = states
    decay = 1.0 - STEP ** (-0.8)

    def moving(old, mean):
        return decay * old + (1.0 - decay) * mean

    def across(values):
        return jnp.broadcast_to(values[:, None], (values.shape[0], LANES))

    res_embed = adafactor(
        embed, g_embed, embed_row, embed_col, row_embed / E, embed_cols[0] / embed.shape[0], 0, 1.0
    )
    new_out_row = moving(out_row, row_out / V)
    new_out_col = moving(out_col, jnp.mean(sq_out, axis=0))
    g_out, new_out = run_out_update(
        g_out,
        w_out,
        across(new_out_row / jnp.mean(new_out_row)),
        new_out_col[None],
        3.0 / math.sqrt(H),
    )
    g_hyper, new_hyper, hyper_rows, new_hyper_col = run_hyper_update(
        hyp_all,
        bias_sums[None, : 4 * NH],
        w_hyper,
        across(hyper_row),
        hyper_col[None],
        1.0 / math.sqrt(E + H + NH + 1),
    )
    new_embed, new_out, new_hyper, *main_pieces = tie(res_embed[1], new_out, new_hyper, *main_pieces)
    res_embed = (res_embed[0], new_embed) + res_embed[2:]
    scale_parts = placed([piece[in_quarter:] for piece in main_pieces], b)
    g_scale = jnp.moveaxis(scale_parts.reshape(n_batch, 3, scale_quarter, width), 0, 1)
    g_scale = g_scale.reshape(3, Z, 4, units).astype(F32)
    new_main_row = moving(main_row, jnp.concatenate([row_in, row_rec]) / (4 * H))
    new_main_col = moving(main_col, col_main.reshape(4, units) / (E + H))
    g_main, new_main = run_main_update(
        me,
        main_pieces,
        w_main,
        across(new_main_row / jnp.mean(new_main_row)),
        new_main_col,
        1.0 / math.sqrt(E),
    )
    res_scale = adafactor(
        w_scale,
        g_scale,
        scale_row,
        scale_col,
        row_scale / (4 * H),
        col_scale.reshape(3, 4, units) / Z,
        1,
        1.0 / math.sqrt(Z),
    )
    zproj_parts = hyp_all[:, :, hyp_quarter - nh_part // n_batch :, : 3 * Z]
    zproj_parts = zproj_parts.transpose(1, 0, 2, 3).reshape(NH, 3 * Z)
    g_zproj = jnp.concatenate([zproj_parts.astype(F32), bias_sums[None, 4 * NH :]], axis=0)
    sq_zproj = g_zproj * g_zproj + EPS_FACT
    res_zproj = adafactor(
        w_zproj,
        g_zproj,
        zproj_row,
        zproj_col,
        jnp.mean(sq_zproj, axis=1),
        jnp.mean(sq_zproj, axis=0),
        0,
        2.0 / math.sqrt(NH),
    )
    state_new = moving(vector_state, g_vec * g_vec + EPS_FACT)
    return (
        (loss_sum[0], count)
        + res_embed
        + (g_main, new_main, new_main_row, new_main_col)
        + res_scale
        + (g_hyper, new_hyper, hyper_rows[:, 0], new_hyper_col[0])
        + res_zproj
        + (g_out, new_out, new_out_row, new_out_col)
        + (g_vec, state_new, main_vectors - 0.1 * g_vec * lax.rsqrt(state_new))
    )


def per_device(
    parts,
    token_ids,
    seq_lengths,
    valid_mask,
    embed,
    w_main,
    w_scale,
    w_hyper,
    w_zproj,
    w_out,
    main_vectors,
    *states,
):
    n_mp, n_batch = parts
    my = lax.axis_index("mp")
    units = w_main.shape[2]
    emb_part = embed.shape[1]
    vocab_part = w_out.shape[1]
    batch_rows, steps = valid_mask.shape
    own = batch_rows // n_mp
    padded = -(-own // ROW_TILE) * ROW_TILE
    own_total = steps * own
    total = batch_rows * steps
    wide = units % LANES == 0

    def by_owner(values):
        return values.reshape(n_mp, own, steps).transpose(0, 2, 1)

    ids = by_owner(token_ids[:, :steps]).reshape(total)
    targets = by_owner(token_ids[:, 1:]).reshape(total)
    positions = jnp.arange(steps, dtype=jnp.int32)
    valid = valid_mask.astype(F32) * (positions[None, :] < seq_lengths[:, None]).astype(F32)
    weight_rows = by_owner(valid).reshape(total)
    count = tree_sum(jnp.sum(weight_rows), "batch", n_batch)

    def to_kernel(stacked):
        if wide:
            return stacked
        rows = stacked.shape[1]
        apart = stacked.reshape(n_mp, rows, 4, units).transpose(1, 2, 0, 3)
        return apart.reshape(1, rows, 4 * H)

    def pad_rows(values):
        return jnp.pad(values, ((0, 0), (0, padded - own), (0, 0))) if padded > own else values

    def unpad(values):
        return values[:, :own] if padded > own else values

    x_part = embed[ids].astype(BF16)
    main_own = w_main.astype(BF16).reshape(E + H, 4 * units)
    tail_own = weight_tail(w_scale, main_vectors)
    scale_own = tail_own[: 3 * Z]
    x_own = lax.all_to_all(x_part.reshape(n_mp, own_total, emb_part), "mp", 0, 0)
    x_own = x_own.transpose(1, 0, 2).reshape(steps, own, E)
    pieces = [to_kernel(lax.all_gather(jnp.concatenate([main_own, tail_own], axis=0), "mp"))]
    blocks = (pieces[0].shape[0], pieces[0].shape[2])
    x_all = lax.all_gather(x_part, "mp", axis=1, tiled=True)
    hyp_low = w_hyper.astype(BF16)
    zp_wide = jnp.pad(w_zproj, ((0, 0), (0, Z))).astype(BF16)
    out_low = w_out.astype(BF16)
    hyp_bias = hyp_low[E + H + NH :].astype(F32)
    zp_bias = zp_wide[NH:].astype(F32)

    pack, *kept = run_forward(
        pad_rows(x_own).reshape(steps * padded, E),
        blocks, None, pieces, hyp_low, hyp_bias, zp_wide[:NH], zp_bias, steps,
    )

    small_own = unpad(pack)[:, :, : H + NH + 3 * Z]
    rows_all = lax.all_gather(small_own.reshape(own_total, H + NH + 3 * Z), "mp")
    h_rows = rows_all[:, :, :H].reshape(total, H)
    logits = matmul(h_rows, out_low)
    local_target = targets - my * vocab_part
    hit = jnp.arange(vocab_part, dtype=jnp.int32)[None, :] == local_target[:, None]
    top = jnp.max(logits, axis=1)
    stats = jnp.stack(
        [
            top,
            jnp.sum(jnp.exp(logits - top[:, None]), axis=1),
            jnp.sum(jnp.where(hit, logits, 0.0), axis=1),
        ]
    )
    stats = lax.all_gather(stats, "mp")
    top_all = jnp.max(stats[:, 0], axis=0)
    exp_sum = jnp.sum(stats[:, 1] * jnp.exp(stats[:, 0] - top_all), axis=0)
    log_total = top_all + jnp.log(exp_sum)
    picked = jnp.sum(stats[:, 2], axis=0)
    loss_sum = tree_sum(jnp.sum((log_total - picked) * weight_rows), "batch", n_batch)
    grad_logits = (
        (jnp.exp(logits - log_total[:, None]) - hit.astype(F32)) * (weight_rows / count)[:, None]
    ).astype(BF16)
    dh_part = dot_last(grad_logits, out_low).reshape(n_mp, own_total, H)
    dh_parts = lax.all_to_all(dh_part.astype(BF16), "mp", 0, 0)
    dh_top = jnp.sum(dh_parts.astype(F32), axis=0)
    dh_top = dh_top.reshape(steps, own, H)
    g_out = dot_first(h_rows, grad_logits).astype(BF16)
    dh_top, g_out = lax.optimization_barrier((dh_top, g_out))
    g_out = lax.psum(g_out, "batch").astype(F32)

    dsda, dx_own, gv = run_backward(
        pad_rows(dh_top), blocks, None, run_turn(blocks, None, pieces), hyp_low, zp_wide[:NH], kept
    )
    nb = blocks[0]
    back = jnp.concatenate([dsda[nb + k, :, :, : 2 * NH] for k in range(3)], axis=2)
    dsda = dsda[:nb]

    if wide:
        dsda = unpad(dsda.reshape(n_mp * steps, padded, 8 * units))
    else:
        dsda = unpad(dsda.reshape(steps, padded, 8 * H)).reshape(own_total, 8, n_mp, units)
        dsda = dsda.transpose(2, 0, 1, 3)
    dsda = dsda.reshape(n_mp, own_total, 8 * units)
    dx_send = unpad(dx_own.reshape(steps, padded, E)).reshape(own_total, n_mp, emb_part)
    sent = jnp.concatenate([dsda, dx_send.transpose(1, 0, 2)], axis=2)
    sent = lax.all_to_all(sent, "mp", 0, 0).reshape(total, 8 * units + emb_part)
    ds = sent[:, : 4 * units].astype(F32)
    da_low = sent[:, 4 * units : 8 * units]
    dx_part = sent[:, 8 * units :]
    back_own = unpad(back)[:, :, : 4 * NH + 3 * Z]
    back_all = lax.all_gather(back_own.reshape(own_total, 4 * NH + 3 * Z), "mp")
    back_all = back_all.reshape(total, 4 * NH + 3 * Z)
    dq_all = back_all[:, : 4 * NH]
    dz_all = back_all[:, 4 * NH :]

    before = jnp.concatenate(
        [jnp.zeros_like(rows_all[:, :own]), rows_all[:, : own_total - own]], axis=1
    ).reshape(total, H + NH + 3 * Z)
    h_before = before[:, :H]
    hh_before = before[:, H : H + NH]
    hh_rows = rows_all[:, :, H : H + NH].reshape(total, NH)
    z_rows = rows_all[:, :, H + NH :].reshape(total, 3, Z)
    uh = matmul(h_before, main_own[E:])
    ux = matmul(x_all, main_own[:E])
    scale_blocks = scale_own.reshape(3, Z, 4 * units)
    one0 = 1.0 + matmul(z_rows[:, 0], scale_blocks[0])
    one1 = 1.0 + matmul(z_rows[:, 1], scale_blocks[1])
    g_in = dot_first(x_all, (ds * one1).astype(BF16))
    g_rec = dot_first(h_before, (ds * one0).astype(BF16))
    d_scales = [(ds * uh).astype(BF16), (ds * ux).astype(BF16), da_low]
    g_scale = jnp.stack([dot_first(z_rows[:, k], d_scales[k]) for k in range(3)])
    nh_part = NH // n_mp
    left = jnp.concatenate(
        [
            x_part,
            lax.dynamic_slice_in_dim(h_before, my * units, units, 1),
            lax.dynamic_slice_in_dim(hh_before, my * nh_part, nh_part, 1),
        ],
        axis=1,
    )
    g_hyper = dot_first(left, dq_all)
    g_zproj = dot_first(lax.dynamic_slice_in_dim(hh_rows, my * nh_part, nh_part, 1), dz_all)

    dx_all = lax.all_gather(dx_part, "batch").reshape(n_batch * total, emb_part)
    ids_all = lax.all_gather(ids, "batch").reshape(n_batch * total)
    g_embed = jax.ops.segment_sum(dx_all.astype(F32), ids_all, num_segments=embed.shape[0])
    g_in, g_rec, g_scale, g_hyper, g_zproj = lax.psum(
        tuple(g.astype(BF16) for g in (g_in, g_rec, g_scale, g_hyper, g_zproj)), "batch"
    )
    flat = lax.all_gather(
        jnp.concatenate([g_hyper.reshape(-1, LANES), g_zproj.reshape(-1, LANES)], axis=0), "mp"
    ).astype(F32)
    n_hyp = g_hyper.size // LANES
    all_hyper = flat[:, :n_hyp].reshape(n_mp, emb_part + units + nh_part, 4 * NH)
    all_zproj = flat[:, n_hyp:].reshape(n_mp * nh_part, 3 * Z)
    if wide:
        gv_parts = gv.reshape(n_mp, 2, 4, units)
    else:
        gv_parts = gv.reshape(2, 4, n_mp, units).transpose(2, 0, 1, 3)
    gv_parts, bias_sums = lax.psum(
        (gv_parts, jnp.sum(back_own.astype(F32), axis=(0, 1))), ("batch", "mp")
    )
    g_vec = lax.dynamic_index_in_dim(gv_parts, my, 0, False)
    g_hyper = jnp.concatenate(
        [
            all_hyper[:, :emb_part].reshape(E, 4 * NH),
            all_hyper[:, emb_part : emb_part + units].reshape(H, 4 * NH),
            all_hyper[:, emb_part + units :].reshape(NH, 4 * NH),
            bias_sums[None, : 4 * NH],
        ],
        axis=0,
    )
    g_zproj = jnp.concatenate([all_zproj, bias_sums[None, 4 * NH :]], axis=0)
    g_main = jnp.concatenate([g_in, g_rec], axis=0).astype(F32).reshape(E + H, 4, units)
    g_scale = g_scale.astype(F32).reshape(3, Z, 4, units)

    sq_embed = g_embed * g_embed + EPS_FACT
    sq_main = g_main * g_main + EPS_FACT
    sq_scale = g_scale * g_scale + EPS_FACT
    sq_out = g_out * g_out + EPS_FACT
    row_out = lax.psum(jnp.sum(sq_out, axis=1), "mp")
    row_embed, row_main, row_scale = lax.psum(
        (
            jnp.sum(sq_embed, axis=1),
            jnp.sum(sq_main, axis=(1, 2)),
            jnp.sum(sq_scale, axis=(2, 3)),
        ),
        "mp",
    )
    return (loss_sum, count) + updates(
        (embed, w_main, w_scale, w_hyper, w_zproj, w_out, main_vectors),
        states,
        (g_embed, g_main, g_scale, g_hyper, g_zproj, g_out, g_vec),
        (row_embed, row_main, row_scale, row_out),
        jnp.mean(sq_embed, axis=0),
    )


def solution(mesh):
    rep = P()
    placed = (
        P("batch", None),
        P("batch"),
        P("batch", None),
        P(None, "mp"),
        P(None, None, "mp"),
        P(None, None, None, "mp"),
        rep,
        rep,
        P(None, "mp"),
        P(None, None, "mp"),
        rep,
        P("mp"),
        rep,
        P(None, "mp"),
        rep,
        P(None, None, "mp"),
        rep,
        rep,
        rep,
        rep,
        rep,
        P("mp"),
        P(None, None, "mp"),
    )
    parts = (mesh.shape["mp"], mesh.shape["batch"])
    body = per_chip if parts == (8, 4) else per_device
    return jax.shard_map(
        functools.partial(body, parts),
        mesh=mesh,
        in_specs=placed,
        out_specs=(
            rep,
            rep,
            P(None, "mp"),
            P(None, "mp"),
            rep,
            P("mp"),
            P(None, None, "mp"),
            P(None, None, "mp"),
            rep,
            P(None, "mp"),
            P(None, None, None, "mp"),
            P(None, None, None, "mp"),
            rep,
            P(None, None, "mp"),
            rep,
            rep,
            rep,
            rep,
            rep,
            rep,
            rep,
            rep,
            P(None, "mp"),
            P(None, "mp"),
            rep,
            P("mp"),
            P(None, None, "mp"),
            P(None, None, "mp"),
            P(None, None, "mp"),
        ),
        check_vma=False,
    )
```

```python
import functools
import math

import jax
import jax.numpy as jnp
from jax import lax
from jax.experimental import pallas as pl
from jax.experimental.pallas import tpu as pltpu
from jax.sharding import PartitionSpec as P

E = 1024
H = 1024
V = 10240
NH = 128
Z = 64
STEP = 10
LANES = 128
ROW_TILE = 16
VMEM_BYTES = 56 * 1024 * 1024

EPS_NORM = 1e-05
EPS_FACT = 1e-30

F32 = jnp.float32
BF16 = jnp.bfloat16


def matmul(left, right):
    return jnp.dot(left, right, preferred_element_type=F32)


def dot_last(left, right):
    return lax.dot_general(left, right, (((1,), (1,)), ((), ())), preferred_element_type=F32)


def dot_first(left, right):
    return lax.dot_general(left, right, (((0,), (0,)), ((), ())), preferred_element_type=F32)


def adafactor(weight, grad, row_old, col_old, row_mean, col_mean, lead, rate):
    decay = 1.0 - STEP ** (-0.8)
    row_new = decay * row_old + (1.0 - decay) * row_mean
    col_new = decay * col_old + (1.0 - decay) * col_mean
    relative = row_new / jnp.mean(row_new, axis=-1, keepdims=True)
    relative = relative.reshape(relative.shape + (1,) * (grad.ndim - relative.ndim))
    spread = col_new[None] if lead == 0 else col_new[:, None]
    updated = weight - rate * grad * lax.rsqrt(relative * spread)
    return (grad, updated, row_new, col_new)


STACK_ROWS = 2304
SCALE_AT = 2 * E
VEC_AT = SCALE_AT + 3 * Z
TAIL_ROWS = STACK_ROWS - SCALE_AT
PACK = H + NH + 4 * Z
STAT_AT = 3 * Z
VOCAB_BLOCK = 256
SLOTS = (0, 2, 4, 6, 1, 3, 5, 7)


def swap(values, axis, size, bit):
    return lax.ppermute(values, axis, [(i, i ^ bit) for i in range(size)])


def tree_sum(values, axis, size):
    if size & (size - 1):
        return lax.psum(values, axis)
    bit = 1
    while bit < size:
        values = values + swap(values, axis, size, bit)
        bit *= 2
    return values


def tie(*values):
    return lax.optimization_barrier(values)


def weight_tail(w_scale, main_vectors):
    width = 4 * main_vectors.shape[2]
    vec = main_vectors.reshape(2, width)
    terms = []
    for _ in range(3):
        term = lax.reduce_precision(vec, 8, 7)
        terms.append(term.astype(BF16))
        vec = vec - term
    return jnp.concatenate(
        [w_scale.astype(BF16).reshape(3 * Z, width)]
        + terms
        + [jnp.zeros((STACK_ROWS - VEC_AT - 6, width), BF16)],
        axis=0,
    )


def piece_copies(refs, plan, main_v, sem, only=None):
    if plan is None:
        return [] if only else [(True, lambda: pltpu.make_async_copy(refs[0], main_v, sem.at[0]))]
    me = lax.axis_index("mp")
    b = lax.axis_index("batch")
    quarter = SCALE_AT // 4
    tail_quarter = TAIL_ROWS // 4
    copies = []

    def add(early, bits, ref, source, target, rows, spot):
        def copy():
            return pltpu.make_async_copy(
                ref.at[pl.ds(source, rows)],
                main_v.at[me ^ bits, pl.ds(target, rows)],
                sem.at[spot],
            )

        copies.append((early, copy))

    for number, (ref, (bits, over, first, rows)) in enumerate(zip(refs, plan)):
        if only is not None and bits != only:
            continue
        spot = 2 * number
        if over is None and rows == SCALE_AT:
            add(True, bits, ref, 0, 0, E, spot)
            add(False, bits, ref, E, E, H, spot + 1)
            continue
        if over is None:
            add(True, bits, ref, 0, first, rows, spot)
            continue
        index = b ^ over
        of_main = max(0, min(rows, quarter - first))
        if of_main:
            start = pl.multiple_of(index * quarter + first, ROW_TILE)
            add(index < 2, bits, ref, 0, start, of_main, spot)
        if rows > of_main:
            start = SCALE_AT + index * tail_quarter + first + of_main - quarter
            add(True, bits, ref, of_main, pl.multiple_of(start, ROW_TILE), rows - of_main, spot + 1)
    return copies


def each_copy(copies, early, act):
    for needed, copy in copies:
        if isinstance(needed, bool):
            if needed == early:
                act(copy())
        else:

            @pl.when(needed if early else jnp.logical_not(needed))
            def _():
                act(copy())


def copy_count(plan):
    return 1 if plan is None else 2 * len(plan)


def load_vectors(vec_ref, main_v):
    for m in range(main_v.shape[0]):
        terms = main_v[m, VEC_AT : VEC_AT + ROW_TILE].astype(F32)
        vec_ref[m] = terms[0:2] + terms[2:4] + terms[4:6]


def masked_thirds(z_wide):
    lane = lax.broadcasted_iota(jnp.int32, z_wide.shape, 1) // Z
    zero = jnp.zeros_like(z_wide)
    return jnp.concatenate([jnp.where(lane == k, z_wide, zero) for k in range(3)], axis=0)


def beside(wide, columns):
    lane = lax.broadcasted_iota(jnp.int32, wide.shape, 1)
    count = len(columns)
    for spot, column in enumerate(columns):
        high = column.astype(BF16).astype(F32)
        wide = jnp.where(lane == STAT_AT + spot, high, wide)
        wide = jnp.where(lane == STAT_AT + count + spot, column - high, wide)
    return wide.astype(BF16)


def column_of(wide, count, spot):
    return wide[:, STAT_AT + spot : STAT_AT + spot + 1] + wide[
        :, STAT_AT + count + spot : STAT_AT + count + spot + 1
    ]


def forward_kernel(plan, x_ref, hyp_ref, hypb_ref, zp_ref, zpb_ref, *refs):
    n_pieces = 1 if plan is None else len(plan)
    forward_body(plan, x_ref, hyp_ref, hypb_ref, zp_ref, zpb_ref, refs[:n_pieces], *refs[n_pieces:])


def forward_body(
    plan, x_ref, hyp_ref, hypb_ref, zp_ref, zpb_ref, piece_refs,
    pack_out, cprev_out, tc_out, hcprev_out, thc_out, hg_out,
    ux_out, uh_out, one0_out, one1_out, n_out, act_out, rstd_out, vec_out,
    main_v, prex_s, h_s, c_s, hh_s, hc_s, sem,
):
    t = pl.program_id(0)
    nb, _, bw = main_v.shape
    bu = bw // 4
    steps, _, rows, _ = ux_out.shape

    @pl.when(t == 0)
    def _():
        pieces = piece_copies(piece_refs, plan, main_v, sem)
        for early in (True, False):
            each_copy(pieces, early, lambda copy: copy.start())
        prex_s[...] = (matmul(x_ref[...], hyp_ref[:E]) + hypb_ref[...]).reshape(steps, rows, 4 * NH)
        h_s[...] = jnp.zeros_like(h_s)
        c_s[...] = jnp.zeros_like(c_s)
        hh_s[...] = jnp.zeros_like(hh_s)
        hc_s[...] = jnp.zeros_like(hc_s)
        me = 0 if plan is None else lax.axis_index("mp")
        for bits in range(nb):
            each_copy(piece_copies(piece_refs, plan, main_v, sem, bits), True, lambda copy: copy.wait())
            m = me ^ bits
            ux = matmul(x_ref[...], main_v[m, :E])
            ux_out[:, m] = ux.reshape(steps, rows, bw)
        load_vectors(vec_out, main_v)
        uh_out[...] = jnp.zeros_like(uh_out)

    @pl.when(t == 1)
    def _():
        each_copy(piece_copies(piece_refs, plan, main_v, sem), False, lambda copy: copy.wait())

    h_prev = h_s[...]

    @pl.when(t > 0)
    def _():
        for m in range(nb):
            uh_out[0, m] = matmul(h_prev, main_v[m, E : 2 * E])

    hh_prev = hh_s[...]
    hc_prev = hc_s[...]
    q = prex_s[t] + matmul(h_prev, hyp_ref[E : E + H]) + matmul(hh_prev, hyp_ref[E + H : E + H + NH])
    q_in = jax.nn.sigmoid(q[:, :NH])
    q_forget = jax.nn.sigmoid(q[:, NH : 2 * NH])
    q_out = jax.nn.sigmoid(q[:, 2 * NH : 3 * NH])
    q_cell = jnp.tanh(q[:, 3 * NH :])
    hc = q_forget * hc_prev + q_in * q_cell
    thc = jnp.tanh(hc)
    hh = (q_out * thc).astype(BF16)
    z_wide = matmul(hh, zp_ref[...]) + zpb_ref[...]
    hcprev_out[0] = hc_prev
    thc_out[0] = thc
    hg_out[0, :, :NH] = q_in
    hg_out[0, :, NH : 2 * NH] = q_forget
    hg_out[0, :, 2 * NH : 3 * NH] = q_out
    hg_out[0, :, 3 * NH :] = q_cell
    pack_out[0, :, H : H + NH] = hh
    hh_s[...] = hh
    hc_s[...] = hc

    thirds = masked_thirds(z_wide.astype(BF16))
    sums = [jnp.zeros((rows, LANES), F32) for _ in range(4)]
    squares = [jnp.zeros((rows, LANES), F32) for _ in range(4)]
    for m in range(nb):
        scl = matmul(thirds, main_v[m, SCALE_AT:])
        uh = uh_out[0, m]
        one0 = 1.0 + scl[:rows]
        one1 = 1.0 + scl[rows : 2 * rows]
        s = one0 * uh + one1 * ux_out[t, m]
        one0_out[0, m] = one0
        one1_out[0, m] = one1
        act_out[0, m] = scl[2 * rows :]
        n_out[0, m] = s
        for g in range(4):
            for j in range(bu // LANES):
                piece = s[:, g * bu + j * LANES : g * bu + (j + 1) * LANES]
                sums[g] += piece
                squares[g] += piece * piece
    centres, rstds = [], []
    for g in range(4):
        centre = jnp.sum(sums[g], axis=1, keepdims=True) / H
        square = jnp.sum(squares[g], axis=1, keepdims=True) / H
        rstd = lax.rsqrt(square - centre * centre + EPS_NORM)
        centres.append(centre)
        rstds.append(rstd)
        rstd_out[0, :, g * LANES : (g + 1) * LANES] = jnp.broadcast_to(rstd, (rows, LANES))
    pack_out[0, :, H + NH :] = beside(z_wide, centres + rstds)

    for m in range(nb):
        cols = slice(m * bu, (m + 1) * bu)
        gates = []
        for g in range(4):
            here = slice(g * bu, (g + 1) * bu)
            n = (n_out[0, m, :, here] - centres[g]) * rstds[g]
            n_out[0, m, :, here] = n
            pre = vec_out[m, 0:1, here] * n + vec_out[m, 1:2, here] + act_out[0, m, :, here]
            gate = jnp.tanh(pre) if g == 3 else jax.nn.sigmoid(pre)
            act_out[0, m, :, here] = gate
            gates.append(gate)
        c_prev = c_s[:, cols]
        c_now = gates[1] * c_prev + gates[0] * gates[3]
        tc = jnp.tanh(c_now)
        h_now = (gates[2] * tc).astype(BF16)
        cprev_out[0, :, cols] = c_prev
        tc_out[0, :, cols] = tc
        c_s[:, cols] = c_now
        h_s[:, cols] = h_now
        pack_out[0, :, cols] = h_now


def turn_kernel(plan, me_ref, *refs):
    n_pieces = 1 if plan is None else len(plan)
    in_out, rec_out, tail_out, main_v, sem = refs[n_pieces:]
    step = pl.program_id(0)

    @pl.when(step == 0)
    def _():
        for _, copy in piece_copies(refs[:n_pieces], plan, main_v, sem):
            copy().start()

    for bits in range(main_v.shape[0]):

        @pl.when(step == bits)
        def _():
            for _, copy in piece_copies(refs[:n_pieces], plan, main_v, sem, bits):
                copy().wait()

    m = step ^ me_ref[0]
    in_out[0] = main_v[m, :E]
    rec_out[0] = main_v[m, E : 2 * E].T
    tail_out[0] = main_v[m, SCALE_AT:].T


def run_turn(blocks, plan, pieces):
    nb, bw = blocks
    me = jnp.zeros((1,), jnp.int32) if plan is None else lax.axis_index("mp").reshape(1)
    shapes = [(E, bw), (bw, H), (bw, TAIL_ROWS)]
    single = dict(pipeline_mode=pl.Buffered(1)) if nb == 1 else {}
    return pl.pallas_call(
        functools.partial(turn_kernel, plan),
        grid_spec=pltpu.PrefetchScalarGridSpec(
            num_scalar_prefetch=1,
            grid=(nb,),
            in_specs=[pl.BlockSpec(memory_space=pl.ANY)] * len(pieces),
            out_specs=[
                pl.BlockSpec((1,) + shape, lambda i, me: (i ^ me[0], 0, 0), **single) for shape in shapes
            ],
            scratch_shapes=[
                pltpu.VMEM((nb, STACK_ROWS, bw), BF16),
                pltpu.SemaphoreType.DMA((copy_count(plan),)),
            ],
        ),
        out_shape=[jax.ShapeDtypeStruct((nb,) + shape, BF16) for shape in shapes],
        compiler_params=kernel_params(),
        cost_estimate=pl.CostEstimate(flops=10**7, bytes_accessed=40_000_000, transcendentals=0),
        name="turn_weights",
    )(me, *pieces)


def backward_kernel(
    plan, in_hbm, rec_hbm, tail_hbm, dh_ref, hyp_ref, zp_ref,
    cprev_ref, tc_ref, hcprev_ref, thc_ref, hg_ref,
    ux_ref, uh_ref, one0_ref, one1_ref, n_ref, act_ref, rstd_ref, vec_ref,
    cols_out, odd_out, back_out, dx_out, gv_out,
    in_v, rec_v, tail_v, dh_s, dc_s, dhh_s, dhc_s, da_s, stack_s, dux_s, dq_s, sem,
):
    step = pl.program_id(0)
    nb, _, bw = in_v.shape
    bu = bw // 4
    steps, rows, _ = dq_s.shape
    t = steps - 1 - step
    me = 0 if plan is None else lax.axis_index("mp")

    def by_core(bits, keep):
        @pl.when(bits % 2 == 0)
        def _():
            keep(cols_out, bits // 2)

        @pl.when(bits % 2 == 1)
        def _():
            keep(odd_out, bits // 2)

    copies = [
        pltpu.make_async_copy(source, target, sem.at[spot])
        for spot, (source, target) in enumerate(((rec_hbm, rec_v), (tail_hbm, tail_v), (in_hbm, in_v)))
    ]

    @pl.when(step == 0)
    def _():
        for copy in copies:
            copy.start()
        dh_s[...] = jnp.zeros_like(dh_s)
        dc_s[...] = jnp.zeros_like(dc_s)
        dhh_s[...] = jnp.zeros_like(dhh_s)
        dhc_s[...] = jnp.zeros_like(dhc_s)
        gv_out[...] = jnp.zeros_like(gv_out)

    first = [jnp.zeros((rows, LANES), F32) for _ in range(4)]
    second = [jnp.zeros((rows, LANES), F32) for _ in range(4)]
    for m in range(nb):
        cols = slice(m * bu, (m + 1) * bu)
        gate = [act_ref[0, m, :, g * bu : (g + 1) * bu] for g in range(4)]
        tc = tc_ref[0, :, cols]
        dh = dh_ref[0, :, cols] + dh_s[:, cols]
        dc = dc_s[:, cols] + dh * gate[2] * (1.0 - tc * tc)
        da = [
            dc * gate[3] * gate[0] * (1.0 - gate[0]),
            dc * cprev_ref[0, :, cols] * gate[1] * (1.0 - gate[1]),
            dh * tc * gate[2] * (1.0 - gate[2]),
            dc * gate[0] * (1.0 - gate[3] * gate[3]),
        ]
        dc_s[:, cols] = dc * gate[1]
        if plan is not None:
            low = dh.astype(BF16)

            def keep_dh(ref, spot):
                ref[spot, t, :, :bu] = low

            by_core(me ^ m, keep_dh)
        for g in range(4):
            here = slice(g * bu, (g + 1) * bu)
            n = n_ref[0, m, :, here]
            da_s[m, :, here] = da[g]
            if plan is None:
                gv_out[m, 0:1, here] += jnp.sum(da[g] * n, axis=0, keepdims=True)
                gv_out[m, 1:2, here] += jnp.sum(da[g], axis=0, keepdims=True)
            dn = vec_ref[m, 0:1, here] * da[g]
            dnn = dn * n
            for j in range(bu // LANES):
                first[g] += dn[:, j * LANES : (j + 1) * LANES]
                second[g] += dnn[:, j * LANES : (j + 1) * LANES]
    means = [
        (jnp.sum(first[g], axis=1, keepdims=True) / H, jnp.sum(second[g], axis=1, keepdims=True) / H)
        for g in range(4)
    ]

    for m in range(nb):
        ds_parts = []
        for g in range(4):
            here = slice(g * bu, (g + 1) * bu)
            dn = vec_ref[m, 0:1, here] * da_s[m, :, here]
            rstd = rstd_ref[0, :, g * LANES : g * LANES + 1]
            ds_parts.append(rstd * (dn - means[g][0] - n_ref[0, m, :, here] * means[g][1]))
        ds = jnp.concatenate(ds_parts, axis=1)
        da_low = da_s[m].astype(BF16)
        if plan is None:
            cols_out[m, t, :, :bw] = ds.astype(BF16)
            cols_out[m, t, :, bw:] = da_low
        stack_s[m, :rows] = (ds * uh_ref[0, m]).astype(BF16)
        stack_s[m, rows : 2 * rows] = (ds * ux_ref[0, m]).astype(BF16)
        stack_s[m, 2 * rows : 3 * rows] = da_low
        stack_s[m, 3 * rows :] = (ds * one0_ref[0, m]).astype(BF16)
        dux_s[t, m] = (ds * one1_ref[0, m]).astype(BF16)

    @pl.when(step == 0)
    def _():
        copies[0].wait()
        copies[1].wait()

    dz_all = jnp.zeros((3 * rows, 4 * Z), F32)
    dh_rec = jnp.zeros((rows, H), F32)
    for m in range(nb):
        dz_all += matmul(stack_s[m, : 3 * rows], tail_v[m])
    for m in range(nb):
        dh_rec += matmul(stack_s[m, 3 * rows :], rec_v[m])

    lane = lax.broadcasted_iota(jnp.int32, (rows, 4 * Z), 1) // Z
    dz = jnp.zeros((rows, 4 * Z), F32)
    for k in range(3):
        dz = jnp.where(lane == k, dz_all[k * rows : (k + 1) * rows], dz)
    half = 2 * NH
    back_out[2, t] = beside(dz, [m[0] for m in means] + [m[1] for m in means])
    q_in = hg_ref[0, :, :NH]
    q_forget = hg_ref[0, :, NH : 2 * NH]
    q_out = hg_ref[0, :, 2 * NH : 3 * NH]
    q_cell = hg_ref[0, :, 3 * NH :]
    thc = thc_ref[0]
    dhh = dhh_s[...] + dot_last(dz.astype(BF16), zp_ref[...])
    dhc = dhc_s[...] + dhh * q_out * (1.0 - thc * thc)
    dq = jnp.concatenate(
        [
            dhc * q_cell * q_in * (1.0 - q_in),
            dhc * hcprev_ref[0] * q_forget * (1.0 - q_forget),
            dhh * thc * q_out * (1.0 - q_out),
            dhc * q_in * (1.0 - q_cell * q_cell),
        ],
        axis=1,
    ).astype(BF16)
    back_out[0, t] = dq[:, :half]
    back_out[1, t] = dq[:, half:]
    dq_s[t] = dq
    dhc_s[...] = dhc * q_forget
    dhh_s[...] = dot_last(dq, hyp_ref[E + H : E + H + NH])
    dh_s[...] = dh_rec + dot_last(dq, hyp_ref[E : E + H])

    @pl.when(step == steps - 1)
    def _():
        copies[2].wait()
        dx = dot_last(dq_s[...].reshape(steps * rows, 4 * NH), hyp_ref[:E])
        for m in range(nb):
            dx += dot_last(dux_s[:, m].reshape(steps * rows, bw), in_v[m])
        if plan is None:
            dx_out[...] = dx.astype(dx_out.dtype)
        else:
            for m in range(nb):
                part = dx[:, m * bu : (m + 1) * bu].astype(BF16).reshape(steps, rows, bu)

                def keep_dx(ref, spot):
                    ref[spot, :, :, bu : 2 * bu] = part

                by_core(me ^ m, keep_dx)


def whole(shape):
    return pl.BlockSpec(shape, lambda t: (0,) * len(shape), pipeline_mode=pl.Buffered(1))


def kernel_params():
    return pltpu.CompilerParams(vmem_limit_bytes=VMEM_BYTES)


def run_forward(x_rows, blocks, plan, pieces, hyp_low, hyp_bias, zp_wide, zp_bias, steps):
    nb, bw = blocks
    rows = x_rows.shape[0] // steps

    def stepped(*tail):
        return pl.BlockSpec((1,) + tail, lambda t: (t,) + (0,) * len(tail))

    tails = [
        (BF16, (rows, PACK)), (F32, (rows, H)), (F32, (rows, H)), (F32, (rows, NH)), (F32, (rows, NH)),
        (F32, (rows, 4 * NH)), (F32, (nb, rows, bw)), (F32, (nb, rows, bw)), (F32, (nb, rows, bw)),
        (F32, (nb, rows, bw)), (F32, (nb, rows, bw)), (F32, (nb, rows, bw)), (F32, (rows, 4 * LANES)),
    ]
    out_specs = [stepped(*tail) for _, tail in tails]
    out_specs[6] = pl.BlockSpec((steps, nb, rows, bw), lambda t: (0, 0, 0, 0))
    out_shape = [jax.ShapeDtypeStruct((steps,) + tail, dtype) for dtype, tail in tails]
    work = steps * rows * 4 * H * (2 * H + E + 3 * 4 * Z)
    return pl.pallas_call(
        functools.partial(forward_kernel, plan),
        grid=(steps,),
        in_specs=[
            whole(x_rows.shape),
            whole(hyp_low.shape),
            whole(hyp_bias.shape),
            whole(zp_wide.shape),
            whole(zp_bias.shape),
        ]
        + [pl.BlockSpec(memory_space=pl.ANY)] * len(pieces),
        out_specs=out_specs + [pl.BlockSpec((nb, 2, bw), lambda t: (0, 0, 0))],
        out_shape=out_shape + [jax.ShapeDtypeStruct((nb, 2, bw), F32)],
        scratch_shapes=[
            pltpu.VMEM((nb, STACK_ROWS, bw), BF16),
            pltpu.VMEM((steps, rows, 4 * NH), F32),
            pltpu.VMEM((rows, H), BF16),
            pltpu.VMEM((rows, H), F32),
            pltpu.VMEM((rows, NH), BF16),
            pltpu.VMEM((rows, NH), F32),
            pltpu.SemaphoreType.DMA((copy_count(plan),)),
        ],
        compiler_params=kernel_params(),
        cost_estimate=pl.CostEstimate(flops=2 * work, bytes_accessed=40_000_000, transcendentals=0),
        name="recurrence_forward",
    )(x_rows, hyp_low, hyp_bias, zp_wide, zp_bias, *pieces)


def run_backward(dh_top, blocks, plan, turned, hyp_low, zp_wide, kept):
    nb, bw = blocks
    steps, rows, _ = dh_top.shape

    def stepped(*tail):
        return pl.BlockSpec((1,) + tail, lambda s: (steps - 1 - s,) + (0,) * len(tail))

    def still(shape):
        return pl.BlockSpec(shape, lambda s: (0,) * len(shape))

    tails = [
        (rows, H), (rows, H), (rows, NH), (rows, NH), (rows, 4 * NH), (nb, rows, bw), (nb, rows, bw),
        (nb, rows, bw), (nb, rows, bw), (nb, rows, bw), (nb, rows, bw), (rows, 4 * LANES),
    ]
    per_owner = 2 * bw if plan is None else 2 * (bw // 4)
    outs = [
        jax.ShapeDtypeStruct((nb if plan is None else nb // 2, steps, rows, per_owner), BF16),
        jax.ShapeDtypeStruct((1 if plan is None else nb // 2, steps, rows, per_owner), BF16),
        jax.ShapeDtypeStruct((3, steps, rows, 2 * NH), BF16),
        jax.ShapeDtypeStruct((steps * rows, E), BF16),
        jax.ShapeDtypeStruct((nb, 2, bw), F32),
    ]
    work = steps * rows * 4 * H * (2 * H + E + 3 * 4 * Z)
    return pl.pallas_call(
        functools.partial(backward_kernel, plan),
        grid=(steps,),
        in_specs=[pl.BlockSpec(memory_space=pl.ANY)] * len(turned)
        + [stepped(rows, H), whole(hyp_low.shape), whole(zp_wide.shape)]
        + [stepped(*tail) for tail in tails]
        + [whole((nb, 2, bw))],
        out_specs=[
            still(out.shape) for out in outs
        ],
        out_shape=outs,
        scratch_shapes=[
            pltpu.VMEM((nb, E, bw), BF16),
            pltpu.VMEM((nb, bw, H), BF16),
            pltpu.VMEM((nb, bw, TAIL_ROWS), BF16),
            pltpu.VMEM((rows, H), F32),
            pltpu.VMEM((rows, H), F32),
            pltpu.VMEM((rows, NH), F32),
            pltpu.VMEM((rows, NH), F32),
            pltpu.VMEM((nb, rows, bw), F32),
            pltpu.VMEM((nb, 4 * rows, bw), BF16),
            pltpu.VMEM((steps, nb, rows, bw), BF16),
            pltpu.VMEM((steps, rows, 4 * NH), BF16),
            pltpu.SemaphoreType.DMA((3,)),
        ],
        compiler_params=kernel_params(),
        cost_estimate=pl.CostEstimate(flops=2 * work, bytes_accessed=60_000_000, transcendentals=0),
        name="recurrence_backward",
    )(*turned, dh_top, hyp_low, zp_wide, *kept)


def column_forward_kernel(
    steps, slots_ref, pack0_ref, pack1_ref, x0_ref, x1_ref, main_ref, tail_ref, vec_ref,
    uh_out, ux_out, one0_out, one1_out, n_out, act_out, cprev_out, tc_out, rstd_out,
    left_out, x_out, hb_out, hhb_out, hh_out, z_out,
):
    _, total, _ = pack0_ref.shape
    rows = total // steps
    width = main_ref.shape[1]
    units = width // 4

    def one_before(values):
        return jnp.concatenate([jnp.zeros_like(values[:rows]), values[: total - rows]], axis=0)

    for half, (pack_ref, x_ref) in enumerate(((pack0_ref, x0_ref), (pack1_ref, x1_ref))):
        h_before = one_before(pack_ref[0, :, :H])
        hh = pack_ref[0, :, H : H + NH]
        z_wide = pack_ref[0, :, H + NH :]
        x_now = jnp.concatenate([x_ref[k, 0] for k in range(x_ref.shape[0])], axis=1)
        mine = pl.ds(pl.multiple_of(slots_ref[0] * units, units), units)
        part = x_ref.shape[3]
        left_out[half, 0, :, :part] = x_ref[slots_ref[0], 0]
        left_out[half, 0, :, part:] = one_before(pack_ref[0, :, mine])
        x_out[half, 0] = x_now
        hb_out[half, 0] = h_before
        hhb_out[half, 0] = one_before(hh)
        hh_out[half, 0] = hh
        z_out[half, 0] = z_wide
        stats = z_wide.astype(F32)
        uh = matmul(h_before, main_ref[E : 2 * E])
        ux = matmul(x_now, main_ref[:E])
        scl = matmul(masked_thirds(z_wide), tail_ref[...])
        one0 = 1.0 + scl[:total]
        one1 = 1.0 + scl[total : 2 * total]
        s = one0 * uh + one1 * ux
        uh_out[half, 0] = uh
        ux_out[half, 0] = ux
        one0_out[half, 0] = one0
        one1_out[half, 0] = one1
        for g in range(4):
            here = slice(g * units, (g + 1) * units)
            rstd = column_of(stats, 8, 4 + g)
            n = (s[:, here] - column_of(stats, 8, g)) * rstd
            pre = vec_ref[0:1, here] * n + vec_ref[1:2, here] + scl[2 * total :, here]
            n_out[half, 0, :, here] = n
            act_out[half, 0, :, here] = jnp.tanh(pre) if g == 3 else jax.nn.sigmoid(pre)
            rstd_out[half, 0, :, here] = jnp.broadcast_to(rstd, (total, units))
        c = jnp.zeros((rows, units), F32)
        for t in range(steps):
            now = slice(t * rows, (t + 1) * rows)
            gate = [act_out[half, 0, now, g * units : (g + 1) * units] for g in range(4)]
            cprev_out[half, 0, now] = c
            c = gate[1] * c + gate[0] * gate[3]
            tc_out[half, 0, now] = jnp.tanh(c)


def column_backward_kernel(
    steps, dh0_ref, dh1_ref, back0_ref, back1_ref, vec_ref,
    uh_ref, ux_ref, one0_ref, one1_ref, n_ref, act_ref, cprev_ref, tc_ref, rstd_ref,
    dux_out, duh_out, d0_out, d1_out, da_out, gv_out,
    dc_s,
):
    _, total, units = dh0_ref.shape
    rows = total // steps

    @pl.when(pl.program_id(0) == 0)
    def _():
        gv_out[...] = jnp.zeros_like(gv_out)

    for half, (dh_ref, back_ref) in enumerate(((dh0_ref, back0_ref), (dh1_ref, back1_ref))):
        means = back_ref[0, 0].astype(F32)
        dh = dh_ref[0].astype(F32)
        gate = [act_ref[half, 0, :, g * units : (g + 1) * units] for g in range(4)]
        tc = tc_ref[half, 0]
        local = dh * gate[2] * (1.0 - tc * tc)
        dc = jnp.zeros((rows, units), F32)
        for t in reversed(range(steps)):
            now = slice(t * rows, (t + 1) * rows)
            dc = dc + local[now]
            dc_s[now] = dc
            dc = dc * gate[1][now]
        dc = dc_s[...]
        da = [
            dc * gate[3] * gate[0] * (1.0 - gate[0]),
            dc * cprev_ref[half, 0] * gate[1] * (1.0 - gate[1]),
            dh * tc * gate[2] * (1.0 - gate[2]),
            dc * gate[0] * (1.0 - gate[3] * gate[3]),
        ]
        for g in range(4):
            here = slice(g * units, (g + 1) * units)
            n = n_ref[half, 0, :, here]
            gv_out[0:1, here] += jnp.sum(da[g] * n, axis=0, keepdims=True)
            gv_out[1:2, here] += jnp.sum(da[g], axis=0, keepdims=True)
            dn = vec_ref[0:1, here] * da[g]
            ds = rstd_ref[half, 0, :, here] * (
                dn - column_of(means, 8, g) - n * column_of(means, 8, 4 + g)
            )
            dux_out[half, 0, :, here] = (ds * one1_ref[half, 0, :, here]).astype(BF16)
            duh_out[half, 0, :, here] = (ds * one0_ref[half, 0, :, here]).astype(BF16)
            d0_out[half, 0, :, here] = (ds * uh_ref[half, 0, :, here]).astype(BF16)
            d1_out[half, 0, :, here] = (ds * ux_ref[half, 0, :, here]).astype(BF16)
            da_out[half, 0, :, here] = da[g].astype(BF16)


def half_specs(total, width):
    return [pl.BlockSpec((1, total, width), lambda i, at=at: (i + at, 0, 0)) for at in (0, 4)]


def run_column_forward(slots, near, rest, x_all, main_own, tail_own, vec, steps):
    per_core, total, _ = near.shape
    n_parts, owners, _, emb_part = x_all.shape
    width = main_own.shape[1]
    units = width // 4
    tails = [(F32, width)] * 6 + [(F32, units)] * 2 + [(F32, width)]
    tails += [(BF16, emb_part + units), (BF16, E), (BF16, H), (BF16, NH), (BF16, NH), (BF16, 4 * Z)]

    def still(shape):
        return pl.BlockSpec(shape, lambda i, slots: (0,) * len(shape), pipeline_mode=pl.Buffered(1))

    return pl.pallas_call(
        functools.partial(column_forward_kernel, steps),
        grid_spec=pltpu.PrefetchScalarGridSpec(
            num_scalar_prefetch=1,
            grid=(per_core,),
            in_specs=[pl.BlockSpec((1, total, PACK), lambda i, slots: (i, 0, 0))] * 2
            + [
                pl.BlockSpec(
                    (n_parts, 1, total, emb_part), lambda i, slots, at=at: (0, slots[i + at], 0, 0)
                )
                for at in (0, per_core)
            ]
            + [still(main_own.shape), still(tail_own.shape), still(vec.shape)],
            out_specs=[
                pl.BlockSpec((2, 1, total, tail), lambda i, slots: (0, i, 0, 0)) for _, tail in tails
            ],
        ),
        out_shape=[jax.ShapeDtypeStruct((2, per_core, total, tail), dtype) for dtype, tail in tails],
        compiler_params=kernel_params(),
        cost_estimate=pl.CostEstimate(
            flops=2 * owners * total * width * 3 * H, bytes_accessed=18_000_000, transcendentals=0
        ),
        name="column_forward",
    )(slots, near, rest, x_all, x_all, main_own, tail_own, vec)


def run_column_backward(moved, back_all, vec, kept, steps):
    owners, total, _ = moved.shape
    width = vec.shape[1]
    units = width // 4
    widths = [width] * 6 + [units] * 2 + [width]
    return pl.pallas_call(
        functools.partial(column_backward_kernel, steps),
        grid=(owners // 2,),
        in_specs=half_specs(total, units)
        + [
            pl.BlockSpec((1, 1, total, 4 * Z), lambda i, at=at: (i + at, 2, 0, 0)) for at in (0, 4)
        ]
        + [whole(vec.shape)]
        + [pl.BlockSpec((2, 1, total, tail), lambda i: (0, i, 0, 0)) for tail in widths],
        out_specs=[pl.BlockSpec((2, 1, total, width), lambda i: (0, i, 0, 0))] * 5
        + [pl.BlockSpec((2, width), lambda i: (0, 0))],
        out_shape=[jax.ShapeDtypeStruct((2, owners // 2, total, width), BF16)] * 5
        + [jax.ShapeDtypeStruct((2, width), F32)],
        scratch_shapes=[pltpu.VMEM((total, units), F32)],
        compiler_params=kernel_params(),
        cost_estimate=pl.CostEstimate(
            flops=40 * owners * total * width, bytes_accessed=16_000_000, transcendentals=0
        ),
        name="column_backward",
    )(moved, moved, back_all, back_all, vec, *kept)


def table_kernel(
    me_ref, told_ref, r0_ref, r1_ref, r2_ref, r3_ref, table_out, row_out, col_out, rows_s, other_s
):
    count = rows_s.shape[0] // 4
    stride = told_ref.shape[0] // 4
    table_out[...] = jnp.zeros_like(table_out)
    other_s[...] = jnp.zeros_like(other_s)
    for part, ref in enumerate((r0_ref, r1_ref, r2_ref, r3_ref)):
        rows_s[part * count : (part + 1) * count] = ref[:count].astype(F32)

    for owner in range(4):
        part = owner ^ me_ref[0]

        @pl.loop(0, count // 16)
        def _(group):
            for lane in range(16):
                here = pl.ds(told_ref[part * stride + group * 16 + lane], 1)
                table = table_out if lane % 2 == 0 else other_s
                table[here] += rows_s[pl.ds(part * count + group * 16 + lane, 1)]

    def measure(block, cols):
        here = pl.ds(pl.multiple_of(block * VOCAB_BLOCK, VOCAB_BLOCK), VOCAB_BLOCK)
        values = table_out[here] + other_s[here]
        table_out[here] = values
        squares = values * values + EPS_FACT
        high = squares.astype(BF16)
        low = (squares - high.astype(F32)).astype(BF16)
        ones = jnp.ones((8, squares.shape[1]), BF16)
        sums = dot_last(ones, high) + dot_last(ones, low)
        row_out[pl.ds(block, 1)] = sums[:1]
        return cols + jnp.sum(squares, axis=0, keepdims=True)

    zero = jnp.zeros((1, table_out.shape[1]), F32)
    col_out[...] = lax.fori_loop(0, row_out.shape[0], measure, zero)


def run_table(me, told, parts, vocab):
    count, lanes = parts[0].shape
    total = count * len(parts)
    blocks = vocab // VOCAB_BLOCK
    return pl.pallas_call(
        table_kernel,
        grid_spec=pltpu.PrefetchScalarGridSpec(
            num_scalar_prefetch=2,
            grid=(1,),
            in_specs=[pl.BlockSpec(part.shape, lambda i, *_: (0, 0)) for part in parts],
            out_specs=[
                pl.BlockSpec((vocab, lanes), lambda i, *_: (0, 0)),
                pl.BlockSpec((blocks, VOCAB_BLOCK), lambda i, *_: (0, 0)),
                pl.BlockSpec((1, lanes), lambda i, *_: (0, 0)),
            ],
            scratch_shapes=[pltpu.VMEM((total, lanes), F32), pltpu.VMEM((vocab, lanes), F32)],
        ),
        out_shape=[
            jax.ShapeDtypeStruct((vocab, lanes), F32),
            jax.ShapeDtypeStruct((blocks, VOCAB_BLOCK), F32),
            jax.ShapeDtypeStruct((1, lanes), F32),
        ],
        compiler_params=kernel_params(),
        cost_estimate=pl.CostEstimate(flops=10**9, bytes_accessed=40_000_000, transcendentals=0),
        name="embedding_table",
    )(me, told, *parts)


def stepped_update(weight, grad, relative, spread, rate):
    return weight - rate * grad * lax.rsqrt(relative * spread)


def main_update_kernel(rate, me_ref, p0, p1, p2, p3, weight_ref, rel_ref, spread_ref, grad_out, new_out):
    quarter, part = pl.program_id(0), pl.program_id(1)
    lanes = weight_ref.shape[1]
    gates = spread_ref.shape[0]
    rows = weight_ref.shape[0] // gates
    for bits, ref in enumerate((p0, p1, p2, p3)):

        @pl.when(quarter == bits)
        def _():
            here = pl.ds(pl.multiple_of(part * rows, rows), rows)
            for g in range(gates):
                spot = pl.ds(g, rows, stride=gates)
                grad = ref[here, g * lanes : (g + 1) * lanes].astype(F32)
                grad_out[spot, :] = grad
                new_out[spot, :] = stepped_update(
                    weight_ref[spot, :], grad, rel_ref[...], spread_ref[g : g + 1], rate
                )


def run_main_update(me, parts, weight, rel_wide, spread, rate):
    total, gates, lanes = weight.shape
    rows = total // 8

    def place(quarter, part, me_ref):
        return (part * 4 + (me_ref[0] ^ quarter), 0)

    block = pl.BlockSpec((rows * gates, lanes), place)
    flat = jax.ShapeDtypeStruct((total * gates, lanes), F32)
    grad, new = pl.pallas_call(
        functools.partial(main_update_kernel, rate),
        grid_spec=pltpu.PrefetchScalarGridSpec(
            num_scalar_prefetch=1,
            grid=(4, 2),
            in_specs=[pl.BlockSpec(part.shape, lambda q, p, m: (0, 0)) for part in parts]
            + [
                block,
                pl.BlockSpec((rows, LANES), place),
                pl.BlockSpec(spread.shape, lambda q, p, m: (0, 0)),
            ],
            out_specs=[block, block],
        ),
        out_shape=[flat, flat],
        compiler_params=kernel_params(),
        cost_estimate=pl.CostEstimate(flops=10**7, bytes_accessed=16_000_000, transcendentals=0),
        name="main_update",
    )(me, *parts, weight.reshape(total * gates, lanes), rel_wide, spread)
    return grad.reshape(weight.shape), new.reshape(weight.shape)


def out_update_kernel(rate, seen_ref, weight_ref, rel_ref, spread_ref, grad_out, new_out):
    for j in range(grad_out.shape[1] // LANES):
        cols = slice(j * LANES, (j + 1) * LANES)
        grad = seen_ref[:, cols].astype(F32)
        grad_out[:, cols] = grad
        new_out[:, cols] = stepped_update(weight_ref[:, cols], grad, rel_ref[...], spread_ref[:, cols], rate)


def run_out_update(seen, weight, rel_wide, spread, rate):
    total, width = weight.shape
    rows = total // 4

    def rows_of(columns):
        return pl.BlockSpec((rows, columns), lambda i: (i, 0))

    return pl.pallas_call(
        functools.partial(out_update_kernel, rate),
        grid=(4,),
        in_specs=[rows_of(width), rows_of(width), rows_of(LANES), pl.BlockSpec(spread.shape, lambda i: (0, 0))],
        out_specs=[rows_of(width)] * 2,
        out_shape=[jax.ShapeDtypeStruct(weight.shape, F32)] * 2,
        compiler_params=kernel_params(),
        cost_estimate=pl.CostEstimate(flops=10**7, bytes_accessed=20_000_000, transcendentals=0),
        name="out_update",
    )(seen, weight, rel_wide, spread)


def factored_update(rate, grad_out, new_out, weight_ref, row_ref, col_ref, row_out, col_out):
    total, width = grad_out.shape
    decay = 1.0 - STEP ** (-0.8)
    blocks = [(at, min(256, total - at)) for at in range(0, total, 256)]
    cols = jnp.zeros((1, width), F32)
    sums = jnp.zeros((1, LANES), F32)
    for at, size in blocks:
        here = slice(at, at + size)
        grad = grad_out[here]
        squares = grad * grad + EPS_FACT
        cols += jnp.sum(squares, axis=0, keepdims=True)
        mean = jnp.sum(squares, axis=1, keepdims=True) / width
        row_new = decay * row_ref[here] + (1.0 - decay) * mean
        row_out[here] = row_new
        sums += jnp.sum(row_new, axis=0, keepdims=True)
    col_new = decay * col_ref[...] + (1.0 - decay) * (cols / total)
    col_out[...] = col_new
    average = sums / total
    for at, size in blocks:
        here = slice(at, at + size)
        relative = row_out[here] / average
        for start in range(0, width, LANES):
            lanes = slice(start, min(start + LANES, width))
            new_out[here, lanes] = stepped_update(
                weight_ref[here, lanes],
                grad_out[here, lanes],
                relative[:, : lanes.stop - start],
                col_new[:, lanes],
                rate,
            )


def hyper_update_kernel(
    rate, zed_rate, parts_ref, bias_ref, weight_ref, row_ref, col_ref,
    zed_bias_ref, zed_weight_ref, zed_row_ref, zed_col_ref,
    grad_out, new_out, row_out, col_out, zed_grad_out, zed_new_out, zed_row_out, zed_col_out,
):
    quarters, owners, _, _ = parts_ref.shape
    total = grad_out.shape[0]
    devices = quarters * owners
    heights = (E // devices, H // devices, NH // devices)
    zed_width = zed_grad_out.shape[1]
    for owner in range(owners):
        for quarter in range(quarters):
            part = parts_ref[quarter, owner].astype(F32)
            place = owner * quarters + quarter
            first, start = 0, 0
            for height, size in zip(heights, (E, H, NH)):
                to = start + place * height
                grad_out[to : to + height] = part[first : first + height]
                first += height
                start += size
            to = place * heights[2]
            zed_grad_out[to : to + heights[2]] = part[first : first + heights[2], :zed_width]
    zed_grad_out[NH:] = zed_bias_ref[...]
    grad_out[total - 1 :] = bias_ref[...]
    factored_update(rate, grad_out, new_out, weight_ref, row_ref, col_ref, row_out, col_out)
    factored_update(
        zed_rate, zed_grad_out, zed_new_out, zed_weight_ref, zed_row_ref, zed_col_ref, zed_row_out, zed_col_out
    )


def run_hyper_update(parts, hyper, zproj, rates):
    values = [*hyper, *zproj]

    def all_of(values):
        return pl.BlockSpec(values.shape, lambda i: (0,) * values.ndim)

    outs = []
    for _, weight, row, col in (hyper, zproj):
        outs += [weight, weight, row, col]
    return pl.pallas_call(
        functools.partial(hyper_update_kernel, *rates),
        grid=(1,),
        in_specs=[all_of(parts)] + [all_of(value) for value in values],
        out_specs=[all_of(out) for out in outs],
        out_shape=[jax.ShapeDtypeStruct(out.shape, F32) for out in outs],
        compiler_params=kernel_params(),
        cost_estimate=pl.CostEstimate(flops=10**7, bytes_accessed=20_000_000, transcendentals=0),
        name="hyper_update",
    )(parts, *values)


def updates(weights, states, grads, row_sums, embed_col_mean):
    embed, w_main, w_scale, w_hyper, w_zproj, w_out, main_vectors = weights
    (
        embed_row, embed_col, main_row, main_col, scale_row, scale_col, hyper_row, hyper_col,
        zproj_row, zproj_col, out_row, out_col, vector_state,
    ) = states
    g_embed, g_main, g_scale, g_hyper, g_zproj, g_out, g_vec = grads
    row_embed, row_main, row_scale, row_out = row_sums
    sq_main, sq_scale, sq_hyper, sq_zproj, sq_out = [
        g * g + EPS_FACT for g in (g_main, g_scale, g_hyper, g_zproj, g_out)
    ]
    res_embed = adafactor(
        embed, g_embed, embed_row, embed_col, row_embed / E, embed_col_mean, 0, 1.0
    )
    res_main = adafactor(
        w_main,
        g_main,
        main_row,
        main_col,
        row_main / (4 * H),
        jnp.mean(sq_main, axis=0),
        0,
        1.0 / math.sqrt(E),
    )
    res_scale = adafactor(
        w_scale,
        g_scale,
        scale_row,
        scale_col,
        row_scale / (4 * H),
        jnp.mean(sq_scale, axis=1),
        1,
        1.0 / math.sqrt(Z),
    )
    res_hyper = adafactor(
        w_hyper,
        g_hyper,
        hyper_row,
        hyper_col,
        jnp.mean(sq_hyper, axis=1),
        jnp.mean(sq_hyper, axis=0),
        0,
        1.0 / math.sqrt(E + H + NH + 1),
    )
    res_zproj = adafactor(
        w_zproj,
        g_zproj,
        zproj_row,
        zproj_col,
        jnp.mean(sq_zproj, axis=1),
        jnp.mean(sq_zproj, axis=0),
        0,
        2.0 / math.sqrt(NH),
    )
    res_out = adafactor(
        w_out, g_out, out_row, out_col, row_out / V, jnp.mean(sq_out, axis=0), 0, 3.0 / math.sqrt(H)
    )
    decay = 1.0 - STEP ** (-0.8)
    state_new = decay * vector_state + (1.0 - decay) * (g_vec * g_vec + EPS_FACT)
    vectors_new = main_vectors - 0.1 * g_vec * lax.rsqrt(state_new)
    return (
        res_embed
        + res_main
        + res_scale
        + res_hyper
        + res_zproj
        + res_out
        + (g_vec, state_new, vectors_new)
    )


def per_chip(
    parts,
    token_ids,
    seq_lengths,
    valid_mask,
    embed,
    w_main,
    w_scale,
    w_hyper,
    w_zproj,
    w_out,
    main_vectors,
    *states,
):
    n_mp, n_batch = parts
    my = lax.axis_index("mp")
    b = lax.axis_index("batch")
    units = w_main.shape[2]
    width = 4 * units
    emb_part = embed.shape[1]
    vocab_part = w_out.shape[1]
    batch_rows, steps = valid_mask.shape
    own = batch_rows // n_mp
    own_total = steps * own
    total = batch_rows * steps
    slots = my ^ jnp.array(SLOTS, jnp.int32)
    order = my ^ jnp.arange(n_mp, dtype=jnp.int32)
    from_slots = order // 2 + (n_mp // 2) * (order % 2)

    def by_owner(values):
        return values.reshape(n_mp, own, steps).transpose(0, 2, 1)

    def to_partners(values):
        return [swap(values, "batch", n_batch, bits) for bits in (1, 2, 3)]

    def quarter_of(values, bits, rows):
        return lax.dynamic_slice_in_dim(values, (b ^ bits) * rows, rows, 0)

    (
        embed_row, embed_col, main_row, main_col, scale_row, scale_col, hyper_row, hyper_col,
        zproj_row, zproj_col, out_row, out_col, vector_state,
    ) = states
    decay = 1.0 - STEP ** (-0.8)

    def moving(old, mean):
        return decay * old + (1.0 - decay) * mean

    def across(values):
        return jnp.broadcast_to(values[:, None], (values.shape[0], LANES))

    def placed(pieces, me):
        out = jnp.zeros((len(pieces),) + pieces[0].shape, pieces[0].dtype)
        for bits, piece in enumerate(pieces):
            out = lax.dynamic_update_slice_in_dim(out, piece[None], me ^ bits, 0)
        return out

    quarter = SCALE_AT // 4
    tail_quarter = TAIL_ROWS // 4
    half = (quarter + tail_quarter) // 2

    def own_rows(first, rows):
        values = lax.dynamic_slice_in_dim(w_main, b * quarter + first, rows, 0)
        return values.astype(BF16).reshape(rows, width)

    head_part = own_rows(0, half)
    head = swap(head_part, "mp", n_mp, 2)
    tail_own = weight_tail(w_scale, main_vectors)
    tail_part = jnp.concatenate(
        [own_rows(half, quarter - half), lax.dynamic_slice_in_dim(tail_own, b * tail_quarter, tail_quarter, 0)], axis=0
    )
    x_part = embed[by_owner(token_ids[:, :steps]).reshape(total)].astype(BF16)
    tail_part, head_part, head, x_part = tie(tail_part, head_part, head, x_part)
    tail = swap(tail_part, "mp", n_mp, 2)
    far = swap(jnp.concatenate([head_part, tail_part], axis=0), "mp", n_mp, 4)
    main_own = w_main.astype(BF16).reshape(2 * E, width)
    hyp_low = w_hyper.astype(BF16)
    far, hyper_wide, zproj_wide = tie(far, across(hyper_row), across(zproj_row))
    both = swap(far, "mp", n_mp, 2)
    x_all = lax.all_gather(x_part, "mp").reshape(n_mp, n_mp, own_total, emb_part)
    x_own = lax.dynamic_index_in_dim(x_all, my, 1, False).transpose(1, 0, 2).reshape(own_total, E)
    found = []
    for array, bits in ((main_own, 0), (swap(main_own, "mp", n_mp, 1), 1)):
        found.append((array, bits, None, 0, SCALE_AT))
    for array, bits in ((tail_own, 0), (swap(tail_own, "mp", n_mp, 1), 1)):
        found.append((array, bits, None, SCALE_AT, TAIL_ROWS))
    for got, bits, start in ((head, 2, 0), (tail, 2, half), (far, 4, 0), (both, 6, 0)):
        cut = got.shape[0] // 2
        along_x = swap(got, "batch", n_batch, 1)
        along_y = swap(got, "batch", n_batch, 2)
        low = swap(along_x[:cut], "batch", n_batch, 2)
        high = swap(along_y[cut:], "batch", n_batch, 1)
        for array, over, first in (
            (got, 0, start), (along_x, 1, start), (along_y, 2, start), (low, 3, start), (high, 3, start + cut),
        ):
            found.append((array, bits, over, first, array.shape[0]))
            found.append((swap(array, "mp", n_mp, 1), bits ^ 1, over, first, array.shape[0]))
    found.sort(key=lambda piece: piece[1])
    plan = [piece[1:] for piece in found]
    pieces = [piece[0] for piece in found]
    blocks = (n_mp, width)
    hyp_bias = hyp_low[E + H + NH :].astype(F32)
    zp_wide = jnp.pad(w_zproj, ((0, 0), (0, Z))).astype(BF16)
    zp_bias = zp_wide[NH:].astype(F32)
    pack, *kept = run_forward(
        x_own, blocks, plan, pieces, hyp_low, hyp_bias, zp_wide[:NH], zp_bias, steps
    )

    def of_chips(values):
        return jnp.stack([values] + [swap(values, "mp", n_mp, bits) for bits in (2, 4, 6)])

    def both_halves(near):
        return jnp.concatenate([near, swap(near, "mp", n_mp, 1)], axis=0)

    pack, token_ids, seq_lengths, valid_mask, w_out, *pieces = tie(
        pack, token_ids, seq_lengths, valid_mask, w_out, *pieces
    )
    near = of_chips(pack.reshape(own_total, PACK))
    positions = jnp.arange(steps, dtype=jnp.int32)
    valid = valid_mask * (positions[None, :] < seq_lengths[:, None]).astype(jnp.int32)
    marks = jnp.stack([token_ids[:, :steps], token_ids[:, 1:], valid])
    marks = marks.reshape(3, n_mp, own, steps).transpose(0, 1, 3, 2)[:, slots].reshape(3, total)
    told = jnp.concatenate([marks[0], jnp.broadcast_to(jnp.sum(valid), (LANES,))])
    told = jnp.concatenate([told, swap(told, "batch", n_batch, 1)])
    weight_rows = marks[2].astype(F32)
    out_low = w_out.astype(BF16)
    turned = run_turn(blocks, plan, pieces)
    near, told, marks, weight_rows, out_low, *turned = tie(near, told, marks, weight_rows, out_low, *turned)
    rest = swap(near, "mp", n_mp, 1)
    h_all = jnp.concatenate([near[:, :, :H], rest[:, :, :H]], axis=0)
    h_rows = h_all.reshape(total, H)
    logits = matmul(h_rows, out_low)
    local_target = marks[1] - my * vocab_part
    hit = jnp.arange(vocab_part, dtype=jnp.int32)[None, :] == local_target[:, None]
    top = jnp.max(logits, axis=1)
    stats = [
        top,
        jnp.sum(jnp.exp(logits - top[:, None]), axis=1),
        jnp.sum(jnp.where(hit, logits, 0.0), axis=1),
    ]

    def merged(one, two):
        top = jnp.maximum(one[0], two[0])
        exps = one[1] * jnp.exp(one[0] - top) + two[1] * jnp.exp(two[0] - top)
        return jnp.stack([top, exps, one[2] + two[2]])

    def from_partner(values, bits):
        spots = [bits ^ slot for slot in SLOTS]
        spots = [spot // 2 + (n_mp // 2) * (spot % 2) for spot in spots]
        turned = jnp.concatenate([values[:, spot : spot + 1] for spot in spots], axis=1)
        return swap(turned, "mp", n_mp, bits)

    stats = jnp.stack(stats).reshape(3, n_mp, own_total)
    pair = merged(stats, from_partner(stats, 1))
    pair, told = tie(pair, told)
    others = [from_partner(pair, bits) for bits in (2, 4, 6)]
    told = jnp.concatenate([told, swap(told, "batch", n_batch, 2)])
    count = sum(told[k * (total + LANES) + total] for k in range(n_batch)).astype(F32)
    stats = merged(merged(pair, others[0]), merged(others[1], others[2]))
    log_total = (stats[0] + jnp.log(stats[1])).reshape(total)
    loss = jnp.sum(
        (log_total[:own_total] - stats[2].reshape(total)[:own_total]) * weight_rows[:own_total]
    )
    grad_logits = (
        (jnp.exp(logits - log_total[:, None]) - hit.astype(F32)) * (weight_rows / count)[:, None]
    ).astype(BF16)
    other = swap(dot_last(grad_logits[total // 2 :], out_low).astype(BF16), "mp", n_mp, 1)
    both_cores = dot_last(grad_logits[: total // 2], out_low) + other.astype(F32)
    near, rest, both_cores = tie(near, rest, both_cores.reshape(n_mp // 2, own_total, H))
    dh_parts = [
        swap(both_cores[spot].astype(BF16), "mp", n_mp, 2 * spot) for spot in range(1, n_mp // 2)
    ]
    vec = main_vectors.reshape(2, width)
    column = run_column_forward(slots, near, rest, x_all, main_own, tail_own, vec, steps)
    dh_parts[1], *column = tie(dh_parts[1], *column)
    h_rows, dh_parts[0] = tie(h_rows, dh_parts[0])
    g_out = dot_first(h_rows, grad_logits).astype(BF16)
    out_quarter = H // n_batch
    out_parts = [quarter_of(g_out, bits, out_quarter) for bits in range(n_batch)]
    dh_top = both_cores[0]
    for part in dh_parts:
        dh_top = dh_top + part.astype(F32)
    dh_top, *out_parts = tie(dh_top, *out_parts)
    out_got = [swap(part, "batch", n_batch, bits) for bits, part in enumerate(out_parts) if bits]
    moved, odd, back_own, _, _ = run_backward(
        dh_top.reshape(steps, own, H), blocks, plan, turned, hyp_low, zp_wide[:NH], kept
    )
    left, x_rows, h_before, hh_before, hh_all, z_all = column[9:]
    moved, odd, back_own, hh_before, hh_all, z_all, loss, told, *out_got = tie(
        moved, odd, back_own, hh_before, hh_all, z_all, loss, told, *out_got
    )
    out_sum = out_parts[0].astype(F32)
    for part in out_got:
        out_sum = out_sum + part.astype(F32)

    moved = moved.reshape(n_mp // 2, own_total, 2 * units)
    back_own = back_own.reshape(3, own_total, 2 * NH)
    crossed = swap(odd.reshape(moved.shape), "mp", n_mp, 1)
    crossed, out_low_sum = tie(crossed, out_sum.astype(BF16))
    g_out = lax.all_gather(out_low_sum, "batch").reshape(H, vocab_part)
    arrived = [
        swap(
            jnp.concatenate([moved[spot : spot + 1], crossed[spot : spot + 1], back_own], axis=0),
            "mp",
            n_mp,
            2 * spot,
        )
        for spot in range(1, n_mp // 2)
    ]
    moved = jnp.stack(
        [moved[0]] + [part[0] for part in arrived] + [crossed[0]] + [part[1] for part in arrived]
    )
    back_all = both_halves(jnp.stack([back_own] + [part[2:] for part in arrived]))
    dx_part = moved[:, :, units:].reshape(total, emb_part)

    nh_part = NH // n_mp
    hyp_rows = emb_part + units + 2 * nh_part
    hyp_quarter = hyp_rows // n_batch

    def own_columns(values, size):
        return lax.dynamic_slice_in_dim(values, my * size, size, values.ndim - 1)

    dq_rows = jnp.concatenate([back_all[:, 0], back_all[:, 1]], axis=2).reshape(total, 4 * NH)
    dz_rows = back_all[:, 2, :, : 3 * Z].reshape(total, 3 * Z)
    hh_left = own_columns(hh_before, nh_part).reshape(total, nh_part)
    hh_own = own_columns(hh_all, nh_part).reshape(total, nh_part)
    g_small = [
        dot_first(left.reshape(total, emb_part + units), dq_rows),
        dot_first(hh_left, dq_rows),
        jnp.pad(dot_first(hh_own, dz_rows), ((0, 0), (0, 4 * NH - 3 * Z))),
    ]
    g_small = [g_small[0][:emb_part], g_small[0][emb_part:], g_small[1], g_small[2]]

    def small_quarter(bits):
        return jnp.concatenate([quarter_of(g, bits, g.shape[0] // n_batch) for g in g_small], axis=0)

    hyp_got, dx_got = [], [dx_part]
    for bits in (1, 2, 3):
        part = small_quarter(bits).astype(BF16).reshape(-1, emb_part)
        got = swap(jnp.concatenate([dx_part, part], axis=0), "batch", n_batch, bits)
        dx_got.append(got)
        hyp_got.append(got[total:].reshape(hyp_quarter, 4 * NH))
    hyp_sum = small_quarter(0)
    for got in hyp_got:
        hyp_sum = hyp_sum + got.astype(F32)
    hyp_all = lax.all_gather(hyp_sum.astype(BF16), ("batch", "mp"))
    hyp_all = hyp_all.reshape(n_batch, n_mp, hyp_quarter, 4 * NH)

    dux, duh, d0, d1, da, gv = run_column_backward(moved, back_all, vec, column[:9], steps)
    x_rows = x_rows.reshape(total, E)
    h_before = h_before.reshape(total, H)
    z_rows = z_all[:, :, :, : 3 * Z].reshape(total, 3, Z)
    g_parts = [dot_first(x_rows, dux.reshape(total, width)), dot_first(h_before, duh.reshape(total, width))] + [
        dot_first(z_rows[:, k], d.reshape(total, width)) for k, d in enumerate((d0, d1, da))
    ]

    def main_quarter(bits):
        return jnp.concatenate(
            [quarter_of(part, bits, part.shape[0] // n_batch) for part in g_parts], axis=0
        )

    g_parts[2], dx_got[3] = tie(g_parts[2], dx_got[3])
    main_got = [swap(main_quarter(bits).astype(BF16), "batch", n_batch, bits) for bits in (1, 2, 3)]

    me = b.reshape(1)
    g_embed, embed_rows, embed_cols = run_table(me, told, dx_got, embed.shape[0])

    g_embed, embed_rows, embed_cols, *main_got = tie(g_embed, embed_rows, embed_cols, *main_got)
    main_sum = main_quarter(0)
    for got in main_got:
        main_sum = main_sum + got.astype(F32)
    main_low = main_sum.astype(BF16)
    main_pieces = [main_low] + to_partners(main_low)
    main_seen = main_low.astype(F32)
    sq_main = main_seen * main_seen + EPS_FACT
    in_quarter = (E + H) // n_batch
    scale_quarter = Z // n_batch

    out_seen = g_out.astype(F32)
    sq_out = out_seen * out_seen + EPS_FACT

    by_rows = tree_sum(
        jnp.concatenate(
            [
                embed_rows.reshape(-1),
                jnp.sum(sq_out, axis=1),
                jnp.sum(sq_main, axis=1),
                loss[None],
            ]
        ),
        "mp",
        n_mp,
    )
    row_embed = by_rows[: embed.shape[0]]
    row_out = by_rows[embed.shape[0] : embed.shape[0] + H]
    sums = jnp.sum(back_all.astype(F32), axis=2)[from_slots]
    sums = jnp.sum(sums, axis=0).reshape(-1)[: 4 * NH + 3 * Z]
    fields = [
        by_rows[embed.shape[0] + H : -1],
        by_rows[-1:],
        jnp.sum(sq_main[:in_quarter], axis=0),
        jnp.sum(sq_main[in_quarter:].reshape(3, scale_quarter, width), axis=1).reshape(-1),
        gv.reshape(-1),
        sums,
    ]
    sizes = [field.shape[0] for field in fields]
    mixed = jnp.concatenate(fields)
    mixed = jnp.stack([mixed, swap(mixed, "batch", n_batch, 1)])
    mixed = placed(list(mixed) + list(swap(mixed, "batch", n_batch, 2)), b)
    rows_four = mixed[:, : sizes[0]]
    added = jnp.sum(mixed[:, sizes[0] :], axis=0)
    ends = [sum(sizes[1 : k + 1]) for k in range(len(sizes))]
    loss_sum, col_main, col_scale, g_vec, bias_sums = [
        added[ends[k] : ends[k + 1]] for k in range(len(sizes) - 1)
    ]
    row_in = rows_four[:, : E // n_batch].reshape(E)
    row_rec = rows_four[:, E // n_batch : in_quarter].reshape(H)
    row_scale = rows_four[:, in_quarter:].reshape(n_batch, 3, scale_quarter)
    row_scale = jnp.moveaxis(row_scale, 0, 1).reshape(3, Z)
    g_vec = g_vec.reshape(2, 4, units)

    res_embed = adafactor(
        embed, g_embed, embed_row, embed_col, row_embed / E, embed_cols[0] / embed.shape[0], 0, 1.0
    )
    new_out_row = moving(out_row, row_out / V)
    new_out_col = moving(out_col, jnp.mean(sq_out, axis=0))
    g_out, new_out = run_out_update(
        g_out,
        w_out,
        across(new_out_row / jnp.mean(new_out_row)),
        new_out_col[None],
        3.0 / math.sqrt(H),
    )
    (
        g_hyper, new_hyper, hyper_rows, new_hyper_col, g_zproj, new_zproj, zproj_rows, new_zproj_col,
    ) = run_hyper_update(
        hyp_all,
        (bias_sums[None, : 4 * NH], w_hyper, hyper_wide, hyper_col[None]),
        (bias_sums[None, 4 * NH :], w_zproj, zproj_wide, zproj_col[None]),
        (1.0 / math.sqrt(E + H + NH + 1), 2.0 / math.sqrt(NH)),
    )
    new_embed, new_out, new_hyper, *main_pieces = tie(res_embed[1], new_out, new_hyper, *main_pieces)
    res_embed = (res_embed[0], new_embed) + res_embed[2:]
    scale_parts = placed([piece[in_quarter:] for piece in main_pieces], b)
    g_scale = jnp.moveaxis(scale_parts.reshape(n_batch, 3, scale_quarter, width), 0, 1)
    g_scale = g_scale.reshape(3, Z, 4, units).astype(F32)
    new_main_row = moving(main_row, jnp.concatenate([row_in, row_rec]) / (4 * H))
    new_main_col = moving(main_col, col_main.reshape(4, units) / (E + H))
    g_main, new_main = run_main_update(
        me,
        main_pieces,
        w_main,
        across(new_main_row / jnp.mean(new_main_row)),
        new_main_col,
        1.0 / math.sqrt(E),
    )
    res_scale = adafactor(
        w_scale,
        g_scale,
        scale_row,
        scale_col,
        row_scale / (4 * H),
        col_scale.reshape(3, 4, units) / Z,
        1,
        1.0 / math.sqrt(Z),
    )
    state_new = moving(vector_state, g_vec * g_vec + EPS_FACT)
    return (
        (loss_sum[0], count)
        + res_embed
        + (g_main, new_main, new_main_row, new_main_col)
        + res_scale
        + (g_hyper, new_hyper, hyper_rows[:, 0], new_hyper_col[0])
        + (g_zproj, new_zproj, zproj_rows[:, 0], new_zproj_col[0])
        + (g_out, new_out, new_out_row, new_out_col)
        + (g_vec, state_new, main_vectors - 0.1 * g_vec * lax.rsqrt(state_new))
    )


def per_device(
    parts,
    token_ids,
    seq_lengths,
    valid_mask,
    embed,
    w_main,
    w_scale,
    w_hyper,
    w_zproj,
    w_out,
    main_vectors,
    *states,
):
    n_mp, n_batch = parts
    my = lax.axis_index("mp")
    units = w_main.shape[2]
    emb_part = embed.shape[1]
    vocab_part = w_out.shape[1]
    batch_rows, steps = valid_mask.shape
    own = batch_rows // n_mp
    padded = -(-own // ROW_TILE) * ROW_TILE
    own_total = steps * own
    total = batch_rows * steps
    wide = units % LANES == 0

    def by_owner(values):
        return values.reshape(n_mp, own, steps).transpose(0, 2, 1)

    ids = by_owner(token_ids[:, :steps]).reshape(total)
    targets = by_owner(token_ids[:, 1:]).reshape(total)
    positions = jnp.arange(steps, dtype=jnp.int32)
    valid = valid_mask.astype(F32) * (positions[None, :] < seq_lengths[:, None]).astype(F32)
    weight_rows = by_owner(valid).reshape(total)
    count = tree_sum(jnp.sum(weight_rows), "batch", n_batch)

    def to_kernel(stacked):
        if wide:
            return stacked
        rows = stacked.shape[1]
        apart = stacked.reshape(n_mp, rows, 4, units).transpose(1, 2, 0, 3)
        return apart.reshape(1, rows, 4 * H)

    def pad_rows(values):
        return jnp.pad(values, ((0, 0), (0, padded - own), (0, 0))) if padded > own else values

    def unpad(values):
        return values[:, :own] if padded > own else values

    x_part = embed[ids].astype(BF16)
    main_own = w_main.astype(BF16).reshape(E + H, 4 * units)
    tail_own = weight_tail(w_scale, main_vectors)
    scale_own = tail_own[: 3 * Z]
    x_own = lax.all_to_all(x_part.reshape(n_mp, own_total, emb_part), "mp", 0, 0)
    x_own = x_own.transpose(1, 0, 2).reshape(steps, own, E)
    pieces = [to_kernel(lax.all_gather(jnp.concatenate([main_own, tail_own], axis=0), "mp"))]
    blocks = (pieces[0].shape[0], pieces[0].shape[2])
    x_all = lax.all_gather(x_part, "mp", axis=1, tiled=True)
    hyp_low = w_hyper.astype(BF16)
    zp_wide = jnp.pad(w_zproj, ((0, 0), (0, Z))).astype(BF16)
    out_low = w_out.astype(BF16)
    hyp_bias = hyp_low[E + H + NH :].astype(F32)
    zp_bias = zp_wide[NH:].astype(F32)

    pack, *kept = run_forward(
        pad_rows(x_own).reshape(steps * padded, E),
        blocks, None, pieces, hyp_low, hyp_bias, zp_wide[:NH], zp_bias, steps,
    )

    small_own = unpad(pack)[:, :, : H + NH + 3 * Z]
    rows_all = lax.all_gather(small_own.reshape(own_total, H + NH + 3 * Z), "mp")
    h_rows = rows_all[:, :, :H].reshape(total, H)
    logits = matmul(h_rows, out_low)
    local_target = targets - my * vocab_part
    hit = jnp.arange(vocab_part, dtype=jnp.int32)[None, :] == local_target[:, None]
    top = jnp.max(logits, axis=1)
    stats = jnp.stack(
        [
            top,
            jnp.sum(jnp.exp(logits - top[:, None]), axis=1),
            jnp.sum(jnp.where(hit, logits, 0.0), axis=1),
        ]
    )
    stats = lax.all_gather(stats, "mp")
    top_all = jnp.max(stats[:, 0], axis=0)
    exp_sum = jnp.sum(stats[:, 1] * jnp.exp(stats[:, 0] - top_all), axis=0)
    log_total = top_all + jnp.log(exp_sum)
    picked = jnp.sum(stats[:, 2], axis=0)
    loss_sum = tree_sum(jnp.sum((log_total - picked) * weight_rows), "batch", n_batch)
    grad_logits = (
        (jnp.exp(logits - log_total[:, None]) - hit.astype(F32)) * (weight_rows / count)[:, None]
    ).astype(BF16)
    dh_part = dot_last(grad_logits, out_low).reshape(n_mp, own_total, H)
    dh_parts = lax.all_to_all(dh_part.astype(BF16), "mp", 0, 0)
    dh_top = jnp.sum(dh_parts.astype(F32), axis=0)
    dh_top = dh_top.reshape(steps, own, H)
    g_out = dot_first(h_rows, grad_logits).astype(BF16)
    dh_top, g_out = lax.optimization_barrier((dh_top, g_out))
    g_out = lax.psum(g_out, "batch").astype(F32)

    dsda, _, back, dx_own, gv = run_backward(
        pad_rows(dh_top), blocks, None, run_turn(blocks, None, pieces), hyp_low, zp_wide[:NH], kept
    )
    back = jnp.concatenate(list(back), axis=2)

    if wide:
        dsda = unpad(dsda.reshape(n_mp * steps, padded, 8 * units))
    else:
        dsda = unpad(dsda.reshape(steps, padded, 8 * H)).reshape(own_total, 8, n_mp, units)
        dsda = dsda.transpose(2, 0, 1, 3)
    dsda = dsda.reshape(n_mp, own_total, 8 * units)
    dx_send = unpad(dx_own.reshape(steps, padded, E)).reshape(own_total, n_mp, emb_part)
    sent = jnp.concatenate([dsda, dx_send.transpose(1, 0, 2)], axis=2)
    sent = lax.all_to_all(sent, "mp", 0, 0).reshape(total, 8 * units + emb_part)
    ds = sent[:, : 4 * units].astype(F32)
    da_low = sent[:, 4 * units : 8 * units]
    dx_part = sent[:, 8 * units :]
    back_own = unpad(back)[:, :, : 4 * NH + 3 * Z]
    back_all = lax.all_gather(back_own.reshape(own_total, 4 * NH + 3 * Z), "mp")
    back_all = back_all.reshape(total, 4 * NH + 3 * Z)
    dq_all = back_all[:, : 4 * NH]
    dz_all = back_all[:, 4 * NH :]

    before = jnp.concatenate(
        [jnp.zeros_like(rows_all[:, :own]), rows_all[:, : own_total - own]], axis=1
    ).reshape(total, H + NH + 3 * Z)
    h_before = before[:, :H]
    hh_before = before[:, H : H + NH]
    hh_rows = rows_all[:, :, H : H + NH].reshape(total, NH)
    z_rows = rows_all[:, :, H + NH :].reshape(total, 3, Z)
    uh = matmul(h_before, main_own[E:])
    ux = matmul(x_all, main_own[:E])
    scale_blocks = scale_own.reshape(3, Z, 4 * units)
    one0 = 1.0 + matmul(z_rows[:, 0], scale_blocks[0])
    one1 = 1.0 + matmul(z_rows[:, 1], scale_blocks[1])
    g_in = dot_first(x_all, (ds * one1).astype(BF16))
    g_rec = dot_first(h_before, (ds * one0).astype(BF16))
    d_scales = [(ds * uh).astype(BF16), (ds * ux).astype(BF16), da_low]
    g_scale = jnp.stack([dot_first(z_rows[:, k], d_scales[k]) for k in range(3)])
    nh_part = NH // n_mp
    left = jnp.concatenate(
        [
            x_part,
            lax.dynamic_slice_in_dim(h_before, my * units, units, 1),
            lax.dynamic_slice_in_dim(hh_before, my * nh_part, nh_part, 1),
        ],
        axis=1,
    )
    g_hyper = dot_first(left, dq_all)
    g_zproj = dot_first(lax.dynamic_slice_in_dim(hh_rows, my * nh_part, nh_part, 1), dz_all)

    dx_all = lax.all_gather(dx_part, "batch").reshape(n_batch * total, emb_part)
    ids_all = lax.all_gather(ids, "batch").reshape(n_batch * total)
    g_embed = jax.ops.segment_sum(dx_all.astype(F32), ids_all, num_segments=embed.shape[0])
    g_in, g_rec, g_scale, g_hyper, g_zproj = lax.psum(
        tuple(g.astype(BF16) for g in (g_in, g_rec, g_scale, g_hyper, g_zproj)), "batch"
    )
    flat = lax.all_gather(
        jnp.concatenate([g_hyper.reshape(-1, LANES), g_zproj.reshape(-1, LANES)], axis=0), "mp"
    ).astype(F32)
    n_hyp = g_hyper.size // LANES
    all_hyper = flat[:, :n_hyp].reshape(n_mp, emb_part + units + nh_part, 4 * NH)
    all_zproj = flat[:, n_hyp:].reshape(n_mp * nh_part, 3 * Z)
    if wide:
        gv_parts = gv.reshape(n_mp, 2, 4, units)
    else:
        gv_parts = gv.reshape(2, 4, n_mp, units).transpose(2, 0, 1, 3)
    gv_parts, bias_sums = lax.psum(
        (gv_parts, jnp.sum(back_own.astype(F32), axis=(0, 1))), ("batch", "mp")
    )
    g_vec = lax.dynamic_index_in_dim(gv_parts, my, 0, False)
    g_hyper = jnp.concatenate(
        [
            all_hyper[:, :emb_part].reshape(E, 4 * NH),
            all_hyper[:, emb_part : emb_part + units].reshape(H, 4 * NH),
            all_hyper[:, emb_part + units :].reshape(NH, 4 * NH),
            bias_sums[None, : 4 * NH],
        ],
        axis=0,
    )
    g_zproj = jnp.concatenate([all_zproj, bias_sums[None, 4 * NH :]], axis=0)
    g_main = jnp.concatenate([g_in, g_rec], axis=0).astype(F32).reshape(E + H, 4, units)
    g_scale = g_scale.astype(F32).reshape(3, Z, 4, units)

    sq_embed = g_embed * g_embed + EPS_FACT
    sq_main = g_main * g_main + EPS_FACT
    sq_scale = g_scale * g_scale + EPS_FACT
    sq_out = g_out * g_out + EPS_FACT
    row_out = lax.psum(jnp.sum(sq_out, axis=1), "mp")
    row_embed, row_main, row_scale = lax.psum(
        (
            jnp.sum(sq_embed, axis=1),
            jnp.sum(sq_main, axis=(1, 2)),
            jnp.sum(sq_scale, axis=(2, 3)),
        ),
        "mp",
    )
    return (loss_sum, count) + updates(
        (embed, w_main, w_scale, w_hyper, w_zproj, w_out, main_vectors),
        states,
        (g_embed, g_main, g_scale, g_hyper, g_zproj, g_out, g_vec),
        (row_embed, row_main, row_scale, row_out),
        jnp.mean(sq_embed, axis=0),
    )


def solution(mesh):
    rep = P()
    placed = (
        P("batch", None),
        P("batch"),
        P("batch", None),
        P(None, "mp"),
        P(None, None, "mp"),
        P(None, None, None, "mp"),
        rep,
        rep,
        P(None, "mp"),
        P(None, None, "mp"),
        rep,
        P("mp"),
        rep,
        P(None, "mp"),
        rep,
        P(None, None, "mp"),
        rep,
        rep,
        rep,
        rep,
        rep,
        P("mp"),
        P(None, None, "mp"),
    )
    parts = (mesh.shape["mp"], mesh.shape["batch"])
    body = per_chip if parts == (8, 4) else per_device
    return jax.shard_map(
        functools.partial(body, parts),
        mesh=mesh,
        in_specs=placed,
        out_specs=(
            rep,
            rep,
            P(None, "mp"),
            P(None, "mp"),
            rep,
            P("mp"),
            P(None, None, "mp"),
            P(None, None, "mp"),
            rep,
            P(None, "mp"),
            P(None, None, None, "mp"),
            P(None, None, None, "mp"),
            rep,
            P(None, None, "mp"),
            rep,
            rep,
            rep,
            rep,
            rep,
            rep,
            rep,
            rep,
            P(None, "mp"),
            P(None, "mp"),
            rep,
            P("mp"),
            P(None, None, "mp"),
            P(None, None, "mp"),
            P(None, None, "mp"),
        ),
        check_vma=False,
    )
```

```python
import functools
import math

import jax
import jax.numpy as jnp
from jax import lax
from jax.experimental import pallas as pl
from jax.experimental.pallas import tpu as pltpu
from jax.sharding import PartitionSpec as P

E = 1024
H = 1024
V = 10240
NH = 128
Z = 64
STEP = 10
LANES = 128
ROW_TILE = 16
VMEM_BYTES = 56 * 1024 * 1024

EPS_NORM = 1e-05
EPS_FACT = 1e-30

F32 = jnp.float32
BF16 = jnp.bfloat16


def matmul(left, right):
    return jnp.dot(left, right, preferred_element_type=F32)


def dot_last(left, right):
    return lax.dot_general(left, right, (((1,), (1,)), ((), ())), preferred_element_type=F32)


def dot_first(left, right):
    return lax.dot_general(left, right, (((0,), (0,)), ((), ())), preferred_element_type=F32)


def adafactor(weight, grad, row_old, col_old, row_mean, col_mean, lead, rate):
    decay = 1.0 - STEP ** (-0.8)
    row_new = decay * row_old + (1.0 - decay) * row_mean
    col_new = decay * col_old + (1.0 - decay) * col_mean
    relative = row_new / jnp.mean(row_new, axis=-1, keepdims=True)
    relative = relative.reshape(relative.shape + (1,) * (grad.ndim - relative.ndim))
    spread = col_new[None] if lead == 0 else col_new[:, None]
    updated = weight - rate * grad * lax.rsqrt(relative * spread)
    return (grad, updated, row_new, col_new)


STACK_ROWS = 2304
SCALE_AT = 2 * E
VEC_AT = SCALE_AT + 3 * Z
TAIL_ROWS = STACK_ROWS - SCALE_AT
PACK = H + NH + 4 * Z
STAT_AT = 3 * Z
VOCAB_BLOCK = 256
SLOTS = (0, 2, 4, 6, 1, 3, 5, 7)


def swap(values, axis, size, bit):
    return lax.ppermute(values, axis, [(i, i ^ bit) for i in range(size)])


def tree_sum(values, axis, size):
    if size & (size - 1):
        return lax.psum(values, axis)
    bit = 1
    while bit < size:
        values = values + swap(values, axis, size, bit)
        bit *= 2
    return values


def tie(*values):
    return lax.optimization_barrier(values)


def weight_tail(w_scale, main_vectors):
    width = 4 * main_vectors.shape[2]
    vec = main_vectors.reshape(2, width)
    terms = []
    for _ in range(3):
        term = lax.reduce_precision(vec, 8, 7)
        terms.append(term.astype(BF16))
        vec = vec - term
    return jnp.concatenate(
        [w_scale.astype(BF16).reshape(3 * Z, width)]
        + terms
        + [jnp.zeros((STACK_ROWS - VEC_AT - 6, width), BF16)],
        axis=0,
    )


def piece_copies(refs, plan, main_v, sem, only=None):
    if plan is None:
        return [] if only else [(True, lambda: pltpu.make_async_copy(refs[0], main_v, sem.at[0]))]
    me = lax.axis_index("mp")
    b = lax.axis_index("batch")
    quarter = SCALE_AT // 4
    tail_quarter = TAIL_ROWS // 4
    copies = []

    def add(early, bits, ref, source, target, rows, spot):
        def copy():
            return pltpu.make_async_copy(
                ref.at[pl.ds(source, rows)],
                main_v.at[me ^ bits, pl.ds(target, rows)],
                sem.at[spot],
            )

        copies.append((early, copy))

    for number, (ref, (bits, over, first, rows)) in enumerate(zip(refs, plan)):
        if only is not None and bits != only:
            continue
        spot = 2 * number
        if over is None and rows == SCALE_AT:
            add(True, bits, ref, 0, 0, E, spot)
            add(False, bits, ref, E, E, H, spot + 1)
            continue
        if over is None:
            add(True, bits, ref, 0, first, rows, spot)
            continue
        index = b ^ over
        of_main = max(0, min(rows, quarter - first))
        if of_main:
            start = pl.multiple_of(index * quarter + first, ROW_TILE)
            add(index < 2, bits, ref, 0, start, of_main, spot)
        if rows > of_main:
            start = SCALE_AT + index * tail_quarter + first + of_main - quarter
            add(True, bits, ref, of_main, pl.multiple_of(start, ROW_TILE), rows - of_main, spot + 1)
    return copies


def each_copy(copies, early, act):
    for needed, copy in copies:
        if isinstance(needed, bool):
            if needed == early:
                act(copy())
        else:

            @pl.when(needed if early else jnp.logical_not(needed))
            def _():
                act(copy())


def copy_count(plan):
    return 1 if plan is None else 2 * len(plan)


def load_vectors(vec_ref, main_v):
    for m in range(main_v.shape[0]):
        terms = main_v[m, VEC_AT : VEC_AT + ROW_TILE].astype(F32)
        vec_ref[m] = terms[0:2] + terms[2:4] + terms[4:6]


def masked_thirds(z_wide):
    lane = lax.broadcasted_iota(jnp.int32, z_wide.shape, 1) // Z
    zero = jnp.zeros_like(z_wide)
    return jnp.concatenate([jnp.where(lane == k, z_wide, zero) for k in range(3)], axis=0)


def beside(wide, columns):
    lane = lax.broadcasted_iota(jnp.int32, wide.shape, 1)
    count = len(columns)
    for spot, column in enumerate(columns):
        high = column.astype(BF16).astype(F32)
        wide = jnp.where(lane == STAT_AT + spot, high, wide)
        wide = jnp.where(lane == STAT_AT + count + spot, column - high, wide)
    return wide.astype(BF16)


def column_of(wide, count, spot):
    return wide[:, STAT_AT + spot : STAT_AT + spot + 1] + wide[
        :, STAT_AT + count + spot : STAT_AT + count + spot + 1
    ]


def forward_kernel(plan, x_ref, hyp_ref, hypb_ref, zp_ref, zpb_ref, *refs):
    n_pieces = 1 if plan is None else len(plan)
    forward_body(plan, x_ref, hyp_ref, hypb_ref, zp_ref, zpb_ref, refs[:n_pieces], *refs[n_pieces:])


def forward_body(
    plan, x_ref, hyp_ref, hypb_ref, zp_ref, zpb_ref, piece_refs,
    pack_out, cprev_out, tc_out, hcprev_out, thc_out, hg_out,
    ux_out, uh_out, one0_out, one1_out, n_out, act_out, rstd_out, vec_out,
    main_v, prex_s, h_s, c_s, hh_s, hc_s, sem,
):
    t = pl.program_id(0)
    nb, _, bw = main_v.shape
    bu = bw // 4
    steps, _, rows, _ = ux_out.shape

    @pl.when(t == 0)
    def _():
        pieces = piece_copies(piece_refs, plan, main_v, sem)
        for early in (True, False):
            each_copy(pieces, early, lambda copy: copy.start())
        prex_s[...] = (matmul(x_ref[...], hyp_ref[:E]) + hypb_ref[...]).reshape(steps, rows, 4 * NH)
        h_s[...] = jnp.zeros_like(h_s)
        c_s[...] = jnp.zeros_like(c_s)
        hh_s[...] = jnp.zeros_like(hh_s)
        hc_s[...] = jnp.zeros_like(hc_s)
        me = 0 if plan is None else lax.axis_index("mp")
        for bits in range(nb):
            each_copy(piece_copies(piece_refs, plan, main_v, sem, bits), True, lambda copy: copy.wait())
            m = me ^ bits
            ux = matmul(x_ref[...], main_v[m, :E])
            ux_out[:, m] = ux.reshape(steps, rows, bw)
        load_vectors(vec_out, main_v)
        uh_out[...] = jnp.zeros_like(uh_out)

    @pl.when(t == 1)
    def _():
        each_copy(piece_copies(piece_refs, plan, main_v, sem), False, lambda copy: copy.wait())

    h_prev = h_s[...]

    @pl.when(t > 0)
    def _():
        for m in range(nb):
            uh_out[0, m] = matmul(h_prev, main_v[m, E : 2 * E])

    hh_prev = hh_s[...]
    hc_prev = hc_s[...]
    q = prex_s[t] + matmul(h_prev, hyp_ref[E : E + H]) + matmul(hh_prev, hyp_ref[E + H : E + H + NH])
    q_in = jax.nn.sigmoid(q[:, :NH])
    q_forget = jax.nn.sigmoid(q[:, NH : 2 * NH])
    q_out = jax.nn.sigmoid(q[:, 2 * NH : 3 * NH])
    q_cell = jnp.tanh(q[:, 3 * NH :])
    hc = q_forget * hc_prev + q_in * q_cell
    thc = jnp.tanh(hc)
    hh = (q_out * thc).astype(BF16)
    z_wide = matmul(hh, zp_ref[...]) + zpb_ref[...]
    hcprev_out[0] = hc_prev
    thc_out[0] = thc
    hg_out[0, :, :NH] = q_in
    hg_out[0, :, NH : 2 * NH] = q_forget
    hg_out[0, :, 2 * NH : 3 * NH] = q_out
    hg_out[0, :, 3 * NH :] = q_cell
    pack_out[0, :, H : H + NH] = hh
    hh_s[...] = hh
    hc_s[...] = hc

    thirds = masked_thirds(z_wide.astype(BF16))
    sums = [jnp.zeros((rows, LANES), F32) for _ in range(4)]
    squares = [jnp.zeros((rows, LANES), F32) for _ in range(4)]
    for m in range(nb):
        scl = matmul(thirds, main_v[m, SCALE_AT:])
        uh = uh_out[0, m]
        one0 = 1.0 + scl[:rows]
        one1 = 1.0 + scl[rows : 2 * rows]
        s = one0 * uh + one1 * ux_out[t, m]
        one0_out[0, m] = one0
        one1_out[0, m] = one1
        act_out[0, m] = scl[2 * rows :]
        n_out[0, m] = s
        for g in range(4):
            for j in range(bu // LANES):
                piece = s[:, g * bu + j * LANES : g * bu + (j + 1) * LANES]
                sums[g] += piece
                squares[g] += piece * piece
    centres, rstds = [], []
    for g in range(4):
        centre = jnp.sum(sums[g], axis=1, keepdims=True) / H
        square = jnp.sum(squares[g], axis=1, keepdims=True) / H
        rstd = lax.rsqrt(square - centre * centre + EPS_NORM)
        centres.append(centre)
        rstds.append(rstd)
        rstd_out[0, :, g * LANES : (g + 1) * LANES] = jnp.broadcast_to(rstd, (rows, LANES))
    pack_out[0, :, H + NH :] = beside(z_wide, centres + rstds)

    for m in range(nb):
        cols = slice(m * bu, (m + 1) * bu)
        gates = []
        for g in range(4):
            here = slice(g * bu, (g + 1) * bu)
            n = (n_out[0, m, :, here] - centres[g]) * rstds[g]
            n_out[0, m, :, here] = n
            pre = vec_out[m, 0:1, here] * n + vec_out[m, 1:2, here] + act_out[0, m, :, here]
            gate = jnp.tanh(pre) if g == 3 else jax.nn.sigmoid(pre)
            act_out[0, m, :, here] = gate
            gates.append(gate)
        c_prev = c_s[:, cols]
        c_now = gates[1] * c_prev + gates[0] * gates[3]
        tc = jnp.tanh(c_now)
        h_now = (gates[2] * tc).astype(BF16)
        cprev_out[0, :, cols] = c_prev
        tc_out[0, :, cols] = tc
        c_s[:, cols] = c_now
        h_s[:, cols] = h_now
        pack_out[0, :, cols] = h_now


def turn_kernel(plan, me_ref, *refs):
    n_pieces = 1 if plan is None else len(plan)
    in_out, rec_out, tail_out, main_v, sem = refs[n_pieces:]
    step = pl.program_id(0)

    @pl.when(step == 0)
    def _():
        for _, copy in piece_copies(refs[:n_pieces], plan, main_v, sem):
            copy().start()

    for bits in range(main_v.shape[0]):

        @pl.when(step == bits)
        def _():
            for _, copy in piece_copies(refs[:n_pieces], plan, main_v, sem, bits):
                copy().wait()

    m = step ^ me_ref[0]
    in_out[0] = main_v[m, :E]
    rec_out[0] = main_v[m, E : 2 * E].T
    tail_out[0] = main_v[m, SCALE_AT:].T


def run_turn(blocks, plan, pieces):
    nb, bw = blocks
    me = jnp.zeros((1,), jnp.int32) if plan is None else lax.axis_index("mp").reshape(1)
    shapes = [(E, bw), (bw, H), (bw, TAIL_ROWS)]
    single = dict(pipeline_mode=pl.Buffered(1)) if nb == 1 else {}
    return pl.pallas_call(
        functools.partial(turn_kernel, plan),
        grid_spec=pltpu.PrefetchScalarGridSpec(
            num_scalar_prefetch=1,
            grid=(nb,),
            in_specs=[pl.BlockSpec(memory_space=pl.ANY)] * len(pieces),
            out_specs=[
                pl.BlockSpec((1,) + shape, lambda i, me: (i ^ me[0], 0, 0), **single) for shape in shapes
            ],
            scratch_shapes=[
                pltpu.VMEM((nb, STACK_ROWS, bw), BF16),
                pltpu.SemaphoreType.DMA((copy_count(plan),)),
            ],
        ),
        out_shape=[jax.ShapeDtypeStruct((nb,) + shape, BF16) for shape in shapes],
        compiler_params=kernel_params(),
        cost_estimate=pl.CostEstimate(flops=10**7, bytes_accessed=40_000_000, transcendentals=0),
        name="turn_weights",
    )(me, *pieces)


def backward_kernel(
    plan, in_hbm, rec_hbm, tail_hbm, dh_ref, hyp_ref, zp_ref,
    cprev_ref, tc_ref, hcprev_ref, thc_ref, hg_ref,
    ux_ref, uh_ref, one0_ref, one1_ref, n_ref, act_ref, rstd_ref, vec_ref,
    cols_out, odd_out, back_out, dx_out, gv_out,
    in_v, rec_v, tail_v, dh_s, dc_s, dhh_s, dhc_s, da_s, stack_s, dux_s, dq_s, sem,
):
    step = pl.program_id(0)
    nb, _, bw = in_v.shape
    bu = bw // 4
    steps, rows, _ = dq_s.shape
    t = steps - 1 - step
    me = 0 if plan is None else lax.axis_index("mp")

    def by_core(bits, keep):
        @pl.when(bits % 2 == 0)
        def _():
            keep(cols_out, bits // 2)

        @pl.when(bits % 2 == 1)
        def _():
            keep(odd_out, bits // 2)

    copies = [
        pltpu.make_async_copy(source, target, sem.at[spot])
        for spot, (source, target) in enumerate(((rec_hbm, rec_v), (tail_hbm, tail_v), (in_hbm, in_v)))
    ]

    @pl.when(step == 0)
    def _():
        for copy in copies:
            copy.start()
        dh_s[...] = jnp.zeros_like(dh_s)
        dc_s[...] = jnp.zeros_like(dc_s)
        dhh_s[...] = jnp.zeros_like(dhh_s)
        dhc_s[...] = jnp.zeros_like(dhc_s)
        gv_out[...] = jnp.zeros_like(gv_out)

    first = [jnp.zeros((rows, LANES), F32) for _ in range(4)]
    second = [jnp.zeros((rows, LANES), F32) for _ in range(4)]
    for m in range(nb):
        cols = slice(m * bu, (m + 1) * bu)
        gate = [act_ref[0, m, :, g * bu : (g + 1) * bu] for g in range(4)]
        tc = tc_ref[0, :, cols]
        dh = dh_ref[0, :, cols] + dh_s[:, cols]
        dc = dc_s[:, cols] + dh * gate[2] * (1.0 - tc * tc)
        da = [
            dc * gate[3] * gate[0] * (1.0 - gate[0]),
            dc * cprev_ref[0, :, cols] * gate[1] * (1.0 - gate[1]),
            dh * tc * gate[2] * (1.0 - gate[2]),
            dc * gate[0] * (1.0 - gate[3] * gate[3]),
        ]
        dc_s[:, cols] = dc * gate[1]
        if plan is not None:
            low = dh.astype(BF16)

            def keep_dh(ref, spot):
                ref[spot, t, :, :bu] = low

            by_core(me ^ m, keep_dh)
        for g in range(4):
            here = slice(g * bu, (g + 1) * bu)
            n = n_ref[0, m, :, here]
            da_s[m, :, here] = da[g]
            if plan is None:
                gv_out[m, 0:1, here] += jnp.sum(da[g] * n, axis=0, keepdims=True)
                gv_out[m, 1:2, here] += jnp.sum(da[g], axis=0, keepdims=True)
            dn = vec_ref[m, 0:1, here] * da[g]
            dnn = dn * n
            for j in range(bu // LANES):
                first[g] += dn[:, j * LANES : (j + 1) * LANES]
                second[g] += dnn[:, j * LANES : (j + 1) * LANES]
    means = [
        (jnp.sum(first[g], axis=1, keepdims=True) / H, jnp.sum(second[g], axis=1, keepdims=True) / H)
        for g in range(4)
    ]

    for m in range(nb):
        ds_parts = []
        for g in range(4):
            here = slice(g * bu, (g + 1) * bu)
            dn = vec_ref[m, 0:1, here] * da_s[m, :, here]
            rstd = rstd_ref[0, :, g * LANES : g * LANES + 1]
            ds_parts.append(rstd * (dn - means[g][0] - n_ref[0, m, :, here] * means[g][1]))
        ds = jnp.concatenate(ds_parts, axis=1)
        da_low = da_s[m].astype(BF16)
        if plan is None:
            cols_out[m, t, :, :bw] = ds.astype(BF16)
            cols_out[m, t, :, bw:] = da_low
        stack_s[m, :rows] = (ds * uh_ref[0, m]).astype(BF16)
        stack_s[m, rows : 2 * rows] = (ds * ux_ref[0, m]).astype(BF16)
        stack_s[m, 2 * rows : 3 * rows] = da_low
        stack_s[m, 3 * rows :] = (ds * one0_ref[0, m]).astype(BF16)
        dux_s[t, m] = (ds * one1_ref[0, m]).astype(BF16)

    @pl.when(step == 0)
    def _():
        copies[0].wait()
        copies[1].wait()

    dz_all = jnp.zeros((3 * rows, 4 * Z), F32)
    dh_rec = jnp.zeros((rows, H), F32)
    for m in range(nb):
        dz_all += matmul(stack_s[m, : 3 * rows], tail_v[m])
    for m in range(nb):
        dh_rec += matmul(stack_s[m, 3 * rows :], rec_v[m])

    lane = lax.broadcasted_iota(jnp.int32, (rows, 4 * Z), 1) // Z
    dz = jnp.zeros((rows, 4 * Z), F32)
    for k in range(3):
        dz = jnp.where(lane == k, dz_all[k * rows : (k + 1) * rows], dz)
    half = 2 * NH
    back_out[2, t] = beside(dz, [m[0] for m in means] + [m[1] for m in means])
    q_in = hg_ref[0, :, :NH]
    q_forget = hg_ref[0, :, NH : 2 * NH]
    q_out = hg_ref[0, :, 2 * NH : 3 * NH]
    q_cell = hg_ref[0, :, 3 * NH :]
    thc = thc_ref[0]
    dhh = dhh_s[...] + dot_last(dz.astype(BF16), zp_ref[...])
    dhc = dhc_s[...] + dhh * q_out * (1.0 - thc * thc)
    dq = jnp.concatenate(
        [
            dhc * q_cell * q_in * (1.0 - q_in),
            dhc * hcprev_ref[0] * q_forget * (1.0 - q_forget),
            dhh * thc * q_out * (1.0 - q_out),
            dhc * q_in * (1.0 - q_cell * q_cell),
        ],
        axis=1,
    ).astype(BF16)
    back_out[0, t] = dq[:, :half]
    back_out[1, t] = dq[:, half:]
    dq_s[t] = dq
    dhc_s[...] = dhc * q_forget
    dhh_s[...] = dot_last(dq, hyp_ref[E + H : E + H + NH])
    dh_s[...] = dh_rec + dot_last(dq, hyp_ref[E : E + H])

    @pl.when(step == steps - 1)
    def _():
        copies[2].wait()
        dx = dot_last(dq_s[...].reshape(steps * rows, 4 * NH), hyp_ref[:E])
        for m in range(nb):
            dx += dot_last(dux_s[:, m].reshape(steps * rows, bw), in_v[m])
        if plan is None:
            dx_out[...] = dx.astype(dx_out.dtype)
        else:
            for m in range(nb):
                part = dx[:, m * bu : (m + 1) * bu].astype(BF16).reshape(steps, rows, bu)

                def keep_dx(ref, spot):
                    ref[spot, :, :, bu : 2 * bu] = part

                by_core(me ^ m, keep_dx)


def whole(shape):
    return pl.BlockSpec(shape, lambda t: (0,) * len(shape), pipeline_mode=pl.Buffered(1))


def kernel_params():
    return pltpu.CompilerParams(vmem_limit_bytes=VMEM_BYTES)


def run_forward(x_rows, blocks, plan, pieces, hyp_low, hyp_bias, zp_wide, zp_bias, steps):
    nb, bw = blocks
    rows = x_rows.shape[0] // steps

    def stepped(*tail):
        return pl.BlockSpec((1,) + tail, lambda t: (t,) + (0,) * len(tail))

    tails = [
        (BF16, (rows, PACK)), (F32, (rows, H)), (F32, (rows, H)), (F32, (rows, NH)), (F32, (rows, NH)),
        (F32, (rows, 4 * NH)), (F32, (nb, rows, bw)), (F32, (nb, rows, bw)), (F32, (nb, rows, bw)),
        (F32, (nb, rows, bw)), (F32, (nb, rows, bw)), (F32, (nb, rows, bw)), (F32, (rows, 4 * LANES)),
    ]
    out_specs = [stepped(*tail) for _, tail in tails]
    out_specs[6] = pl.BlockSpec((steps, nb, rows, bw), lambda t: (0, 0, 0, 0))
    out_shape = [jax.ShapeDtypeStruct((steps,) + tail, dtype) for dtype, tail in tails]
    work = steps * rows * 4 * H * (2 * H + E + 3 * 4 * Z)
    return pl.pallas_call(
        functools.partial(forward_kernel, plan),
        grid=(steps,),
        in_specs=[
            whole(x_rows.shape),
            whole(hyp_low.shape),
            whole(hyp_bias.shape),
            whole(zp_wide.shape),
            whole(zp_bias.shape),
        ]
        + [pl.BlockSpec(memory_space=pl.ANY)] * len(pieces),
        out_specs=out_specs + [pl.BlockSpec((nb, 2, bw), lambda t: (0, 0, 0))],
        out_shape=out_shape + [jax.ShapeDtypeStruct((nb, 2, bw), F32)],
        scratch_shapes=[
            pltpu.VMEM((nb, STACK_ROWS, bw), BF16),
            pltpu.VMEM((steps, rows, 4 * NH), F32),
            pltpu.VMEM((rows, H), BF16),
            pltpu.VMEM((rows, H), F32),
            pltpu.VMEM((rows, NH), BF16),
            pltpu.VMEM((rows, NH), F32),
            pltpu.SemaphoreType.DMA((copy_count(plan),)),
        ],
        compiler_params=kernel_params(),
        cost_estimate=pl.CostEstimate(flops=2 * work, bytes_accessed=40_000_000, transcendentals=0),
        name="recurrence_forward",
    )(x_rows, hyp_low, hyp_bias, zp_wide, zp_bias, *pieces)


def run_backward(dh_top, blocks, plan, turned, hyp_low, zp_wide, kept):
    nb, bw = blocks
    steps, rows, _ = dh_top.shape

    def stepped(*tail):
        return pl.BlockSpec((1,) + tail, lambda s: (steps - 1 - s,) + (0,) * len(tail))

    def still(shape):
        return pl.BlockSpec(shape, lambda s: (0,) * len(shape))

    tails = [
        (rows, H), (rows, H), (rows, NH), (rows, NH), (rows, 4 * NH), (nb, rows, bw), (nb, rows, bw),
        (nb, rows, bw), (nb, rows, bw), (nb, rows, bw), (nb, rows, bw), (rows, 4 * LANES),
    ]
    per_owner = 2 * bw if plan is None else 2 * (bw // 4)
    outs = [
        jax.ShapeDtypeStruct((nb if plan is None else nb // 2, steps, rows, per_owner), BF16),
        jax.ShapeDtypeStruct((1 if plan is None else nb // 2, steps, rows, per_owner), BF16),
        jax.ShapeDtypeStruct((3, steps, rows, 2 * NH), BF16),
        jax.ShapeDtypeStruct((steps * rows, E), BF16),
        jax.ShapeDtypeStruct((nb, 2, bw), F32),
    ]
    work = steps * rows * 4 * H * (2 * H + E + 3 * 4 * Z)
    return pl.pallas_call(
        functools.partial(backward_kernel, plan),
        grid=(steps,),
        in_specs=[pl.BlockSpec(memory_space=pl.ANY)] * len(turned)
        + [stepped(rows, H), whole(hyp_low.shape), whole(zp_wide.shape)]
        + [stepped(*tail) for tail in tails]
        + [whole((nb, 2, bw))],
        out_specs=[
            still(out.shape) for out in outs
        ],
        out_shape=outs,
        scratch_shapes=[
            pltpu.VMEM((nb, E, bw), BF16),
            pltpu.VMEM((nb, bw, H), BF16),
            pltpu.VMEM((nb, bw, TAIL_ROWS), BF16),
            pltpu.VMEM((rows, H), F32),
            pltpu.VMEM((rows, H), F32),
            pltpu.VMEM((rows, NH), F32),
            pltpu.VMEM((rows, NH), F32),
            pltpu.VMEM((nb, rows, bw), F32),
            pltpu.VMEM((nb, 4 * rows, bw), BF16),
            pltpu.VMEM((steps, nb, rows, bw), BF16),
            pltpu.VMEM((steps, rows, 4 * NH), BF16),
            pltpu.SemaphoreType.DMA((3,)),
        ],
        compiler_params=kernel_params(),
        cost_estimate=pl.CostEstimate(flops=2 * work, bytes_accessed=60_000_000, transcendentals=0),
        name="recurrence_backward",
    )(*turned, dh_top, hyp_low, zp_wide, *kept)


def column_forward_kernel(
    steps, slots_ref, pack0_ref, pack1_ref, x0_ref, x1_ref, main_ref, tail_ref, vec_ref,
    uh_out, ux_out, one0_out, one1_out, n_out, act_out, cprev_out, tc_out, rstd_out,
    left_out, x_out, hb_out, hhb_out, hh_out, z_out,
):
    _, total, _ = pack0_ref.shape
    rows = total // steps
    width = main_ref.shape[1]
    units = width // 4

    def one_before(values):
        return jnp.concatenate([jnp.zeros_like(values[:rows]), values[: total - rows]], axis=0)

    for half, (pack_ref, x_ref) in enumerate(((pack0_ref, x0_ref), (pack1_ref, x1_ref))):
        h_before = one_before(pack_ref[0, :, :H])
        hh = pack_ref[0, :, H : H + NH]
        z_wide = pack_ref[0, :, H + NH :]
        x_now = jnp.concatenate([x_ref[k, 0] for k in range(x_ref.shape[0])], axis=1)
        mine = pl.ds(pl.multiple_of(slots_ref[0] * units, units), units)
        part = x_ref.shape[3]
        left_out[half, 0, :, :part] = x_ref[slots_ref[0], 0]
        left_out[half, 0, :, part:] = one_before(pack_ref[0, :, mine])
        x_out[half, 0] = x_now
        hb_out[half, 0] = h_before
        hhb_out[half, 0] = one_before(hh)
        hh_out[half, 0] = hh
        z_out[half, 0] = z_wide
        stats = z_wide.astype(F32)
        uh = matmul(h_before, main_ref[E : 2 * E])
        ux = matmul(x_now, main_ref[:E])
        scl = matmul(masked_thirds(z_wide), tail_ref[...])
        one0 = 1.0 + scl[:total]
        one1 = 1.0 + scl[total : 2 * total]
        s = one0 * uh + one1 * ux
        uh_out[half, 0] = uh
        ux_out[half, 0] = ux
        one0_out[half, 0] = one0
        one1_out[half, 0] = one1
        for g in range(4):
            here = slice(g * units, (g + 1) * units)
            rstd = column_of(stats, 8, 4 + g)
            n = (s[:, here] - column_of(stats, 8, g)) * rstd
            pre = vec_ref[0:1, here] * n + vec_ref[1:2, here] + scl[2 * total :, here]
            n_out[half, 0, :, here] = n
            act_out[half, 0, :, here] = jnp.tanh(pre) if g == 3 else jax.nn.sigmoid(pre)
            rstd_out[half, 0, :, here] = jnp.broadcast_to(rstd, (total, units))
        c = jnp.zeros((rows, units), F32)
        for t in range(steps):
            now = slice(t * rows, (t + 1) * rows)
            gate = [act_out[half, 0, now, g * units : (g + 1) * units] for g in range(4)]
            cprev_out[half, 0, now] = c
            c = gate[1] * c + gate[0] * gate[3]
            tc_out[half, 0, now] = jnp.tanh(c)


def column_backward_kernel(
    steps, dh0_ref, dh1_ref, back0_ref, back1_ref, vec_ref,
    uh_ref, ux_ref, one0_ref, one1_ref, n_ref, act_ref, cprev_ref, tc_ref, rstd_ref,
    dux_out, duh_out, d0_out, d1_out, da_out, gv_out,
    dc_s,
):
    _, total, units = dh0_ref.shape
    rows = total // steps

    @pl.when(pl.program_id(0) == 0)
    def _():
        gv_out[...] = jnp.zeros_like(gv_out)

    for half, (dh_ref, back_ref) in enumerate(((dh0_ref, back0_ref), (dh1_ref, back1_ref))):
        means = back_ref[0, 0].astype(F32)
        dh = dh_ref[0].astype(F32)
        gate = [act_ref[half, 0, :, g * units : (g + 1) * units] for g in range(4)]
        tc = tc_ref[half, 0]
        local = dh * gate[2] * (1.0 - tc * tc)
        dc = jnp.zeros((rows, units), F32)
        for t in reversed(range(steps)):
            now = slice(t * rows, (t + 1) * rows)
            dc = dc + local[now]
            dc_s[now] = dc
            dc = dc * gate[1][now]
        dc = dc_s[...]
        da = [
            dc * gate[3] * gate[0] * (1.0 - gate[0]),
            dc * cprev_ref[half, 0] * gate[1] * (1.0 - gate[1]),
            dh * tc * gate[2] * (1.0 - gate[2]),
            dc * gate[0] * (1.0 - gate[3] * gate[3]),
        ]
        for g in range(4):
            here = slice(g * units, (g + 1) * units)
            n = n_ref[half, 0, :, here]
            gv_out[0:1, here] += jnp.sum(da[g] * n, axis=0, keepdims=True)
            gv_out[1:2, here] += jnp.sum(da[g], axis=0, keepdims=True)
            dn = vec_ref[0:1, here] * da[g]
            ds = rstd_ref[half, 0, :, here] * (
                dn - column_of(means, 8, g) - n * column_of(means, 8, 4 + g)
            )
            dux_out[half, 0, :, here] = (ds * one1_ref[half, 0, :, here]).astype(BF16)
            duh_out[half, 0, :, here] = (ds * one0_ref[half, 0, :, here]).astype(BF16)
            d0_out[half, 0, :, here] = (ds * uh_ref[half, 0, :, here]).astype(BF16)
            d1_out[half, 0, :, here] = (ds * ux_ref[half, 0, :, here]).astype(BF16)
            da_out[half, 0, :, here] = da[g].astype(BF16)


def half_specs(total, width):
    return [pl.BlockSpec((1, total, width), lambda i, at=at: (i + at, 0, 0)) for at in (0, 4)]


def run_column_forward(slots, near, rest, x_all, main_own, tail_own, vec, steps):
    per_core, total, _ = near.shape
    n_parts, owners, _, emb_part = x_all.shape
    width = main_own.shape[1]
    units = width // 4
    tails = [(F32, width)] * 6 + [(F32, units)] * 2 + [(F32, width)]
    tails += [(BF16, emb_part + units), (BF16, E), (BF16, H), (BF16, NH), (BF16, NH), (BF16, 4 * Z)]

    def still(shape):
        return pl.BlockSpec(shape, lambda i, slots: (0,) * len(shape), pipeline_mode=pl.Buffered(1))

    return pl.pallas_call(
        functools.partial(column_forward_kernel, steps),
        grid_spec=pltpu.PrefetchScalarGridSpec(
            num_scalar_prefetch=1,
            grid=(per_core,),
            in_specs=[pl.BlockSpec((1, total, PACK), lambda i, slots: (i, 0, 0))] * 2
            + [
                pl.BlockSpec(
                    (n_parts, 1, total, emb_part), lambda i, slots, at=at: (0, slots[i + at], 0, 0)
                )
                for at in (0, per_core)
            ]
            + [still(main_own.shape), still(tail_own.shape), still(vec.shape)],
            out_specs=[
                pl.BlockSpec((2, 1, total, tail), lambda i, slots: (0, i, 0, 0)) for _, tail in tails
            ],
        ),
        out_shape=[jax.ShapeDtypeStruct((2, per_core, total, tail), dtype) for dtype, tail in tails],
        compiler_params=kernel_params(),
        cost_estimate=pl.CostEstimate(
            flops=2 * owners * total * width * 3 * H, bytes_accessed=18_000_000, transcendentals=0
        ),
        name="column_forward",
    )(slots, near, rest, x_all, x_all, main_own, tail_own, vec)


def run_column_backward(moved, back_all, vec, kept, steps):
    owners, total, _ = moved.shape
    width = vec.shape[1]
    units = width // 4
    widths = [width] * 6 + [units] * 2 + [width]
    return pl.pallas_call(
        functools.partial(column_backward_kernel, steps),
        grid=(owners // 2,),
        in_specs=half_specs(total, units)
        + [
            pl.BlockSpec((1, 1, total, 4 * Z), lambda i, at=at: (i + at, 2, 0, 0)) for at in (0, 4)
        ]
        + [whole(vec.shape)]
        + [pl.BlockSpec((2, 1, total, tail), lambda i: (0, i, 0, 0)) for tail in widths],
        out_specs=[pl.BlockSpec((2, 1, total, width), lambda i: (0, i, 0, 0))] * 5
        + [pl.BlockSpec((2, width), lambda i: (0, 0))],
        out_shape=[jax.ShapeDtypeStruct((2, owners // 2, total, width), BF16)] * 5
        + [jax.ShapeDtypeStruct((2, width), F32)],
        scratch_shapes=[pltpu.VMEM((total, units), F32)],
        compiler_params=kernel_params(),
        cost_estimate=pl.CostEstimate(
            flops=40 * owners * total * width, bytes_accessed=16_000_000, transcendentals=0
        ),
        name="column_backward",
    )(moved, moved, back_all, back_all, vec, *kept)


def table_kernel(
    me_ref, told_ref, r0_ref, r1_ref, r2_ref, r3_ref, table_out, row_out, col_out, rows_s, other_s
):
    count = rows_s.shape[0] // 4
    stride = told_ref.shape[0] // 4
    table_out[...] = jnp.zeros_like(table_out)
    other_s[...] = jnp.zeros_like(other_s)
    for part, ref in enumerate((r0_ref, r1_ref, r2_ref, r3_ref)):
        rows_s[part * count : (part + 1) * count] = ref[:count].astype(F32)

    for owner in range(4):
        part = owner ^ me_ref[0]

        @pl.loop(0, count // 32)
        def _(group):
            for lane in range(32):
                here = pl.ds(told_ref[part * stride + group * 32 + lane], 1)
                table = table_out if lane % 2 == 0 else other_s
                table[here] += rows_s[pl.ds(part * count + group * 32 + lane, 1)]

    def measure(block, cols):
        here = pl.ds(pl.multiple_of(block * VOCAB_BLOCK, VOCAB_BLOCK), VOCAB_BLOCK)
        values = table_out[here] + other_s[here]
        table_out[here] = values
        squares = values * values + EPS_FACT
        high = squares.astype(BF16)
        low = (squares - high.astype(F32)).astype(BF16)
        ones = jnp.ones((8, squares.shape[1]), BF16)
        sums = dot_last(ones, high) + dot_last(ones, low)
        row_out[pl.ds(block, 1)] = sums[:1]
        return cols + jnp.sum(squares, axis=0, keepdims=True)

    zero = jnp.zeros((1, table_out.shape[1]), F32)
    col_out[...] = lax.fori_loop(0, row_out.shape[0], measure, zero)


def run_table(me, told, parts, vocab):
    count, lanes = parts[0].shape
    total = count * len(parts)
    blocks = vocab // VOCAB_BLOCK
    return pl.pallas_call(
        table_kernel,
        grid_spec=pltpu.PrefetchScalarGridSpec(
            num_scalar_prefetch=2,
            grid=(1,),
            in_specs=[pl.BlockSpec(part.shape, lambda i, *_: (0, 0)) for part in parts],
            out_specs=[
                pl.BlockSpec((vocab, lanes), lambda i, *_: (0, 0)),
                pl.BlockSpec((blocks, VOCAB_BLOCK), lambda i, *_: (0, 0)),
                pl.BlockSpec((1, lanes), lambda i, *_: (0, 0)),
            ],
            scratch_shapes=[pltpu.VMEM((total, lanes), F32), pltpu.VMEM((vocab, lanes), F32)],
        ),
        out_shape=[
            jax.ShapeDtypeStruct((vocab, lanes), F32),
            jax.ShapeDtypeStruct((blocks, VOCAB_BLOCK), F32),
            jax.ShapeDtypeStruct((1, lanes), F32),
        ],
        compiler_params=kernel_params(),
        cost_estimate=pl.CostEstimate(flops=10**9, bytes_accessed=40_000_000, transcendentals=0),
        name="embedding_table",
    )(me, told, *parts)


def stepped_update(weight, grad, relative, spread, rate):
    return weight - rate * grad * lax.rsqrt(relative * spread)


def main_update_kernel(rate, me_ref, p0, p1, p2, p3, weight_ref, rel_ref, spread_ref, grad_out, new_out):
    quarter, part = pl.program_id(0), pl.program_id(1)
    lanes = weight_ref.shape[1]
    gates = spread_ref.shape[0]
    rows = weight_ref.shape[0] // gates
    for bits, ref in enumerate((p0, p1, p2, p3)):

        @pl.when(quarter == bits)
        def _():
            here = pl.ds(pl.multiple_of(part * rows, rows), rows)
            for g in range(gates):
                spot = pl.ds(g, rows, stride=gates)
                grad = ref[here, g * lanes : (g + 1) * lanes].astype(F32)
                grad_out[spot, :] = grad
                new_out[spot, :] = stepped_update(
                    weight_ref[spot, :], grad, rel_ref[...], spread_ref[g : g + 1], rate
                )


def run_main_update(me, parts, weight, rel_wide, spread, rate):
    total, gates, lanes = weight.shape
    rows = total // 8

    def place(quarter, part, me_ref):
        return (part * 4 + (me_ref[0] ^ quarter), 0)

    block = pl.BlockSpec((rows * gates, lanes), place)
    flat = jax.ShapeDtypeStruct((total * gates, lanes), F32)
    grad, new = pl.pallas_call(
        functools.partial(main_update_kernel, rate),
        grid_spec=pltpu.PrefetchScalarGridSpec(
            num_scalar_prefetch=1,
            grid=(4, 2),
            in_specs=[pl.BlockSpec(part.shape, lambda q, p, m: (0, 0)) for part in parts]
            + [
                block,
                pl.BlockSpec((rows, LANES), place),
                pl.BlockSpec(spread.shape, lambda q, p, m: (0, 0)),
            ],
            out_specs=[block, block],
        ),
        out_shape=[flat, flat],
        compiler_params=kernel_params(),
        cost_estimate=pl.CostEstimate(flops=10**7, bytes_accessed=16_000_000, transcendentals=0),
        name="main_update",
    )(me, *parts, weight.reshape(total * gates, lanes), rel_wide, spread)
    return grad.reshape(weight.shape), new.reshape(weight.shape)


def out_update_kernel(rate, seen_ref, weight_ref, rel_ref, spread_ref, grad_out, new_out):
    for j in range(grad_out.shape[1] // LANES):
        cols = slice(j * LANES, (j + 1) * LANES)
        grad = seen_ref[:, cols].astype(F32)
        grad_out[:, cols] = grad
        new_out[:, cols] = stepped_update(weight_ref[:, cols], grad, rel_ref[...], spread_ref[:, cols], rate)


def run_out_update(seen, weight, rel_wide, spread, rate):
    total, width = weight.shape
    rows = total // 4

    def rows_of(columns):
        return pl.BlockSpec((rows, columns), lambda i: (i, 0))

    return pl.pallas_call(
        functools.partial(out_update_kernel, rate),
        grid=(4,),
        in_specs=[rows_of(width), rows_of(width), rows_of(LANES), pl.BlockSpec(spread.shape, lambda i: (0, 0))],
        out_specs=[rows_of(width)] * 2,
        out_shape=[jax.ShapeDtypeStruct(weight.shape, F32)] * 2,
        compiler_params=kernel_params(),
        cost_estimate=pl.CostEstimate(flops=10**7, bytes_accessed=20_000_000, transcendentals=0),
        name="out_update",
    )(seen, weight, rel_wide, spread)


def factored_update(rate, grad_out, new_out, weight_ref, row_ref, col_ref, row_out, col_out):
    total, width = grad_out.shape
    decay = 1.0 - STEP ** (-0.8)
    blocks = [(at, min(256, total - at)) for at in range(0, total, 256)]
    cols = jnp.zeros((1, width), F32)
    sums = jnp.zeros((1, LANES), F32)
    for at, size in blocks:
        here = slice(at, at + size)
        grad = grad_out[here]
        squares = grad * grad + EPS_FACT
        cols += jnp.sum(squares, axis=0, keepdims=True)
        mean = jnp.sum(squares, axis=1, keepdims=True) / width
        row_new = decay * row_ref[here] + (1.0 - decay) * mean
        row_out[here] = row_new
        sums += jnp.sum(row_new, axis=0, keepdims=True)
    col_new = decay * col_ref[...] + (1.0 - decay) * (cols / total)
    col_out[...] = col_new
    average = sums / total
    for at, size in blocks:
        here = slice(at, at + size)
        relative = row_out[here] / average
        for start in range(0, width, LANES):
            lanes = slice(start, min(start + LANES, width))
            new_out[here, lanes] = stepped_update(
                weight_ref[here, lanes],
                grad_out[here, lanes],
                relative[:, : lanes.stop - start],
                col_new[:, lanes],
                rate,
            )


def hyper_update_kernel(
    rate, zed_rate, parts_ref, bias_ref, weight_ref, row_ref, col_ref,
    zed_bias_ref, zed_weight_ref, zed_row_ref, zed_col_ref,
    grad_out, new_out, row_out, col_out, zed_grad_out, zed_new_out, zed_row_out, zed_col_out,
):
    quarters, owners, _, _ = parts_ref.shape
    total = grad_out.shape[0]
    devices = quarters * owners
    heights = (E // devices, H // devices, NH // devices)
    zed_width = zed_grad_out.shape[1]
    for owner in range(owners):
        for quarter in range(quarters):
            part = parts_ref[quarter, owner].astype(F32)
            place = owner * quarters + quarter
            first, start = 0, 0
            for height, size in zip(heights, (E, H, NH)):
                to = start + place * height
                grad_out[to : to + height] = part[first : first + height]
                first += height
                start += size
            to = place * heights[2]
            zed_grad_out[to : to + heights[2]] = part[first : first + heights[2], :zed_width]
    zed_grad_out[NH:] = zed_bias_ref[...]
    grad_out[total - 1 :] = bias_ref[...]
    factored_update(rate, grad_out, new_out, weight_ref, row_ref, col_ref, row_out, col_out)
    factored_update(
        zed_rate, zed_grad_out, zed_new_out, zed_weight_ref, zed_row_ref, zed_col_ref, zed_row_out, zed_col_out
    )


def run_hyper_update(parts, hyper, zproj, rates):
    values = [*hyper, *zproj]

    def all_of(values):
        return pl.BlockSpec(values.shape, lambda i: (0,) * values.ndim)

    outs = []
    for _, weight, row, col in (hyper, zproj):
        outs += [weight, weight, row, col]
    return pl.pallas_call(
        functools.partial(hyper_update_kernel, *rates),
        grid=(1,),
        in_specs=[all_of(parts)] + [all_of(value) for value in values],
        out_specs=[all_of(out) for out in outs],
        out_shape=[jax.ShapeDtypeStruct(out.shape, F32) for out in outs],
        compiler_params=kernel_params(),
        cost_estimate=pl.CostEstimate(flops=10**7, bytes_accessed=20_000_000, transcendentals=0),
        name="hyper_update",
    )(parts, *values)


def updates(weights, states, grads, row_sums, embed_col_mean):
    embed, w_main, w_scale, w_hyper, w_zproj, w_out, main_vectors = weights
    (
        embed_row, embed_col, main_row, main_col, scale_row, scale_col, hyper_row, hyper_col,
        zproj_row, zproj_col, out_row, out_col, vector_state,
    ) = states
    g_embed, g_main, g_scale, g_hyper, g_zproj, g_out, g_vec = grads
    row_embed, row_main, row_scale, row_out = row_sums
    sq_main, sq_scale, sq_hyper, sq_zproj, sq_out = [
        g * g + EPS_FACT for g in (g_main, g_scale, g_hyper, g_zproj, g_out)
    ]
    res_embed = adafactor(
        embed, g_embed, embed_row, embed_col, row_embed / E, embed_col_mean, 0, 1.0
    )
    res_main = adafactor(
        w_main,
        g_main,
        main_row,
        main_col,
        row_main / (4 * H),
        jnp.mean(sq_main, axis=0),
        0,
        1.0 / math.sqrt(E),
    )
    res_scale = adafactor(
        w_scale,
        g_scale,
        scale_row,
        scale_col,
        row_scale / (4 * H),
        jnp.mean(sq_scale, axis=1),
        1,
        1.0 / math.sqrt(Z),
    )
    res_hyper = adafactor(
        w_hyper,
        g_hyper,
        hyper_row,
        hyper_col,
        jnp.mean(sq_hyper, axis=1),
        jnp.mean(sq_hyper, axis=0),
        0,
        1.0 / math.sqrt(E + H + NH + 1),
    )
    res_zproj = adafactor(
        w_zproj,
        g_zproj,
        zproj_row,
        zproj_col,
        jnp.mean(sq_zproj, axis=1),
        jnp.mean(sq_zproj, axis=0),
        0,
        2.0 / math.sqrt(NH),
    )
    res_out = adafactor(
        w_out, g_out, out_row, out_col, row_out / V, jnp.mean(sq_out, axis=0), 0, 3.0 / math.sqrt(H)
    )
    decay = 1.0 - STEP ** (-0.8)
    state_new = decay * vector_state + (1.0 - decay) * (g_vec * g_vec + EPS_FACT)
    vectors_new = main_vectors - 0.1 * g_vec * lax.rsqrt(state_new)
    return (
        res_embed
        + res_main
        + res_scale
        + res_hyper
        + res_zproj
        + res_out
        + (g_vec, state_new, vectors_new)
    )


def per_chip(
    parts,
    token_ids,
    seq_lengths,
    valid_mask,
    embed,
    w_main,
    w_scale,
    w_hyper,
    w_zproj,
    w_out,
    main_vectors,
    *states,
):
    n_mp, n_batch = parts
    my = lax.axis_index("mp")
    b = lax.axis_index("batch")
    units = w_main.shape[2]
    width = 4 * units
    emb_part = embed.shape[1]
    vocab_part = w_out.shape[1]
    batch_rows, steps = valid_mask.shape
    own = batch_rows // n_mp
    own_total = steps * own
    total = batch_rows * steps
    slots = my ^ jnp.array(SLOTS, jnp.int32)
    order = my ^ jnp.arange(n_mp, dtype=jnp.int32)
    from_slots = order // 2 + (n_mp // 2) * (order % 2)

    def by_owner(values):
        return values.reshape(n_mp, own, steps).transpose(0, 2, 1)

    def to_partners(values):
        return [swap(values, "batch", n_batch, bits) for bits in (1, 2, 3)]

    def quarter_of(values, bits, rows):
        return lax.dynamic_slice_in_dim(values, (b ^ bits) * rows, rows, 0)

    (
        embed_row, embed_col, main_row, main_col, scale_row, scale_col, hyper_row, hyper_col,
        zproj_row, zproj_col, out_row, out_col, vector_state,
    ) = states
    decay = 1.0 - STEP ** (-0.8)

    def moving(old, mean):
        return decay * old + (1.0 - decay) * mean

    def across(values):
        return jnp.broadcast_to(values[:, None], (values.shape[0], LANES))

    def placed(pieces, me):
        out = jnp.zeros((len(pieces),) + pieces[0].shape, pieces[0].dtype)
        for bits, piece in enumerate(pieces):
            out = lax.dynamic_update_slice_in_dim(out, piece[None], me ^ bits, 0)
        return out

    quarter = SCALE_AT // 4
    tail_quarter = TAIL_ROWS // 4
    half = (quarter + tail_quarter) // 2

    def own_rows(first, rows):
        values = lax.dynamic_slice_in_dim(w_main, b * quarter + first, rows, 0)
        return values.astype(BF16).reshape(rows, width)

    head_part = own_rows(0, half)
    head = swap(head_part, "mp", n_mp, 2)
    tail_own = weight_tail(w_scale, main_vectors)
    tail_part = jnp.concatenate(
        [own_rows(half, quarter - half), lax.dynamic_slice_in_dim(tail_own, b * tail_quarter, tail_quarter, 0)], axis=0
    )
    x_part = embed[by_owner(token_ids[:, :steps]).reshape(total)].astype(BF16)
    tail_part, head_part, head, x_part = tie(tail_part, head_part, head, x_part)
    tail = swap(tail_part, "mp", n_mp, 2)
    far = swap(jnp.concatenate([head_part, tail_part], axis=0), "mp", n_mp, 4)
    main_own = w_main.astype(BF16).reshape(2 * E, width)
    hyp_low = w_hyper.astype(BF16)
    far, hyper_wide, zproj_wide = tie(far, across(hyper_row), across(zproj_row))
    both = swap(far, "mp", n_mp, 2)
    x_all = lax.all_gather(x_part, "mp").reshape(n_mp, n_mp, own_total, emb_part)
    x_own = lax.dynamic_index_in_dim(x_all, my, 1, False).transpose(1, 0, 2).reshape(own_total, E)
    found = []
    for array, bits in ((main_own, 0), (swap(main_own, "mp", n_mp, 1), 1)):
        found.append((array, bits, None, 0, SCALE_AT))
    for array, bits in ((tail_own, 0), (swap(tail_own, "mp", n_mp, 1), 1)):
        found.append((array, bits, None, SCALE_AT, TAIL_ROWS))
    for got, bits, start in ((head, 2, 0), (tail, 2, half), (far, 4, 0), (both, 6, 0)):
        cut = got.shape[0] // 2
        along_x = swap(got, "batch", n_batch, 1)
        along_y = swap(got, "batch", n_batch, 2)
        low = swap(along_x[:cut], "batch", n_batch, 2)
        high = swap(along_y[cut:], "batch", n_batch, 1)
        for array, over, first in (
            (got, 0, start), (along_x, 1, start), (along_y, 2, start), (low, 3, start), (high, 3, start + cut),
        ):
            found.append((array, bits, over, first, array.shape[0]))
            found.append((swap(array, "mp", n_mp, 1), bits ^ 1, over, first, array.shape[0]))
    found.sort(key=lambda piece: piece[1])
    plan = [piece[1:] for piece in found]
    pieces = [piece[0] for piece in found]
    blocks = (n_mp, width)
    hyp_bias = hyp_low[E + H + NH :].astype(F32)
    zp_wide = jnp.pad(w_zproj, ((0, 0), (0, Z))).astype(BF16)
    zp_bias = zp_wide[NH:].astype(F32)
    pack, *kept = run_forward(
        x_own, blocks, plan, pieces, hyp_low, hyp_bias, zp_wide[:NH], zp_bias, steps
    )

    def of_chips(values):
        return jnp.stack([values] + [swap(values, "mp", n_mp, bits) for bits in (2, 4, 6)])

    def both_halves(near):
        return jnp.concatenate([near, swap(near, "mp", n_mp, 1)], axis=0)

    pack, token_ids, seq_lengths, valid_mask, w_out, *pieces = tie(
        pack, token_ids, seq_lengths, valid_mask, w_out, *pieces
    )
    near = of_chips(pack.reshape(own_total, PACK))
    positions = jnp.arange(steps, dtype=jnp.int32)
    valid = valid_mask * (positions[None, :] < seq_lengths[:, None]).astype(jnp.int32)
    marks = jnp.stack([token_ids[:, :steps], token_ids[:, 1:], valid])
    marks = marks.reshape(3, n_mp, own, steps).transpose(0, 1, 3, 2)[:, slots].reshape(3, total)
    told = jnp.concatenate([marks[0], jnp.broadcast_to(jnp.sum(valid), (LANES,))])
    told = jnp.concatenate([told, swap(told, "batch", n_batch, 1)])
    weight_rows = marks[2].astype(F32)
    out_low = w_out.astype(BF16)
    turned = run_turn(blocks, plan, pieces)
    near, told, marks, weight_rows, out_low, *turned = tie(near, told, marks, weight_rows, out_low, *turned)
    rest = swap(near, "mp", n_mp, 1)
    h_all = jnp.concatenate([near[:, :, :H], rest[:, :, :H]], axis=0)
    h_rows = h_all.reshape(total, H)
    logits = matmul(h_rows, out_low)
    local_target = marks[1] - my * vocab_part
    hit = jnp.arange(vocab_part, dtype=jnp.int32)[None, :] == local_target[:, None]
    top = jnp.max(logits, axis=1)
    stats = [
        top,
        jnp.sum(jnp.exp(logits - top[:, None]), axis=1),
        jnp.sum(jnp.where(hit, logits, 0.0), axis=1),
    ]

    def merged(one, two):
        top = jnp.maximum(one[0], two[0])
        exps = one[1] * jnp.exp(one[0] - top) + two[1] * jnp.exp(two[0] - top)
        return jnp.stack([top, exps, one[2] + two[2]])

    def from_partner(values, bits):
        spots = [bits ^ slot for slot in SLOTS]
        spots = [spot // 2 + (n_mp // 2) * (spot % 2) for spot in spots]
        turned = jnp.concatenate([values[:, spot : spot + 1] for spot in spots], axis=1)
        return swap(turned, "mp", n_mp, bits)

    stats = jnp.stack(stats).reshape(3, n_mp, own_total)
    pair = merged(stats, from_partner(stats, 1))
    pair, told = tie(pair, told)
    others = [from_partner(pair, bits) for bits in (2, 4, 6)]
    told = jnp.concatenate([told, swap(told, "batch", n_batch, 2)])
    count = sum(told[k * (total + LANES) + total] for k in range(n_batch)).astype(F32)
    stats = merged(merged(pair, others[0]), merged(others[1], others[2]))
    log_total = (stats[0] + jnp.log(stats[1])).reshape(total)
    loss = jnp.sum(
        (log_total[:own_total] - stats[2].reshape(total)[:own_total]) * weight_rows[:own_total]
    )
    grad_logits = (
        (jnp.exp(logits - log_total[:, None]) - hit.astype(F32)) * (weight_rows / count)[:, None]
    ).astype(BF16)
    other = swap(dot_last(grad_logits[total // 2 :], out_low).astype(BF16), "mp", n_mp, 1)
    both_cores = dot_last(grad_logits[: total // 2], out_low) + other.astype(F32)
    near, rest, both_cores = tie(near, rest, both_cores.reshape(n_mp // 2, own_total, H))
    dh_parts = [
        swap(both_cores[spot].astype(BF16), "mp", n_mp, 2 * spot) for spot in range(1, n_mp // 2)
    ]
    vec = main_vectors.reshape(2, width)
    column = run_column_forward(slots, near, rest, x_all, main_own, tail_own, vec, steps)
    dh_parts[1], *column = tie(dh_parts[1], *column)
    h_rows, dh_parts[0] = tie(h_rows, dh_parts[0])
    g_out = dot_first(h_rows, grad_logits).astype(BF16)
    out_quarter = H // n_batch
    out_parts = [quarter_of(g_out, bits, out_quarter) for bits in range(n_batch)]
    dh_top = both_cores[0]
    for part in dh_parts:
        dh_top = dh_top + part.astype(F32)
    dh_top, *out_parts = tie(dh_top, *out_parts)
    out_got = [swap(part, "batch", n_batch, bits) for bits, part in enumerate(out_parts) if bits]
    moved, odd, back_own, _, _ = run_backward(
        dh_top.reshape(steps, own, H), blocks, plan, turned, hyp_low, zp_wide[:NH], kept
    )
    left, x_rows, h_before, hh_before, hh_all, z_all = column[9:]
    moved, odd, back_own, hh_before, hh_all, z_all, loss, told, *out_got = tie(
        moved, odd, back_own, hh_before, hh_all, z_all, loss, told, *out_got
    )
    out_sum = out_parts[0].astype(F32)
    for part in out_got:
        out_sum = out_sum + part.astype(F32)

    moved = moved.reshape(n_mp // 2, own_total, 2 * units)
    back_own = back_own.reshape(3, own_total, 2 * NH)
    crossed = swap(odd.reshape(moved.shape), "mp", n_mp, 1)
    crossed, out_low_sum = tie(crossed, out_sum.astype(BF16))
    g_out = lax.all_gather(out_low_sum, "batch").reshape(H, vocab_part)
    arrived = [
        swap(
            jnp.concatenate([moved[spot : spot + 1], crossed[spot : spot + 1], back_own], axis=0),
            "mp",
            n_mp,
            2 * spot,
        )
        for spot in range(1, n_mp // 2)
    ]
    moved = jnp.stack(
        [moved[0]] + [part[0] for part in arrived] + [crossed[0]] + [part[1] for part in arrived]
    )
    back_all = both_halves(jnp.stack([back_own] + [part[2:] for part in arrived]))
    dx_part = moved[:, :, units:].reshape(total, emb_part)

    nh_part = NH // n_mp
    hyp_rows = emb_part + units + 2 * nh_part
    hyp_quarter = hyp_rows // n_batch

    def own_columns(values, size):
        return lax.dynamic_slice_in_dim(values, my * size, size, values.ndim - 1)

    dq_rows = jnp.concatenate([back_all[:, 0], back_all[:, 1]], axis=2).reshape(total, 4 * NH)
    dz_rows = back_all[:, 2, :, : 3 * Z].reshape(total, 3 * Z)
    hh_left = own_columns(hh_before, nh_part).reshape(total, nh_part)
    hh_own = own_columns(hh_all, nh_part).reshape(total, nh_part)
    g_small = [
        dot_first(left.reshape(total, emb_part + units), dq_rows),
        dot_first(hh_left, dq_rows),
        jnp.pad(dot_first(hh_own, dz_rows), ((0, 0), (0, 4 * NH - 3 * Z))),
    ]
    g_small = [g_small[0][:emb_part], g_small[0][emb_part:], g_small[1], g_small[2]]

    def small_quarter(bits):
        return jnp.concatenate([quarter_of(g, bits, g.shape[0] // n_batch) for g in g_small], axis=0)

    hyp_got, dx_got = [], [dx_part]
    for bits in (1, 2, 3):
        part = small_quarter(bits).astype(BF16).reshape(-1, emb_part)
        got = swap(jnp.concatenate([dx_part, part], axis=0), "batch", n_batch, bits)
        dx_got.append(got)
        hyp_got.append(got[total:].reshape(hyp_quarter, 4 * NH))
    hyp_sum = small_quarter(0)
    for got in hyp_got:
        hyp_sum = hyp_sum + got.astype(F32)
    hyp_all = lax.all_gather(hyp_sum.astype(BF16), ("batch", "mp"))
    hyp_all = hyp_all.reshape(n_batch, n_mp, hyp_quarter, 4 * NH)

    dux, duh, d0, d1, da, gv = run_column_backward(moved, back_all, vec, column[:9], steps)
    x_rows = x_rows.reshape(total, E)
    h_before = h_before.reshape(total, H)
    z_rows = z_all[:, :, :, : 3 * Z].reshape(total, 3, Z)
    g_parts = [dot_first(x_rows, dux.reshape(total, width)), dot_first(h_before, duh.reshape(total, width))] + [
        dot_first(z_rows[:, k], d.reshape(total, width)) for k, d in enumerate((d0, d1, da))
    ]

    def main_quarter(bits):
        return jnp.concatenate(
            [quarter_of(part, bits, part.shape[0] // n_batch) for part in g_parts], axis=0
        )

    g_parts[2], dx_got[3] = tie(g_parts[2], dx_got[3])
    main_got = [swap(main_quarter(bits).astype(BF16), "batch", n_batch, bits) for bits in (1, 2, 3)]

    me = b.reshape(1)
    g_embed, embed_rows, embed_cols = run_table(me, told, dx_got, embed.shape[0])

    g_embed, embed_rows, embed_cols, *main_got = tie(g_embed, embed_rows, embed_cols, *main_got)
    main_sum = main_quarter(0)
    for got in main_got:
        main_sum = main_sum + got.astype(F32)
    main_low = main_sum.astype(BF16)
    main_pieces = [main_low] + to_partners(main_low)
    main_seen = main_low.astype(F32)
    sq_main = main_seen * main_seen + EPS_FACT
    in_quarter = (E + H) // n_batch
    scale_quarter = Z // n_batch

    out_seen = g_out.astype(F32)
    sq_out = out_seen * out_seen + EPS_FACT

    by_rows = tree_sum(
        jnp.concatenate(
            [
                embed_rows.reshape(-1),
                jnp.sum(sq_out, axis=1),
                jnp.sum(sq_main, axis=1),
                loss[None],
            ]
        ),
        "mp",
        n_mp,
    )
    row_embed = by_rows[: embed.shape[0]]
    row_out = by_rows[embed.shape[0] : embed.shape[0] + H]
    sums = jnp.sum(back_all.astype(F32), axis=2)[from_slots]
    sums = jnp.sum(sums, axis=0).reshape(-1)[: 4 * NH + 3 * Z]
    fields = [
        by_rows[embed.shape[0] + H : -1],
        by_rows[-1:],
        jnp.sum(sq_main[:in_quarter], axis=0),
        jnp.sum(sq_main[in_quarter:].reshape(3, scale_quarter, width), axis=1).reshape(-1),
        gv.reshape(-1),
        sums,
    ]
    sizes = [field.shape[0] for field in fields]
    mixed = jnp.concatenate(fields)
    mixed = jnp.stack([mixed, swap(mixed, "batch", n_batch, 1)])
    mixed = placed(list(mixed) + list(swap(mixed, "batch", n_batch, 2)), b)
    rows_four = mixed[:, : sizes[0]]
    added = jnp.sum(mixed[:, sizes[0] :], axis=0)
    ends = [sum(sizes[1 : k + 1]) for k in range(len(sizes))]
    loss_sum, col_main, col_scale, g_vec, bias_sums = [
        added[ends[k] : ends[k + 1]] for k in range(len(sizes) - 1)
    ]
    row_in = rows_four[:, : E // n_batch].reshape(E)
    row_rec = rows_four[:, E // n_batch : in_quarter].reshape(H)
    row_scale = rows_four[:, in_quarter:].reshape(n_batch, 3, scale_quarter)
    row_scale = jnp.moveaxis(row_scale, 0, 1).reshape(3, Z)
    g_vec = g_vec.reshape(2, 4, units)

    res_embed = adafactor(
        embed, g_embed, embed_row, embed_col, row_embed / E, embed_cols[0] / embed.shape[0], 0, 1.0
    )
    new_out_row = moving(out_row, row_out / V)
    new_out_col = moving(out_col, jnp.mean(sq_out, axis=0))
    g_out, new_out = run_out_update(
        g_out,
        w_out,
        across(new_out_row / jnp.mean(new_out_row)),
        new_out_col[None],
        3.0 / math.sqrt(H),
    )
    (
        g_hyper, new_hyper, hyper_rows, new_hyper_col, g_zproj, new_zproj, zproj_rows, new_zproj_col,
    ) = run_hyper_update(
        hyp_all,
        (bias_sums[None, : 4 * NH], w_hyper, hyper_wide, hyper_col[None]),
        (bias_sums[None, 4 * NH :], w_zproj, zproj_wide, zproj_col[None]),
        (1.0 / math.sqrt(E + H + NH + 1), 2.0 / math.sqrt(NH)),
    )
    new_embed, new_out, new_hyper, *main_pieces = tie(res_embed[1], new_out, new_hyper, *main_pieces)
    res_embed = (res_embed[0], new_embed) + res_embed[2:]
    scale_parts = placed([piece[in_quarter:] for piece in main_pieces], b)
    g_scale = jnp.moveaxis(scale_parts.reshape(n_batch, 3, scale_quarter, width), 0, 1)
    g_scale = g_scale.reshape(3, Z, 4, units).astype(F32)
    new_main_row = moving(main_row, jnp.concatenate([row_in, row_rec]) / (4 * H))
    new_main_col = moving(main_col, col_main.reshape(4, units) / (E + H))
    g_main, new_main = run_main_update(
        me,
        main_pieces,
        w_main,
        across(new_main_row / jnp.mean(new_main_row)),
        new_main_col,
        1.0 / math.sqrt(E),
    )
    res_scale = adafactor(
        w_scale,
        g_scale,
        scale_row,
        scale_col,
        row_scale / (4 * H),
        col_scale.reshape(3, 4, units) / Z,
        1,
        1.0 / math.sqrt(Z),
    )
    state_new = moving(vector_state, g_vec * g_vec + EPS_FACT)
    return (
        (loss_sum[0], count)
        + res_embed
        + (g_main, new_main, new_main_row, new_main_col)
        + res_scale
        + (g_hyper, new_hyper, hyper_rows[:, 0], new_hyper_col[0])
        + (g_zproj, new_zproj, zproj_rows[:, 0], new_zproj_col[0])
        + (g_out, new_out, new_out_row, new_out_col)
        + (g_vec, state_new, main_vectors - 0.1 * g_vec * lax.rsqrt(state_new))
    )


def per_device(
    parts,
    token_ids,
    seq_lengths,
    valid_mask,
    embed,
    w_main,
    w_scale,
    w_hyper,
    w_zproj,
    w_out,
    main_vectors,
    *states,
):
    n_mp, n_batch = parts
    my = lax.axis_index("mp")
    units = w_main.shape[2]
    emb_part = embed.shape[1]
    vocab_part = w_out.shape[1]
    batch_rows, steps = valid_mask.shape
    own = batch_rows // n_mp
    padded = -(-own // ROW_TILE) * ROW_TILE
    own_total = steps * own
    total = batch_rows * steps
    wide = units % LANES == 0

    def by_owner(values):
        return values.reshape(n_mp, own, steps).transpose(0, 2, 1)

    ids = by_owner(token_ids[:, :steps]).reshape(total)
    targets = by_owner(token_ids[:, 1:]).reshape(total)
    positions = jnp.arange(steps, dtype=jnp.int32)
    valid = valid_mask.astype(F32) * (positions[None, :] < seq_lengths[:, None]).astype(F32)
    weight_rows = by_owner(valid).reshape(total)
    count = tree_sum(jnp.sum(weight_rows), "batch", n_batch)

    def to_kernel(stacked):
        if wide:
            return stacked
        rows = stacked.shape[1]
        apart = stacked.reshape(n_mp, rows, 4, units).transpose(1, 2, 0, 3)
        return apart.reshape(1, rows, 4 * H)

    def pad_rows(values):
        return jnp.pad(values, ((0, 0), (0, padded - own), (0, 0))) if padded > own else values

    def unpad(values):
        return values[:, :own] if padded > own else values

    x_part = embed[ids].astype(BF16)
    main_own = w_main.astype(BF16).reshape(E + H, 4 * units)
    tail_own = weight_tail(w_scale, main_vectors)
    scale_own = tail_own[: 3 * Z]
    x_own = lax.all_to_all(x_part.reshape(n_mp, own_total, emb_part), "mp", 0, 0)
    x_own = x_own.transpose(1, 0, 2).reshape(steps, own, E)
    pieces = [to_kernel(lax.all_gather(jnp.concatenate([main_own, tail_own], axis=0), "mp"))]
    blocks = (pieces[0].shape[0], pieces[0].shape[2])
    x_all = lax.all_gather(x_part, "mp", axis=1, tiled=True)
    hyp_low = w_hyper.astype(BF16)
    zp_wide = jnp.pad(w_zproj, ((0, 0), (0, Z))).astype(BF16)
    out_low = w_out.astype(BF16)
    hyp_bias = hyp_low[E + H + NH :].astype(F32)
    zp_bias = zp_wide[NH:].astype(F32)

    pack, *kept = run_forward(
        pad_rows(x_own).reshape(steps * padded, E),
        blocks, None, pieces, hyp_low, hyp_bias, zp_wide[:NH], zp_bias, steps,
    )

    small_own = unpad(pack)[:, :, : H + NH + 3 * Z]
    rows_all = lax.all_gather(small_own.reshape(own_total, H + NH + 3 * Z), "mp")
    h_rows = rows_all[:, :, :H].reshape(total, H)
    logits = matmul(h_rows, out_low)
    local_target = targets - my * vocab_part
    hit = jnp.arange(vocab_part, dtype=jnp.int32)[None, :] == local_target[:, None]
    top = jnp.max(logits, axis=1)
    stats = jnp.stack(
        [
            top,
            jnp.sum(jnp.exp(logits - top[:, None]), axis=1),
            jnp.sum(jnp.where(hit, logits, 0.0), axis=1),
        ]
    )
    stats = lax.all_gather(stats, "mp")
    top_all = jnp.max(stats[:, 0], axis=0)
    exp_sum = jnp.sum(stats[:, 1] * jnp.exp(stats[:, 0] - top_all), axis=0)
    log_total = top_all + jnp.log(exp_sum)
    picked = jnp.sum(stats[:, 2], axis=0)
    loss_sum = tree_sum(jnp.sum((log_total - picked) * weight_rows), "batch", n_batch)
    grad_logits = (
        (jnp.exp(logits - log_total[:, None]) - hit.astype(F32)) * (weight_rows / count)[:, None]
    ).astype(BF16)
    dh_part = dot_last(grad_logits, out_low).reshape(n_mp, own_total, H)
    dh_parts = lax.all_to_all(dh_part.astype(BF16), "mp", 0, 0)
    dh_top = jnp.sum(dh_parts.astype(F32), axis=0)
    dh_top = dh_top.reshape(steps, own, H)
    g_out = dot_first(h_rows, grad_logits).astype(BF16)
    dh_top, g_out = lax.optimization_barrier((dh_top, g_out))
    g_out = lax.psum(g_out, "batch").astype(F32)

    dsda, _, back, dx_own, gv = run_backward(
        pad_rows(dh_top), blocks, None, run_turn(blocks, None, pieces), hyp_low, zp_wide[:NH], kept
    )
    back = jnp.concatenate(list(back), axis=2)

    if wide:
        dsda = unpad(dsda.reshape(n_mp * steps, padded, 8 * units))
    else:
        dsda = unpad(dsda.reshape(steps, padded, 8 * H)).reshape(own_total, 8, n_mp, units)
        dsda = dsda.transpose(2, 0, 1, 3)
    dsda = dsda.reshape(n_mp, own_total, 8 * units)
    dx_send = unpad(dx_own.reshape(steps, padded, E)).reshape(own_total, n_mp, emb_part)
    sent = jnp.concatenate([dsda, dx_send.transpose(1, 0, 2)], axis=2)
    sent = lax.all_to_all(sent, "mp", 0, 0).reshape(total, 8 * units + emb_part)
    ds = sent[:, : 4 * units].astype(F32)
    da_low = sent[:, 4 * units : 8 * units]
    dx_part = sent[:, 8 * units :]
    back_own = unpad(back)[:, :, : 4 * NH + 3 * Z]
    back_all = lax.all_gather(back_own.reshape(own_total, 4 * NH + 3 * Z), "mp")
    back_all = back_all.reshape(total, 4 * NH + 3 * Z)
    dq_all = back_all[:, : 4 * NH]
    dz_all = back_all[:, 4 * NH :]

    before = jnp.concatenate(
        [jnp.zeros_like(rows_all[:, :own]), rows_all[:, : own_total - own]], axis=1
    ).reshape(total, H + NH + 3 * Z)
    h_before = before[:, :H]
    hh_before = before[:, H : H + NH]
    hh_rows = rows_all[:, :, H : H + NH].reshape(total, NH)
    z_rows = rows_all[:, :, H + NH :].reshape(total, 3, Z)
    uh = matmul(h_before, main_own[E:])
    ux = matmul(x_all, main_own[:E])
    scale_blocks = scale_own.reshape(3, Z, 4 * units)
    one0 = 1.0 + matmul(z_rows[:, 0], scale_blocks[0])
    one1 = 1.0 + matmul(z_rows[:, 1], scale_blocks[1])
    g_in = dot_first(x_all, (ds * one1).astype(BF16))
    g_rec = dot_first(h_before, (ds * one0).astype(BF16))
    d_scales = [(ds * uh).astype(BF16), (ds * ux).astype(BF16), da_low]
    g_scale = jnp.stack([dot_first(z_rows[:, k], d_scales[k]) for k in range(3)])
    nh_part = NH // n_mp
    left = jnp.concatenate(
        [
            x_part,
            lax.dynamic_slice_in_dim(h_before, my * units, units, 1),
            lax.dynamic_slice_in_dim(hh_before, my * nh_part, nh_part, 1),
        ],
        axis=1,
    )
    g_hyper = dot_first(left, dq_all)
    g_zproj = dot_first(lax.dynamic_slice_in_dim(hh_rows, my * nh_part, nh_part, 1), dz_all)

    dx_all = lax.all_gather(dx_part, "batch").reshape(n_batch * total, emb_part)
    ids_all = lax.all_gather(ids, "batch").reshape(n_batch * total)
    g_embed = jax.ops.segment_sum(dx_all.astype(F32), ids_all, num_segments=embed.shape[0])
    g_in, g_rec, g_scale, g_hyper, g_zproj = lax.psum(
        tuple(g.astype(BF16) for g in (g_in, g_rec, g_scale, g_hyper, g_zproj)), "batch"
    )
    flat = lax.all_gather(
        jnp.concatenate([g_hyper.reshape(-1, LANES), g_zproj.reshape(-1, LANES)], axis=0), "mp"
    ).astype(F32)
    n_hyp = g_hyper.size // LANES
    all_hyper = flat[:, :n_hyp].reshape(n_mp, emb_part + units + nh_part, 4 * NH)
    all_zproj = flat[:, n_hyp:].reshape(n_mp * nh_part, 3 * Z)
    if wide:
        gv_parts = gv.reshape(n_mp, 2, 4, units)
    else:
        gv_parts = gv.reshape(2, 4, n_mp, units).transpose(2, 0, 1, 3)
    gv_parts, bias_sums = lax.psum(
        (gv_parts, jnp.sum(back_own.astype(F32), axis=(0, 1))), ("batch", "mp")
    )
    g_vec = lax.dynamic_index_in_dim(gv_parts, my, 0, False)
    g_hyper = jnp.concatenate(
        [
            all_hyper[:, :emb_part].reshape(E, 4 * NH),
            all_hyper[:, emb_part : emb_part + units].reshape(H, 4 * NH),
            all_hyper[:, emb_part + units :].reshape(NH, 4 * NH),
            bias_sums[None, : 4 * NH],
        ],
        axis=0,
    )
    g_zproj = jnp.concatenate([all_zproj, bias_sums[None, 4 * NH :]], axis=0)
    g_main = jnp.concatenate([g_in, g_rec], axis=0).astype(F32).reshape(E + H, 4, units)
    g_scale = g_scale.astype(F32).reshape(3, Z, 4, units)

    sq_embed = g_embed * g_embed + EPS_FACT
    sq_main = g_main * g_main + EPS_FACT
    sq_scale = g_scale * g_scale + EPS_FACT
    sq_out = g_out * g_out + EPS_FACT
    row_out = lax.psum(jnp.sum(sq_out, axis=1), "mp")
    row_embed, row_main, row_scale = lax.psum(
        (
            jnp.sum(sq_embed, axis=1),
            jnp.sum(sq_main, axis=(1, 2)),
            jnp.sum(sq_scale, axis=(2, 3)),
        ),
        "mp",
    )
    return (loss_sum, count) + updates(
        (embed, w_main, w_scale, w_hyper, w_zproj, w_out, main_vectors),
        states,
        (g_embed, g_main, g_scale, g_hyper, g_zproj, g_out, g_vec),
        (row_embed, row_main, row_scale, row_out),
        jnp.mean(sq_embed, axis=0),
    )


def solution(mesh):
    rep = P()
    placed = (
        P("batch", None),
        P("batch"),
        P("batch", None),
        P(None, "mp"),
        P(None, None, "mp"),
        P(None, None, None, "mp"),
        rep,
        rep,
        P(None, "mp"),
        P(None, None, "mp"),
        rep,
        P("mp"),
        rep,
        P(None, "mp"),
        rep,
        P(None, None, "mp"),
        rep,
        rep,
        rep,
        rep,
        rep,
        P("mp"),
        P(None, None, "mp"),
    )
    parts = (mesh.shape["mp"], mesh.shape["batch"])
    body = per_chip if parts == (8, 4) else per_device
    return jax.shard_map(
        functools.partial(body, parts),
        mesh=mesh,
        in_specs=placed,
        out_specs=(
            rep,
            rep,
            P(None, "mp"),
            P(None, "mp"),
            rep,
            P("mp"),
            P(None, None, "mp"),
            P(None, None, "mp"),
            rep,
            P(None, "mp"),
            P(None, None, None, "mp"),
            P(None, None, None, "mp"),
            rep,
            P(None, None, "mp"),
            rep,
            rep,
            rep,
            rep,
            rep,
            rep,
            rep,
            rep,
            P(None, "mp"),
            P(None, "mp"),
            rep,
            P("mp"),
            P(None, None, "mp"),
            P(None, None, "mp"),
            P(None, None, "mp"),
        ),
        check_vma=False,
    )
```
